32 devices in a mesh: wide: 8 (over z, y), narrow: 4 (over x, core).
Axes of the slice: x: 2, y: 2, z: 4, core: 2. Of those that a mesh axis runs over, the one named last changes fastest.
Arguments:
- patch_feature_matrix: bfloat16 [768, 100, 512], P(('wide', 'narrow')), may hold values from -6 to 6
- occupied_pane_tally: int32 [32], P(('wide', 'narrow')), may hold values from 8 to 24, as said below
- mask_zone_labels: int32 [768, 100], P(('wide', 'narrow')), may hold values from 0 to 8, as said below
- opening_scale_factor: bfloat16 [512], P(('wide', 'narrow')), may hold values from 0.25 to 1.75
- opening_offset: bfloat16 [512], P(('wide', 'narrow')), may hold values from -4 to 4
- qkv_weight_matrix: bfloat16 [512, 1536], P(('wide', 'narrow')), may hold values from -0.375 to 0.375
- question_offset: bfloat16 [512], P(('wide', 'narrow')), may hold values from -4 to 4
- content_offset: bfloat16 [512], P(('wide', 'narrow')), may hold values from -4 to 4
- projection_back_matrix: bfloat16 [512, 512], P(('wide', 'narrow')), may hold values from -1.5 to 1.5
- projection_back_offset: bfloat16 [512], P(('wide', 'narrow')), may hold values from -4 to 4
- central_scale_factor: bfloat16 [512], P(('wide', 'narrow')), may hold values from 0.25 to 1.75
- central_offset: bfloat16 [512], P(('wide', 'narrow')), may hold values from -4 to 4
- widening_matrix: bfloat16 [512, 2048], P(('wide', 'narrow')), may hold values from -0.25 to 0.25
- widening_offset: bfloat16 [2048], P(('wide', 'narrow')), may hold values from -4 to 4
- narrowing_matrix: bfloat16 [2048, 512], P(('wide', 'narrow')), may hold values from -0.1875 to 0.1875
- narrowing_offset: bfloat16 [512], P(('wide', 'narrow')), may hold values from -4 to 4
- displacement_bias_table: bfloat16 [16, 361], replicated, may hold values from -6 to 6
- upstream_sensitivity: bfloat16 [768, 100, 512], P(('wide', 'narrow')), may hold values from -6 to 6
Outputs:
- block_output: bfloat16 [768, 100, 512], P(('wide', 'narrow'))
- grad_input: bfloat16 [768, 100, 512], P(('wide', 'narrow'))
- grad_pregain: float32 [512], P(('wide', 'narrow'))
- opening_offset_derivative: float32 [512], P(('wide', 'narrow'))
- grad_projector: float32 [512, 1536], P(('wide', 'narrow'))
- grad_querybias: float32 [512], P(('wide', 'narrow'))
- grad_valuebias: float32 [512], P(('wide', 'narrow'))
- grad_outmatrix: float32 [512, 512], P(('wide', 'narrow'))
- grad_outbias: float32 [512], P(('wide', 'narrow'))
- grad_midgain: float32 [512], P(('wide', 'narrow'))
- grad_midshift: float32 [512], P(('wide', 'narrow'))
- grad_expander: float32 [512, 2048], P(('wide', 'narrow'))
- grad_expandbias: float32 [2048], P(('wide', 'narrow'))
- grad_reducer: float32 [2048, 512], P(('wide', 'narrow'))
- grad_reducebias: float32 [512], P(('wide', 'narrow'))
- grad_reltable: float32 [16, 361], replicated
The draws below stay inside these ranges and needn't reach their ends.
Inputs may be any that keep to these rules, and one draw needn't show every extreme that they name: Device d's first occupied_pane_tally[d] slots are live and its other slots are empty; some device has all 24 slots live and some device the fewest. `mask_zone_labels`: inside a window the id is 3 a + b, where a is 0 in windows of no last row and otherwise 1 for window rows below 5 and 2 for the rest, and b likewise over columns.
All inputs are finite; a program needn't handle non-finite values.
Results may differ from the reference program's by a relative error of at most 0.023.
Values may be sent and summed in bfloat16 or wider, within the bound.
No kernel may reach another device: no remote copies, remote signals or barrier semaphores. Data moves between devices by JAX's collectives and lax.ppermute only.
A program may use at most 256 MiB of HBM per device.

```python
import jax
import jax.numpy as jnp
from jax import lax

EMBED_BREADTH = 512
HEADS = 16
HEAD = 32
FF = 2048
WS = 10
SHIFT = 5
WIN_DEV = 24
WTOK = 100
RELS = 361
SLOTS = 768


def draw_occupied_pane_tally(key, part):
    key = jax.random.fold_in(key, 7)
    first_key, second_key = jax.random.split(key)
    device_count = SLOTS // WIN_DEV
    fewest = max(WIN_DEV // 3, 1)
    counts_drawn = jax.random.randint(first_key, (device_count,), fewest, WIN_DEV + 1)
    ranking = jax.random.permutation(second_key, device_count)
    counts_drawn = jnp.where(ranking == 0, WIN_DEV, counts_drawn)
    return jnp.where(ranking == 1, fewest, counts_drawn).astype(jnp.int32)


def draw_mask_zone_labels(key, part):
    key = jax.random.fold_in(key, 11)
    row_key, col_key, pick_key = jax.random.split(key, 3)
    slot_index = jnp.arange(SLOTS, dtype=jnp.int32)
    picked = jax.random.randint(pick_key, (), 0, SLOTS)
    row_last = jax.random.randint(row_key, (SLOTS,), 0, 3) == 0
    col_last = jax.random.randint(col_key, (SLOTS,), 0, 3) == 0
    interior = slot_index == (picked + 1) % SLOTS
    row_last = jnp.where(slot_index == picked, True, jnp.where(interior, False, row_last))
    col_last = jnp.where(slot_index == picked, True, jnp.where(interior, False, col_last))
    cell_index = jnp.arange(WS * WS, dtype=jnp.int32)
    row_side = (cell_index // WS >= WS - SHIFT).astype(jnp.int32)
    col_side = (cell_index % WS >= WS - SHIFT).astype(jnp.int32)
    row_part = jnp.where(row_last[:, None], 1 + row_side[None, :], 0)
    col_part = jnp.where(col_last[:, None], 1 + col_side[None, :], 0)
    return (3 * row_part + col_part).astype(jnp.int32)


def spiked(entries, own_key, source, target, blocks, factor):
    def block_of(dim):
        return (jnp.arange(entries.shape[dim]) // (entries.shape[dim] // blocks)).reshape((-1,) + (1,) * (entries.ndim - 1 - dim))

    near = jax.random.permutation(own_key, blocks)[block_of(target)]
    second = (block_of(target) + blocks // 2) % blocks
    return jnp.where((block_of(source) == near) | (block_of(source) == second), factor * entries, entries)


def level_of(rng, shape, cuts, least, high):
    loudness, own = 1.0, jax.random.fold_in(rng, 6)
    for axis_at, blocks in cuts:
        steps = jnp.exp(jax.random.uniform(jax.random.fold_in(own, axis_at), (blocks,), jnp.float32, least / len(cuts), high / len(cuts)))
        loudness = loudness * jnp.repeat(steps, shape[axis_at] // blocks).reshape([-1 if axis == axis_at else 1 for axis in range(len(shape))])
    return loudness


def normal_values(own_key, shape, spread, bound, cuts=(), kind=jnp.bfloat16):
    entries = jax.random.normal(own_key, shape, jnp.float32) * spread
    if len(cuts) > 0:
        entries = level_of(own_key, shape, cuts, -0.22, 0.18) * entries
    return jnp.clip(entries, min=-bound, max=bound).astype(kind)


def bell_draw_with(rng, shape, spread, reach, cuts, heavy, held_as=jnp.bfloat16):
    drawn = spread * jax.random.normal(rng, shape, jnp.float32)
    if cuts:
        drawn = drawn * level_of(rng, shape, cuts, -0.22, 0.18)
    return jnp.clip(spiked(drawn, jax.random.fold_in(rng, 3), *heavy), -reach, reach).astype(held_as)


def setup_inputs(seed: int = 0) -> dict:
    key_list = jax.random.split(jax.random.key(seed), 19)
    patch_feature_matrix = normal_values(key_list[0], (SLOTS, WTOK, EMBED_BREADTH), 1.0, 6.0, ((0, 32),))
    occupied_pane_tally = draw_occupied_pane_tally(jax.random.fold_in(key_list[18], 71), 0)
    mask_zone_labels = draw_mask_zone_labels(jax.random.fold_in(key_list[18], 71), 0)
    opening_scale_factor = jnp.clip(1.0 + 0.15 * jax.random.normal(key_list[3], (EMBED_BREADTH,), jnp.float32), 0.25, 1.75).astype(jnp.bfloat16)
    opening_offset = normal_values(key_list[4], (EMBED_BREADTH,), 0.3, 4.0, ((0, 32),))
    qkv_weight_matrix = normal_values(key_list[5], (EMBED_BREADTH, 3 * EMBED_BREADTH), (EMBED_BREADTH // 2) ** -0.5, 0.375, ((0, 32),))
    question_offset = normal_values(key_list[6], (EMBED_BREADTH,), 0.3, 4.0, ((0, 32),))
    content_offset = normal_values(key_list[7], (EMBED_BREADTH,), 0.3, 4.0, ((0, 32),))
    projection_back_matrix = normal_values(key_list[8], (EMBED_BREADTH, EMBED_BREADTH), (EMBED_BREADTH // 32) ** -0.5, 1.5, ((0, 32),))
    projection_back_offset = normal_values(key_list[9], (EMBED_BREADTH,), 0.3, 4.0, ((0, 32),))
    central_scale_factor = jnp.clip(1.0 + 0.15 * jax.random.normal(key_list[10], (EMBED_BREADTH,), jnp.float32), 0.25, 1.75).astype(jnp.bfloat16)
    central_offset = normal_values(key_list[11], (EMBED_BREADTH,), 0.3, 4.0, ((0, 32),))
    widening_matrix = normal_values(key_list[12], (EMBED_BREADTH, FF), EMBED_BREADTH ** -0.5, 0.25, ((0, 32),))
    widening_offset = normal_values(key_list[13], (FF,), 0.3, 4.0, ((0, 32),))
    narrowing_matrix = normal_values(key_list[14], (FF, EMBED_BREADTH), (FF // 2) ** -0.5, 0.1875, ((0, 32),))
    narrowing_offset = normal_values(key_list[15], (EMBED_BREADTH,), 0.3, 4.0, ((0, 32),))
    displacement_bias_table = normal_values(key_list[16], (HEADS, RELS), 1.0, 6.0)
    upstream_sensitivity = bell_draw_with(key_list[17], (SLOTS, WTOK, EMBED_BREADTH), 1.0, 6.0, ((0, 32),), (0, 2, 32, 2.75))
    return dict(patch_feature_matrix=patch_feature_matrix, occupied_pane_tally=occupied_pane_tally, mask_zone_labels=mask_zone_labels, opening_scale_factor=opening_scale_factor, opening_offset=opening_offset, qkv_weight_matrix=qkv_weight_matrix, question_offset=question_offset, content_offset=content_offset, projection_back_matrix=projection_back_matrix, projection_back_offset=projection_back_offset, central_scale_factor=central_scale_factor, central_offset=central_offset, widening_matrix=widening_matrix, widening_offset=widening_offset, narrowing_matrix=narrowing_matrix, narrowing_offset=narrowing_offset, displacement_bias_table=displacement_bias_table, upstream_sensitivity=upstream_sensitivity)


@jax.custom_vjp
def low(v):
    return lax.optimization_barrier(v.astype(jnp.bfloat16)).astype(jnp.float32)

@jax.custom_vjp
def low_back(v):
    return v

def low_keep(v):
    return (low(v), None)

def low_pass(kept, grad):
    return (grad,)

def back_keep(v):
    return (v, None)

def back_low(kept, grad):
    return (low(grad),)
low.defvjp(low_keep, low_pass)
low_back.defvjp(back_keep, back_low)
highest = lax.Precision.HIGHEST

def standardize_features(rows, gain, shift):
    center = rows - lax.optimization_barrier(jnp.mean(rows, axis=-1, keepdims=True))
    inverse = lax.rsqrt(lax.optimization_barrier(jnp.mean(center * center, axis=-1, keepdims=True)) + 1e-05)
    return center * inverse * gain + shift

def relative_offsets():
    position = jnp.arange(WS * WS, dtype=jnp.int32)
    row_pos = position // WS
    col_pos = position % WS
    return (row_pos[:, None] - row_pos[None, :] + WS - 1) * (2 * WS - 1) + col_pos[:, None] - col_pos[None, :] + WS - 1

def window_group(learned_weights, group_tokens, group_regions, live_count):
    opening_scale_factor, opening_offset, qkv_weight_matrix, question_offset, content_offset, projection_back_matrix, projection_back_offset, central_scale_factor, central_offset, widening_matrix, widening_offset, narrowing_matrix, narrowing_offset, displacement_bias_table = learned_weights
    windows = group_tokens.shape[0]
    model_width = HEADS * HEAD
    merged_patch_lines = group_tokens.reshape(windows * WTOK, model_width)
    opening_result = low(standardize_features(merged_patch_lines, opening_scale_factor, opening_offset))
    joint = jnp.dot(opening_result, qkv_weight_matrix, precision=highest) + jnp.concatenate([question_offset, jnp.zeros_like(question_offset), content_offset])
    joint = low_back(joint)
    queries = low(joint[:, :model_width] * HEAD ** (-0.5)).reshape(windows, WTOK, HEADS, HEAD)
    keyset = low(joint[:, model_width:2 * model_width]).reshape(windows, WTOK, HEADS, HEAD)
    valset = low(joint[:, 2 * model_width:]).reshape(windows, WTOK, HEADS, HEAD)
    scores = jnp.einsum('wqhe,wkhe->whqk', queries, keyset, precision=highest) + displacement_bias_table[:, relative_offsets()][None]
    same_region = group_regions[:, :, None] == group_regions[:, None, :]
    scores = low_back(jnp.where(same_region[:, None], scores, -1000000000.0))
    row_peak = lax.optimization_barrier(jnp.max(scores, axis=-1, keepdims=True))
    exponent = jnp.exp(scores - row_peak)
    probability = low(exponent / lax.optimization_barrier(jnp.sum(exponent, axis=-1, keepdims=True)))
    context = jnp.einsum('whqk,wkhe->wqhe', probability, valset, precision=highest).reshape(windows * WTOK, model_width)
    context = low(low_back(context))
    attended = low_back(jnp.dot(context, projection_back_matrix, precision=highest) + projection_back_offset)
    residual = merged_patch_lines + attended
    second = low(standardize_features(residual, central_scale_factor, central_offset))
    preact = low_back(jnp.dot(second, widening_matrix, precision=highest) + widening_offset)
    active = low(jax.nn.gelu(preact, approximate=False))
    branch = low_back(jnp.dot(active, narrowing_matrix, precision=highest) + narrowing_offset)
    output = (residual + branch).reshape(windows, WTOK, model_width)
    live = jnp.arange(windows, dtype=jnp.int32) < live_count
    return jnp.where(live[:, None, None], output, group_tokens)

def reference(patch_feature_matrix, occupied_pane_tally, mask_zone_labels, opening_scale_factor, opening_offset, qkv_weight_matrix, question_offset, content_offset, projection_back_matrix, projection_back_offset, central_scale_factor, central_offset, widening_matrix, widening_offset, narrowing_matrix, narrowing_offset, displacement_bias_table, upstream_sensitivity):
    device_count = occupied_pane_tally.shape[0]
    learned_weights = tuple((member.astype(jnp.float32) for member in (opening_scale_factor, opening_offset, qkv_weight_matrix, question_offset, content_offset, projection_back_matrix, projection_back_offset, central_scale_factor, central_offset, widening_matrix, widening_offset, narrowing_matrix, narrowing_offset, displacement_bias_table)))
    grouped = patch_feature_matrix.astype(jnp.float32).reshape(device_count, -1, WTOK, patch_feature_matrix.shape[2])
    region_groups = mask_zone_labels.reshape(device_count, -1, WTOK)
    checked = jax.checkpoint(window_group)

    def forward(weights, grouped_tokens):

        def per_group(inputs):
            group_tokens, group_regions, live_count = inputs
            return checked(weights, group_tokens, group_regions, live_count)
        return lax.map(per_group, (grouped_tokens, region_groups, occupied_pane_tally))
    outputs, pullback = jax.vjp(forward, learned_weights, grouped)
    grad_params, grad_tokens = pullback(upstream_sensitivity.astype(jnp.float32).reshape(outputs.shape))
    return (outputs.reshape(patch_feature_matrix.shape).astype(jnp.bfloat16), grad_tokens.reshape(patch_feature_matrix.shape).astype(jnp.bfloat16), grad_params[0], grad_params[1], grad_params[2], grad_params[3], grad_params[4], grad_params[5], grad_params[6], grad_params[7], grad_params[8], grad_params[9], grad_params[10], grad_params[11], grad_params[12], grad_params[13])
```

```python
import functools

import jax
import jax.numpy as jnp
from jax import lax
from jax.experimental import pallas as pl
from jax.experimental.pallas import tpu as pltpu
from jax.sharding import PartitionSpec as P

F32 = jnp.float32
BF = jnp.bfloat16
WS = 10
TP = 104
SEG = 128
BLK = 16
EPS = 1e-5
NW = 4
VMEM = 60 << 20

NT = (((1,), (1,)), ((), ()))
TN = (((0,), (0,)), ((), ()))
NN = (((1,), (0,)), ((), ()))


def dot(a, b, dims=NN):
    return lax.dot_general(a, b, dims, preferred_element_type=F32)


def normalize(v):
    c = v - jnp.mean(v, axis=-1, keepdims=True)
    inv = lax.rsqrt(jnp.mean(c * c, axis=-1, keepdims=True) + EPS)
    return c * inv, inv


def norm_back(g, xhat, inv, gain):
    s = g * gain
    return inv * (
        s
        - jnp.mean(s, axis=-1, keepdims=True)
        - xhat * jnp.mean(s * xhat, axis=-1, keepdims=True)
    )


def head_masks():
    lane = lax.broadcasted_iota(jnp.int32, (1, 128), 1)
    return [(lane // 32) == h for h in range(4)]


def head_ones():
    return [jnp.where(m, 1.0, 0.0).astype(BF) for m in head_masks()]


def stack_heads(v, ones):
    return jnp.concatenate([v * m for m in ones], axis=0)


def load_rows(dst, src_ref, nw, tokens):
    for w in range(nw):
        dst[w * TP : w * TP + tokens, :] = src_ref[w].astype(F32)


def fetch_blocks(slots_ref, src, dst, sem):
    count = src.shape[0]

    def copy(d):
        return pltpu.make_async_copy(
            src.at[slots_ref[d]], dst.at[pl.ds(d * BLK, BLK), :], sem.at[d]
        )

    for d in range(count):
        copy(d).start()
    for d in range(count):
        copy(d).wait()


def split_blocks(bit, keep_ref, send_ref, column, acc):
    width = acc.shape[1]
    for k in range(keep_ref.shape[0]):
        if (k + 1) * 2 * BLK > acc.shape[0]:
            break
        mine = pl.multiple_of(k * 2 * BLK + bit * BLK, BLK)
        other = pl.multiple_of(k * 2 * BLK + (1 - bit) * BLK, BLK)
        keep_ref[k, :, column : column + width] = acc[pl.ds(mine, BLK), :].astype(BF)
        send_ref[k, :, column : column + width] = acc[pl.ds(other, BLK), :].astype(BF)


def block_at(i, scal):
    return jnp.minimum(i, (scal[0] + NW - 1) // NW - 1)


def whole(shape):
    return pl.BlockSpec(shape, lambda *a: (0,) * len(shape))


def rows_spec(cols, col=0):
    return pl.BlockSpec((NW * TP, cols), lambda i, scal, *r: (block_at(i, scal), col))


def win_spec(shape, live_only=True):
    if live_only:
        return pl.BlockSpec(
            (NW,) + shape, lambda i, scal, *r: (block_at(i, scal),) + (0,) * len(shape)
        )
    return pl.BlockSpec((NW,) + shape, lambda i, *r: (i,) + (0,) * len(shape))


def any_spec():
    return pl.BlockSpec(memory_space=pl.ANY)


def call(body, name, grid, prefetch, args, in_specs, out_shape, out_specs, scratch, cost):
    return pl.pallas_call(
        body,
        grid_spec=pltpu.PrefetchScalarGridSpec(
            num_scalar_prefetch=len(prefetch),
            grid=grid,
            in_specs=in_specs,
            out_specs=out_specs,
            scratch_shapes=scratch,
        ),
        out_shape=out_shape,
        compiler_params=pltpu.CompilerParams(vmem_limit_bytes=VMEM),
        cost_estimate=pl.CostEstimate(
            flops=int(cost * 8e8), bytes_accessed=int(cost * 1e6), transcendentals=0
        ),
        name=name,
    )(*prefetch, *args)


def sds(shape, dtype):
    return jax.ShapeDtypeStruct(shape, dtype)


def attention_body(
    tokens, scal, slots, x_ref, reg_ref, bias_ref, wq_hbm,
    first_ref, qkv_ref, p_ref, ctx_ref, prm_ref,
    xs, js, cs, wq, sem,
):
    i = pl.program_id(0)
    width = x_ref.shape[2]
    rows = NW * TP
    live = scal[0]

    @pl.when(i == 0)
    def _():
        xs[...] = jnp.zeros_like(xs)
        js[rows : rows + SEG - TP, :] = jnp.zeros((SEG - TP, 3 * width), F32)
        fetch_blocks(slots, wq_hbm, wq, sem)
        prm_ref[...] = jnp.transpose(wq[:, 3 * width :].astype(F32))[0:16]

    @pl.when(i * NW < live)
    def _():
        load_rows(xs, x_ref, NW, tokens)
        xhat, _ = normalize(xs[...])
        first = (xhat * prm_ref[0:1, :] + prm_ref[1:2, :]).astype(BF)
        first_ref[...] = first
        scale = 32.0**-0.5
        for part in range(3):
            j = dot(first, wq[:, part * width : (part + 1) * width])
            if part == 0:
                j = (j + prm_ref[2:3, :]) * scale
            if part == 2:
                j = j + prm_ref[3:4, :]
            js[0:rows, part * width : (part + 1) * width] = j
        ones = head_ones()
        eye = lax.broadcasted_iota(jnp.int32, (TP, SEG), 0) == lax.broadcasted_iota(
            jnp.int32, (TP, SEG), 1
        )
        masks = []
        for w in range(NW):
            qkv_ref[w] = js[w * TP : w * TP + SEG, :].astype(BF)
            row = jnp.broadcast_to(reg_ref[w], (TP, SEG))
            col = jnp.max(jnp.where(eye, row, -1.0), axis=1, keepdims=True)
            masks.append(jnp.where(row == col, 0.0, -1e30))

        def scores(n):
            w, g = n
            c = 128 * g
            keys = stack_heads(qkv_ref[w, :, width + c : width + c + 128], ones)
            return dot(qkv_ref[w, 0:TP, c : c + 128], keys, NT)

        def softmax(n, s):
            w, g = n
            out = []
            for h in range(4):
                lanes = slice(SEG * h, SEG * (h + 1))
                sh = s[:, lanes] + bias_ref[g, :, lanes] + masks[w]
                e = jnp.exp(sh - jnp.max(sh, axis=1, keepdims=True))
                out.append((e * (1.0 / jnp.sum(e, axis=1, keepdims=True))).astype(BF))
            p = jnp.concatenate(out, axis=1)
            p_ref[w, g] = p
            return p

        def values(n, p):
            w, g = n
            c = 128 * g
            stacked = stack_heads(qkv_ref[w, :, 2 * width + c : 2 * width + c + 128], ones)
            cs[w * TP : (w + 1) * TP, c : c + 128] = dot(p, stacked)

        pairs = [(w, g) for w in range(NW) for g in range(width // 128)]
        for k in range(0, len(pairs), 8):
            part = pairs[k : k + 8]
            ss = [scores(n) for n in part]
            pp = [softmax(n, s) for n, s in zip(part, ss)]
            for n, p in zip(part, pp):
                values(n, p)
        ctx_ref[...] = cs[...].astype(BF)


def attention_forward(scal, slots, x, regions, bias, wq):
    windows, tokens, width = x.shape
    rows = NW * TP
    groups = width // 128
    return call(
        functools.partial(attention_body, tokens), "attn_fwd", (windows // NW,), (scal, slots),
        (x, regions, bias, wq),
        [win_spec((tokens, width)), win_spec((1, SEG)), whole(bias.shape), any_spec()],
        [sds((windows * TP, width), BF), sds((windows, SEG, 3 * width), BF),
         sds((windows, groups, TP, 512), BF), sds((windows * TP, width), BF), sds((16, width), F32)],
        [rows_spec(width), win_spec((SEG, 3 * width)), win_spec((groups, TP, 512)), rows_spec(width),
         whole((16, width))],
        [pltpu.VMEM((rows, width), F32), pltpu.VMEM((rows + SEG - TP, 3 * width), F32),
         pltpu.VMEM((rows, width), F32), pltpu.VMEM((width, wq.shape[2]), BF),
         pltpu.SemaphoreType.DMA((wq.shape[0],))],
        24,
    )


ERF = (0.254829592, -0.284496736, 1.421413741, -1.453152027, 1.061405429)
ERF_P = 0.3275911 / 2**0.5


def normal_parts(z):
    bell = jnp.exp(z * z * -0.5)
    t = 1.0 / (1.0 + ERF_P * jnp.abs(z))
    tail = 0.5 * ERF[4]
    for a in ERF[3::-1]:
        tail = 0.5 * a + t * tail
    tail = t * tail * bell
    return jnp.where(z >= 0, 1.0 - tail, tail), bell


def hidden_chunks(second, up, ww, wn, bw, acts, gps, eb_ref, er, rr, step=256):
    count = acts.shape[1] // step

    def products(c):
        cols = slice(c * step, (c + 1) * step)
        return dot(up, wn(c * step, step), NT), dot(second, ww(c * step, step))

    def activate(c, ga, z):
        cols = slice(c * step, (c + 1) * step)
        z = z + bw(c * step, step)
        phi, bell = normal_parts(z)
        acts[:, cols] = (z * phi).astype(BF)
        gp = (ga * (phi + z * bell * 0.3989422804014327)).astype(BF)
        gps[:, cols] = gp
        eb_ref[:, cols] += jnp.sum(gp.astype(F32), axis=0, keepdims=True)

    t = products(0)
    for c in range(count):
        later = products(c + 1) if c + 1 < count else None
        activate(c, *t)
        t = later
    for c in range(count):
        cols = slice(c * step, (c + 1) * step)
        er[:, cols] += dot(second, gps[:, cols], TN)
        rr[cols, :] += dot(acts[:, cols], up, TN)


def hidden_first_body(
    tokens, scal, slots, x_ref, u_ref, ctx_ref, prm_ref, w_hbm,
    res_ref, second_ref, up_ref, act_ref, gp_ref, eb_ref, keep_ref, send_ref,
    xs, us, er, rr, wb, sem,
):
    i = pl.program_id(0)
    width = x_ref.shape[2]
    half = act_ref.shape[1]
    live = scal[0]

    @pl.when(i == 0)
    def _():
        fetch_blocks(slots, w_hbm, wb, sem)
        xs[...] = jnp.zeros_like(xs)
        us[...] = jnp.zeros_like(us)
        er[...] = jnp.zeros_like(er)
        rr[...] = jnp.zeros_like(rr)
        eb_ref[...] = jnp.zeros_like(eb_ref)

    @pl.when(i * NW < live)
    def _():
        load_rows(xs, x_ref, NW, tokens)
        for w in range(NW):
            us[w * TP : w * TP + tokens, :] = jnp.where(
                i * NW + w < live, u_ref[w].astype(F32), 0.0
            )
        up = us[...].astype(BF)
        up_ref[...] = up
        res = xs[...] + dot(ctx_ref[...], wb[:, 0:width]) + prm_ref[4:5, :]
        res_ref[...] = res
        xhat, _ = normalize(res)
        second = (xhat * prm_ref[5:6, :] + prm_ref[6:7, :]).astype(BF)
        second_ref[...] = second

        def ww(c, n):
            return wb[:, width + c : width + c + n]

        def wn(c, n):
            return wb[c % width : c % width + n, width + half + c // width * width :][:, 0:width]

        def bw(c, n):
            return prm_ref[8 + c // width : 9 + c // width, c % width : c % width + n]

        hidden_chunks(second, up, ww, wn, bw, act_ref, gp_ref, eb_ref, er, rr)

    @pl.when(i == pl.num_programs(0) - 1)
    def _():
        split_blocks(scal[1], keep_ref, send_ref, 0, er)
        for c in range(half // width):
            split_blocks(scal[1], keep_ref, send_ref, half + c * width, rr.at[c * width : (c + 1) * width])


def hidden_first(scal, slots, x, u, ctx, prm, wb):
    windows, tokens, width = x.shape
    rows = NW * TP
    half = (wb.shape[2] - width) // 2
    pairs = wb.shape[0] // 2
    return call(
        functools.partial(hidden_first_body, tokens), "hidden_first", (windows // NW,), (scal, slots),
        (x, u, ctx, prm, wb),
        [win_spec((tokens, width)), win_spec((tokens, width)), rows_spec(width), whole(prm.shape), any_spec()],
        [sds((windows * TP, width), F32), sds((windows * TP, width), BF), sds((windows * TP, width), BF),
         sds((windows * TP, half), BF), sds((windows * TP, half), BF), sds((1, half), F32),
         sds((pairs, BLK, 2 * half), BF), sds((pairs, BLK, 2 * half), BF)],
        [rows_spec(width), rows_spec(width), rows_spec(width), rows_spec(half), rows_spec(half),
         whole((1, half)), whole((pairs, BLK, 2 * half)), whole((pairs, BLK, 2 * half))],
        [pltpu.VMEM((rows, width), F32), pltpu.VMEM((rows, width), F32),
         pltpu.VMEM((width, half), F32), pltpu.VMEM((half, width), F32),
         pltpu.VMEM((width, wb.shape[2]), BF), pltpu.SemaphoreType.DMA((wb.shape[0],))],
        28,
    )


def hidden_second_body(
    scal, slots_a, slots_b, x_ref, ctx_ref, res_ref, second_ref, up_ref, act_ref, gp_ref, prm_ref,
    wa_hbm, wb_hbm,
    out_ref, gr_ref, gc_ref, eb_ref, sb_ref, keep_ref, send_ref,
    acts, gps, er, rr, om, wa, wb, sem_a, sem_b,
):
    i = pl.program_id(0)
    tokens, width = x_ref.shape[1:]
    half = act_ref.shape[1]
    live = scal[0]

    @pl.when(i == 0)
    def _():
        fetch_blocks(slots_a, wa_hbm, wa, sem_a)
        fetch_blocks(slots_b, wb_hbm, wb, sem_b)
        er[...] = jnp.zeros_like(er)
        rr[...] = jnp.zeros_like(rr)
        om[...] = jnp.zeros_like(om)
        eb_ref[...] = jnp.zeros_like(eb_ref)
        sb_ref[...] = jnp.zeros_like(sb_ref)

    @pl.when(i * NW >= live)
    def _():
        out_ref[...] = x_ref[...]

    @pl.when(i * NW < live)
    def _():
        second = second_ref[...]
        up = up_ref[...]
        res = res_ref[...]

        def ww(c, n):
            return wb[:, c : c + n]

        def wn(c, n):
            return wb[c % width : c % width + n, half + c // width * width :][:, 0:width]

        def bw(c, n):
            r = (half + c) // width
            return prm_ref[8 + r : 9 + r, c % width : c % width + n]

        hidden_chunks(second, up, ww, wn, bw, acts, gps, eb_ref, er, rr)
        o = res + prm_ref[7:8, :]
        for c in range(half // width):
            lanes = slice(c * width, (c + 1) * width)
            o += dot(act_ref[:, lanes], wa[:, width + half + c * width :][:, 0:width])
            o += dot(acts[:, lanes], wb[:, half + c * width :][:, 0:width])
        for w in range(NW):

            @pl.when(i * NW + w < live)
            def _():
                out_ref[w] = o[w * TP : w * TP + tokens].astype(BF)

            @pl.when(i * NW + w >= live)
            def _():
                out_ref[w] = x_ref[w]

        gs = dot(gp_ref[...], wa[:, width : width + half], NT) + dot(gps[...], wb[:, 0:half], NT)
        xhat, inv = normalize(res)
        gres = up.astype(F32) + norm_back(gs, xhat, inv, prm_ref[5:6, :])
        gr_ref[...] = gres
        ga = gres.astype(BF)
        om[...] += dot(ctx_ref[...], ga, TN)
        sb_ref[0:1, :] += jnp.sum(up.astype(F32), axis=0, keepdims=True)
        sb_ref[1:2, :] += jnp.sum(ga.astype(F32), axis=0, keepdims=True)
        gc = dot(ga, wa[:, 0:width], NT)
        for w in range(NW):
            gc_ref[w] = gc[w * TP : (w + 1) * TP].astype(BF)

    @pl.when(i == pl.num_programs(0) - 1)
    def _():
        split_blocks(scal[1], keep_ref, send_ref, 0, er)
        for c in range(half // width):
            split_blocks(scal[1], keep_ref, send_ref, half + c * width, rr.at[c * width : (c + 1) * width])
        split_blocks(scal[1], keep_ref, send_ref, 2 * half, om)


def hidden_second(scal, slots_a, slots_b, x, ctx, res, second, up, act, gp, prm, wa, wb):
    windows, tokens, width = x.shape
    rows = NW * TP
    half = wb.shape[2] // 2
    pairs = wb.shape[0] // 2
    cols = 2 * half + width
    return call(
        hidden_second_body, "hidden_second", (windows // NW,), (scal, slots_a, slots_b),
        (x, ctx, res, second, up, act, gp, prm, wa, wb),
        [win_spec((tokens, width), False), rows_spec(width), rows_spec(width), rows_spec(width),
         rows_spec(width), rows_spec(half), rows_spec(half), whole(prm.shape), any_spec(), any_spec()],
        [sds(x.shape, BF), sds((windows * TP, width), F32), sds((windows, TP, width), BF),
         sds((1, half), F32), sds((2, width), F32),
         sds((pairs, BLK, cols), BF), sds((pairs, BLK, cols), BF)],
        [win_spec((tokens, width), False), rows_spec(width), win_spec((TP, width)),
         whole((1, half)), whole((2, width)), whole((pairs, BLK, cols)), whole((pairs, BLK, cols))],
        [pltpu.VMEM((rows, half), BF), pltpu.VMEM((rows, half), BF),
         pltpu.VMEM((width, half), F32), pltpu.VMEM((half, width), F32), pltpu.VMEM((width, width), F32),
         pltpu.VMEM((width, wa.shape[2]), BF), pltpu.VMEM((width, wb.shape[2]), BF),
         pltpu.SemaphoreType.DMA((wa.shape[0],)), pltpu.SemaphoreType.DMA((wb.shape[0],))],
        34,
    )


def attention_back_body(
    scal, q_ref, k_ref, v_ref, p_ref, gc_ref, first_ref,
    gj_ref, gb_ref, ra_ref, keep_ref, send_ref,
    gjs, pj,
):
    i = pl.program_id(0)
    part = q_ref.shape[2]
    live = scal[0]

    @pl.when(i == 0)
    def _():
        pj[...] = jnp.zeros_like(pj)
        gb_ref[...] = jnp.zeros_like(gb_ref)
        ra_ref[...] = jnp.zeros_like(ra_ref)

    @pl.when(i * NW < live)
    def _():
        masks = head_masks()
        ones = head_ones()
        scale = 32.0**-0.5

        def to_probs(n):
            w, g = n
            lanes = slice(128 * g, 128 * g + 128)
            return dot(gc_ref[w, :, lanes], stack_heads(v_ref[w, :, lanes], ones), NT)

        def softmax_back(n, dp):
            w, g = n
            out = []
            for h in range(4):
                lanes = slice(SEG * h, SEG * (h + 1))
                ph = p_ref[w, g, :, lanes].astype(F32)
                t = dp[:, lanes] * ph
                out.append(t - ph * jnp.sum(t, axis=1, keepdims=True))
            return jnp.concatenate(out, axis=1).astype(BF)

        def combine(r):
            o = jnp.where(masks[0], r[0:TP], 0.0)
            for h in range(1, 4):
                o = jnp.where(masks[h], r[SEG * h : SEG * h + TP], o)
            return o

        def to_joint(n, ds):
            w, g = n
            lanes = slice(128 * g, 128 * g + 128)
            rows = slice(w * TP, (w + 1) * TP)
            keys = stack_heads(k_ref[w, :, lanes], ones)
            gjs[rows, lanes] = dot(ds, keys) * scale
            gjs[rows, part + 128 * g : part + 128 * g + 128] = combine(
                dot(ds, q_ref[w, 0:TP, lanes], TN)
            )
            gjs[rows, 2 * part + 128 * g : 2 * part + 128 * g + 128] = combine(
                dot(p_ref[w, g], gc_ref[w, :, lanes], TN)
            )

        pairs = [(w, g) for g in range(part // 128) for w in range(NW)]
        size = 2
        parts = [pairs[k : k + size] for k in range(0, len(pairs), size)]
        dps = [to_probs(n) for n in parts[0]]
        before = None
        for k, group in enumerate(parts):
            later = [to_probs(n) for n in parts[k + 1]] if k + 1 < len(parts) else None
            dss = [softmax_back(n, dp) for n, dp in zip(group, dps)]
            if before is not None:
                for n, ds in zip(*before):
                    to_joint(n, ds)
            total = dss[0].astype(F32)
            for ds in dss[1:]:
                total += ds.astype(F32)
            ra_ref[group[0][1]] += total
            before = (group, dss)
            dps = later
        for n, ds in zip(*before):
            to_joint(n, ds)
        gj = gjs[...].astype(BF)
        gj_ref[...] = gj
        gb_ref[...] += jnp.sum(gj.astype(F32), axis=0, keepdims=True)
        pj[...] += dot(first_ref[...], gj, TN)

    @pl.when(i == pl.num_programs(0) - 1)
    def _():
        split_blocks(scal[1], keep_ref, send_ref, 0, pj)


def attention_back(scal, which, qkv, p, gc, first):
    windows = qkv.shape[0]
    width = gc.shape[2]
    part = width // 2
    rows = NW * TP
    groups = part // 128
    pairs = width // BLK // 2

    def cols(n, col):
        return pl.BlockSpec((NW, n, part), lambda i, s: (block_at(i, s), 0, col))

    return call(
        attention_back_body, f"attn_back{which}", (windows // NW,), (scal,),
        (qkv, qkv, qkv, p, gc, first),
        [cols(SEG, which), cols(SEG, 2 + which), cols(SEG, 4 + which),
         pl.BlockSpec((NW, groups, TP, 512), lambda i, s: (block_at(i, s), which, 0, 0)),
         cols(TP, which), rows_spec(width)],
        [sds((windows * TP, 3 * part), BF), sds((1, 3 * part), F32), sds((groups, TP, 512), F32),
         sds((pairs, BLK, 3 * part), BF), sds((pairs, BLK, 3 * part), BF)],
        [rows_spec(3 * part), whole((1, 3 * part)), whole((groups, TP, 512)),
         whole((pairs, BLK, 3 * part)), whole((pairs, BLK, 3 * part))],
        [pltpu.VMEM((rows, 3 * part), F32), pltpu.VMEM((width, 3 * part), F32)],
        14,
    )


def input_grad_body(
    tokens, scal, slots, x_ref, u_ref, ga_ref, gb_ref, gr_ref, prm_ref, wq_hbm, gi_ref, xs, wq, sem
):
    i = pl.program_id(0)
    width = x_ref.shape[2]
    live = scal[0]

    @pl.when(i == 0)
    def _():
        xs[...] = jnp.zeros_like(xs)
        fetch_blocks(slots, wq_hbm, wq, sem)

    @pl.when(i * NW >= live)
    def _():
        gi_ref[...] = u_ref[...]

    @pl.when(i * NW < live)
    def _():
        load_rows(xs, x_ref, NW, tokens)
        xhat, inv = normalize(xs[...])
        part = width // 2
        gj = jnp.concatenate(
            [r[:, k * part : (k + 1) * part] for k in range(3) for r in (ga_ref, gb_ref)], axis=1
        )
        gf = dot(gj, wq[:, 0 : 3 * width], NT)
        o = gr_ref[...] + norm_back(gf, xhat, inv, prm_ref[0:1, :])
        for w in range(NW):

            @pl.when(i * NW + w < live)
            def _():
                gi_ref[w] = o[w * TP : w * TP + tokens].astype(BF)

            @pl.when(i * NW + w >= live)
            def _():
                gi_ref[w] = u_ref[w]


def input_grad(scal, slots, x, u, gja, gjb, gr, prm, wq):
    windows, tokens, width = x.shape
    rows = NW * TP
    return call(
        functools.partial(input_grad_body, tokens), "input_grad", (windows // NW,), (scal, slots),
        (x, u, gja, gjb, gr, prm, wq),
        [win_spec((tokens, width)), win_spec((tokens, width), False), rows_spec(3 * width // 2),
         rows_spec(3 * width // 2), rows_spec(width), whole(prm.shape), any_spec()],
        [sds(x.shape, BF)],
        [win_spec((tokens, width), False)],
        [pltpu.VMEM((rows, width), F32), pltpu.VMEM((width, wq.shape[2]), BF),
         pltpu.SemaphoreType.DMA((wq.shape[0],))],
        10,
    )[0]


AXES = ("wide", "narrow")


def exchange(v, mask, n):
    return lax.ppermute(v, AXES, [(i, i ^ mask) for i in range(n)])


def gather_relative(v, n):
    cur = v[None]
    for shift in (3, 1):
        cur = jnp.concatenate(
            [cur] + [exchange(cur, m << shift, n) for m in (1, 2, 3)], axis=0
        )
    return jnp.concatenate([cur, exchange(cur, 1, n)], axis=0)


def relative_slots(me, n):
    m = jnp.arange(n, dtype=jnp.int32) ^ me
    return ((m & 1) << 4) | (((m >> 1) & 3) << 2) | (m >> 3)


def add_split_body(scal, *refs):
    ins, outs = refs[:-4], refs[-4:]
    me = scal[0]
    for m in range(4):
        at = m ^ me
        total = ins[0][0, at].astype(F32)
        for r in ins[1:]:
            total += r[0, at].astype(F32)
        outs[m][0] = total.astype(BF)


def add_split(me, arrays):
    quads, rows, cols = arrays[0].shape[0] // 4, arrays[0].shape[1], arrays[0].shape[2]
    shaped = [a.reshape(quads, 4, rows, cols) for a in arrays]
    spec_in = pl.BlockSpec((1, 4, rows, cols), lambda i, s: (i, 0, 0, 0))
    spec_out = pl.BlockSpec((1, rows, cols), lambda i, s: (i, 0, 0))
    return call(
        add_split_body, "add_split", (quads,), (me.reshape(1),), shaped,
        [spec_in] * len(shaped), [sds((quads, rows, cols), BF)] * 4, [spec_out] * 4, [], 2,
    )


def scatter_sum(keep, send, me, n):
    got = exchange(send, 1, n)
    p = add_split((me >> 1) & 3, [keep, got])
    r = [exchange(p[m], m << 1, n) for m in (1, 2, 3)]
    q = add_split(me >> 3, [p[0]] + r)
    s = [exchange(q[m], m << 3, n) for m in (1, 2, 3)]
    return sum([t[0].astype(F32) for t in s], q[0][0].astype(F32))


def offset_onehot():
    position = jnp.arange(WS * WS, dtype=jnp.int32)
    r, c = position // WS, position % WS
    offset = (
        (r[:, None] - r[None, :] + WS - 1) * (2 * WS - 1) + c[:, None] - c[None, :] + WS - 1
    )
    entries = jnp.arange((2 * WS - 1) ** 2, dtype=jnp.int32)
    return (offset.reshape(-1, 1) == entries[None, :]).astype(BF)


def per_device(
    x, tally, labels, gain1, shift1, wqkv, qbias, vbias, wout, obias,
    gain2, shift2, widen, widen_b, narrow, narrow_b, table, up,
):
    windows, tokens, width = x.shape
    heads, entries = table.shape
    n = lax.axis_size("wide") * lax.axis_size("narrow")
    me = lax.axis_index("wide") * lax.axis_size("narrow") + lax.axis_index("narrow")
    me = me.astype(jnp.int32)
    own = width // n
    fast = own == BLK and n == 32
    half = widen.shape[1] // 2
    pairs = width // BLK // 2

    widen_p = widen.reshape(own, n, 4, own).transpose(0, 2, 1, 3).reshape(own, 4 * width)
    narrow_p = narrow.reshape(4, own, width).transpose(1, 0, 2).reshape(own, 4 * width)
    vectors = [gain1, shift1, qbias, vbias, obias, gain2, shift2, narrow_b]
    small = jnp.concatenate(
        [jnp.stack(vectors, axis=1), widen_b.reshape(4, own).T], axis=1
    )
    small = jnp.pad(small, ((0, 0), (0, 128 - small.shape[1])))
    pay_q = jnp.concatenate([wqkv, small], axis=1)
    pay_a = jnp.concatenate([wout, widen_p[:, :half], narrow_p[:, :half]], axis=1)
    pay_b = jnp.concatenate([widen_p[:, half:], narrow_p[:, half:]], axis=1)

    def gather_plain(v):
        return lax.all_gather(v, AXES, axis=0, tiled=True).reshape(width // BLK, BLK, v.shape[1])

    natural = jnp.arange(width // BLK, dtype=jnp.int32)
    slots = relative_slots(me, n) if fast else natural
    gather = (lambda v: gather_relative(v, n)) if fast else gather_plain
    wq = gather(pay_q)
    wa = gather(pay_a)
    wb = gather_plain(pay_b)

    regions = jnp.pad(labels.astype(F32), ((0, 0), (0, SEG - tokens)), constant_values=-1.0)
    regions = regions[:, None, :]
    onehot = offset_onehot()
    bias = lax.dot_general(table, onehot, NT, preferred_element_type=F32)
    bias = bias.reshape(heads // 4, 4, tokens, tokens).transpose(0, 2, 1, 3)
    bias = jnp.pad(bias, ((0, 0), (0, TP - tokens), (0, 0), (0, SEG - tokens)))
    bias = bias.reshape(heads // 4, TP, 4 * SEG)

    bit = (me & 1) if fast else jnp.int32(0)
    scal = jnp.stack([tally[0], bit])
    first, qkv, p, ctx, prm = attention_forward(scal, slots, x, regions, bias, wq)
    res, second, upm, act, gp, eb1, keep1, send1 = hidden_first(scal, slots, x, up, ctx, prm, wa)
    out, gr, gc, eb2, sb, keep2, send2 = hidden_second(
        scal, slots, natural, x, ctx, res, second, upm, act, gp, prm, wa, wb
    )
    gja, gba, raa, keep3, send3 = attention_back(scal, 0, qkv, p, gc, first)
    gjb, gbb, rab, keep4, send4 = attention_back(scal, 1, qkv, p, gc, first)
    grad_in = input_grad(scal, slots, x, up, gja, gjb, gr, prm, wq)

    ra = jnp.concatenate([raa, rab], axis=0).reshape(heads // 4, TP, 4, SEG)
    ra = ra[:, :tokens, :, :tokens].transpose(0, 2, 1, 3).reshape(heads, -1)
    table_part = lax.dot_general(ra, onehot.astype(F32), NN, precision=lax.Precision.HIGHEST)

    sums = jnp.concatenate(
        [eb1[0], eb2[0], sb[0], sb[1], gba[0], gbb[0], table_part.reshape(-1)]
    )
    sums = lax.psum(sums, AXES)

    def scatter_plain(keep, send):
        v = jnp.stack([keep, send], axis=1).reshape(width, keep.shape[2])
        return lax.psum_scatter(v, AXES, scatter_dimension=0, tiled=True).astype(F32)

    scatter = (lambda k, s: scatter_sum(k, s, me, n)) if fast else scatter_plain
    own1 = scatter(keep1, send1)
    own2 = scatter(keep2, send2)
    own3 = scatter(keep3, send3)
    own4 = scatter(keep4, send4)

    hidden = 4 * width
    eb = sums[:hidden]
    reducebias = sums[hidden : hidden + width]
    outbias = sums[hidden + width : hidden + 2 * width]
    at = hidden + 2 * width
    part = width // 2
    joint_a = sums[at : at + 3 * part].reshape(3, part)
    joint_b = sums[at + 3 * part : at + 6 * part].reshape(3, part)
    joint_bias = jnp.stack([joint_a, joint_b], axis=1).reshape(3 * width)
    grad_table = sums[at + 6 * part :].reshape(heads, entries)

    expander_p = jnp.concatenate([own1[:, :half], own2[:, :half]], axis=1)
    reducer_p = jnp.concatenate([own1[:, half:], own2[:, half : 2 * half]], axis=1)
    outmatrix = own2[:, 2 * half :]
    projector = jnp.stack([own3.reshape(own, 3, part), own4.reshape(own, 3, part)], axis=2)
    projector = projector.reshape(own, 3 * width)

    widen_f = widen_p.astype(F32)
    midshift = jnp.sum(widen_f * eb[None, :], axis=1)
    midgain = jnp.sum(
        widen_f * (expander_p - shift2.astype(F32)[:, None] * eb[None, :]), axis=1
    ) / gain2.astype(F32)
    wqkv_f = wqkv.astype(F32)
    offset_grad = jnp.sum(wqkv_f * joint_bias[None, :], axis=1)
    pregain = jnp.sum(
        wqkv_f * (projector - shift1.astype(F32)[:, None] * joint_bias[None, :]), axis=1
    ) / gain1.astype(F32)

    expander = expander_p.reshape(own, 4, n, own).transpose(0, 2, 1, 3).reshape(own, hidden)
    reducer = reducer_p.reshape(own, 4, width).transpose(1, 0, 2).reshape(4 * own, width)

    def mine(v):
        return lax.dynamic_slice_in_dim(v, me * own, own, 0)

    expandbias = eb.reshape(4, n, own)
    expandbias = lax.dynamic_index_in_dim(expandbias, me, 1, keepdims=False).reshape(-1)
    return (
        out, grad_in, pregain, offset_grad, projector, mine(joint_bias[:width]),
        mine(joint_bias[2 * width :]), outmatrix, mine(outbias), midgain, midshift,
        expander, expandbias, reducer, mine(reducebias), grad_table,
    )


def solution(mesh):
    both = ("wide", "narrow")
    v1, v2, v3 = P(both), P(both, None), P(both, None, None)
    in_specs = (v3, v1, v2, v1, v1, v2, v1, v1, v2, v1, v1, v1, v2, v1, v2, v1, P(), v3)
    out_specs = (v3, v3, v1, v1, v2, v1, v1, v2, v1, v1, v1, v2, v1, v2, v1, P())
    return jax.shard_map(
        per_device, mesh=mesh, in_specs=in_specs, out_specs=out_specs, check_vma=False
    )
```

```python
import functools

import jax
import jax.numpy as jnp
from jax import lax
from jax.experimental import pallas as pl
from jax.experimental.pallas import tpu as pltpu
from jax.sharding import PartitionSpec as P

F32 = jnp.float32
BF = jnp.bfloat16
WS = 10
TP = 104
SEG = 128
BLK = 16
EPS = 1e-5
NW = 4
VMEM = 60 << 20

NT = (((1,), (1,)), ((), ()))
TN = (((0,), (0,)), ((), ()))
NN = (((1,), (0,)), ((), ()))


def dot(a, b, dims=NN):
    return lax.dot_general(a, b, dims, preferred_element_type=F32)


def normalize(v):
    c = v - jnp.mean(v, axis=-1, keepdims=True)
    inv = lax.rsqrt(jnp.mean(c * c, axis=-1, keepdims=True) + EPS)
    return c * inv, inv


def norm_back(g, xhat, inv, gain):
    s = g * gain
    return inv * (
        s
        - jnp.mean(s, axis=-1, keepdims=True)
        - xhat * jnp.mean(s * xhat, axis=-1, keepdims=True)
    )


def head_masks():
    lane = lax.broadcasted_iota(jnp.int32, (1, 128), 1)
    return [(lane // 32) == h for h in range(4)]


def head_ones():
    return [jnp.where(m, 1.0, 0.0).astype(BF) for m in head_masks()]


def stack_heads(v, ones):
    return jnp.concatenate([v * m for m in ones], axis=0)


def load_rows(src_ref):
    return src_ref[...].astype(F32).reshape(NW * TP, src_ref.shape[2])


def fetch_blocks(me, sources, parts, sem):
    copies = []
    for s, src in enumerate(sources):
        for z in range(src.shape[0]):
            m = 8 * z + 2 * (s % 4) + s // 4
            d = m ^ me
            for k, (row, rows, dst, lanes) in enumerate(parts):
                to = pl.ds(pl.multiple_of(d * rows, rows), rows)
                copies.append(
                    pltpu.make_async_copy(
                        src.at[z, pl.ds(row, rows), :], dst.at[to, lanes], sem.at[k, m]
                    )
                )
    for c in copies:
        c.start()
    for c in copies:
        c.wait()


def split_blocks(bit, keep_ref, send_ref, row, rows, acc, cols=None):
    lanes = slice(None) if cols is None else cols
    for k in range(acc.shape[0] // (2 * rows)):
        mine = pl.multiple_of(k * 2 * rows + bit * rows, rows)
        other = pl.multiple_of(k * 2 * rows + (1 - bit) * rows, rows)
        keep_ref[k, row : row + rows, :] = acc[pl.ds(mine, rows), lanes].astype(BF)
        send_ref[k, row : row + rows, :] = acc[pl.ds(other, rows), lanes].astype(BF)


def block_at(i, scal):
    return jnp.minimum(i, (scal[0] + NW - 1) // NW - 1)


def whole(shape):
    return pl.BlockSpec(shape, lambda *a: (0,) * len(shape))


def rows_spec(cols, col=0):
    return pl.BlockSpec((NW * TP, cols), lambda i, scal, *r: (block_at(i, scal), col))


def win_spec(shape, live_only=True):
    if live_only:
        return pl.BlockSpec(
            (NW,) + shape, lambda i, scal, *r: (block_at(i, scal),) + (0,) * len(shape)
        )
    return pl.BlockSpec((NW,) + shape, lambda i, *r: (i,) + (0,) * len(shape))


def any_spec():
    return pl.BlockSpec(memory_space=pl.ANY)


def call(body, name, grid, prefetch, args, in_specs, out_shape, out_specs, scratch, cost, gate=()):
    first = len(prefetch) + len(args)

    def without_gate(*refs):
        body(*refs[:first], *refs[first + len(gate) :])

    return pl.pallas_call(
        without_gate,
        grid_spec=pltpu.PrefetchScalarGridSpec(
            num_scalar_prefetch=len(prefetch),
            grid=grid,
            in_specs=list(in_specs) + [any_spec()] * len(gate),
            out_specs=out_specs,
            scratch_shapes=scratch,
        ),
        out_shape=out_shape,
        compiler_params=pltpu.CompilerParams(vmem_limit_bytes=VMEM),
        cost_estimate=pl.CostEstimate(
            flops=int(cost * 8e8), bytes_accessed=int(cost * 1e6), transcendentals=0
        ),
        name=name,
    )(*prefetch, *args, *gate)


def sds(shape, dtype):
    return jax.ShapeDtypeStruct(shape, dtype)


def attention_body(
    scal, x_ref, reg_ref, bias_ref, *refs
):
    sources, refs = refs[:8], refs[8:]
    first_ref, qkv_ref, p_ref, ctx_ref, prm_ref, bw_ref, js, cs, wq, sem = refs
    i = pl.program_id(0)
    width = x_ref.shape[2]
    rows = NW * TP
    live = scal[0]

    @pl.when(i == 0)
    def _():
        js[rows : rows + SEG - TP, :] = jnp.zeros((SEG - TP, 3 * width), F32)
        fetch_blocks(scal[1], sources, [(0, BLK, wq, slice(None))], sem)
        small = wq[:, 3 * width :].astype(F32)
        shares = jnp.concatenate([small[r : r + 1] for r in range(0, width, BLK)], axis=0)
        count = width // BLK
        place = lax.broadcasted_iota(jnp.int32, (count, width), 1)
        mine = place // BLK == lax.broadcasted_iota(jnp.int32, (count, width), 0)
        source = lax.broadcasted_iota(jnp.int32, (128, width), 0)
        target = lax.broadcasted_iota(jnp.int32, (128, width), 1) % BLK
        for v in range(8):
            pick = jnp.where(source == target + BLK * v, 1.0, 0.0).astype(BF)
            spread = dot(shares.astype(BF), pick)
            prm_ref[v : v + 1, :] = jnp.sum(jnp.where(mine, spread, 0.0), axis=0, keepdims=True)
        left = lax.broadcasted_iota(jnp.int32, (1, 128), 1) < 64
        for k in range(width // (2 * BLK)):
            r = 2 * BLK * k
            right = pltpu.roll(small[r + BLK : r + BLK + 8], 64, 1)[1:2]
            bw_ref[0:1, 128 * k : 128 * k + 128] = jnp.where(left, small[r + 1 : r + 2], right)

    @pl.when(i * NW < live)
    def _():
        xhat, _ = normalize(load_rows(x_ref))
        first = (xhat * prm_ref[0:1, :] + prm_ref[1:2, :]).astype(BF)
        first_ref[...] = first
        scale = 32.0**-0.5
        for part in range(3):
            j = dot(first, wq[:, part * width : (part + 1) * width])
            if part == 0:
                j = (j + prm_ref[2:3, :]) * scale
            if part == 2:
                j = j + prm_ref[3:4, :]
            js[0:rows, part * width : (part + 1) * width] = j
        ones = head_ones()
        eye = lax.broadcasted_iota(jnp.int32, (TP, SEG), 0) == lax.broadcasted_iota(
            jnp.int32, (TP, SEG), 1
        )
        masks = []
        for w in range(NW):
            qkv_ref[w] = js[w * TP : w * TP + SEG, :].astype(BF)
            row = jnp.broadcast_to(reg_ref[w], (TP, SEG))
            col = jnp.max(jnp.where(eye, row, -1.0), axis=1, keepdims=True)
            masks.append(jnp.where(row == col, 0.0, -1e30))

        def scores(n):
            w, g = n
            c = 128 * g
            keys = stack_heads(qkv_ref[w, :, width + c : width + c + 128], ones)
            return dot(qkv_ref[w, 0:TP, c : c + 128], keys, NT)

        def softmax(n, s):
            w, g = n
            out = []
            for h in range(4):
                lanes = slice(SEG * h, SEG * (h + 1))
                sh = s[:, lanes] + bias_ref[g, :, lanes] + masks[w]
                e = jnp.exp(sh - jnp.max(sh, axis=1, keepdims=True))
                out.append((e * (1.0 / jnp.sum(e, axis=1, keepdims=True))).astype(BF))
            p = jnp.concatenate(out, axis=1)
            p_ref[w, g] = p
            return p

        def values(n, p):
            w, g = n
            c = 128 * g
            stacked = stack_heads(qkv_ref[w, :, 2 * width + c : 2 * width + c + 128], ones)
            cs[w * TP : (w + 1) * TP, c : c + 128] = dot(p, stacked)

        pairs = [(w, g) for w in range(NW) for g in range(width // 128)]
        for k in range(0, len(pairs), 8):
            part = pairs[k : k + 8]
            ss = [scores(n) for n in part]
            pp = [softmax(n, s) for n, s in zip(part, ss)]
            for n, p in zip(part, pp):
                values(n, p)
        ctx_ref[...] = cs[...].astype(BF)


def attention_forward(scal, x, regions, bias, sources, gate):
    windows, _, width = x.shape
    rows = NW * TP
    groups = width // 128
    return call(
        attention_body, "attn_fwd", (windows // NW,), (scal,), [x, regions, bias] + sources,
        [win_spec((TP, width)), win_spec((1, SEG)), whole(bias.shape)] + [any_spec()] * 8,
        [sds((windows * TP, width), BF), sds((windows, SEG, 3 * width), BF),
         sds((windows, groups, TP, 512), BF), sds((windows * TP, width), BF),
         sds((8, width), F32), sds((1, 4 * width), F32)],
        [rows_spec(width), win_spec((SEG, 3 * width)), win_spec((groups, TP, 512)), rows_spec(width),
         whole((8, width)), whole((1, 4 * width))],
        [pltpu.VMEM((rows + SEG - TP, 3 * width), F32),
         pltpu.VMEM((rows, width), F32), pltpu.VMEM((width, sources[0].shape[2]), BF),
         pltpu.SemaphoreType.DMA((1, width // BLK))],
        24, gate,
    )


def normal_parts(z):
    return 0.5 + 0.5 * lax.erf(z * 0.7071067811865476), jnp.exp(z * z * -0.5)


def hidden_body(
    tokens, scal, x_ref, u_ref, ctx_ref, prm_ref, bw_ref, *refs
):
    sources, refs = refs[:8], refs[8:]
    out_ref, gr_ref, gc_ref, eb_ref, sb_ref, keep_ref, send_ref = refs[:7]
    acts, gps, er, rr, om, wo, wn, ww, sem = refs[7:]
    i = pl.program_id(0)
    width = x_ref.shape[2]
    hidden = ww.shape[1]
    live = scal[0]
    step = 256

    @pl.when(i == 0)
    def _():
        parts = [(0, BLK, wo, slice(None)), (BLK, 4 * BLK, wn, slice(None))]
        for c in range(4):
            parts.append(((5 + c) * BLK, BLK, ww, slice(c * width, (c + 1) * width)))
        fetch_blocks(scal[1], sources, parts, sem)
        er[...] = jnp.zeros_like(er)
        rr[...] = jnp.zeros_like(rr)
        om[...] = jnp.zeros_like(om)
        eb_ref[...] = jnp.zeros_like(eb_ref)
        sb_ref[...] = jnp.zeros_like(sb_ref)

    @pl.when(i * NW >= live)
    def _():
        out_ref[...] = x_ref[:, 0:tokens, :]

    @pl.when(i * NW < live)
    def _():
        xs = load_rows(x_ref)
        row = lax.broadcasted_iota(jnp.int32, (NW * TP, 1), 0)
        us = jnp.where(row < (live - i * NW) * TP, load_rows(u_ref), 0.0)
        ctx = ctx_ref[...]
        up = us.astype(BF)
        res = xs + dot(ctx, wo[...]) + prm_ref[4:5, :]
        xhat, inv = normalize(res)
        second = (xhat * prm_ref[5:6, :] + prm_ref[6:7, :]).astype(BF)

        def products(c):
            cols = slice(c * step, (c + 1) * step)
            return dot(up, wn[cols, :], NT), dot(second, ww[:, cols])

        def activate(c, ga, z):
            cols = slice(c * step, (c + 1) * step)
            z = z + bw_ref[:, cols]
            phi, bell = normal_parts(z)
            acts[:, cols] = (z * phi).astype(BF)
            gp = (ga * (phi + z * bell * 0.3989422804014327)).astype(BF)
            gps[:, cols] = gp
            eb_ref[:, cols] += jnp.sum(gp.astype(F32), axis=0, keepdims=True)

        count = hidden // step
        t = products(0)
        for c in range(count):
            later = products(c + 1) if c + 1 < count else None
            activate(c, *t)
            t = later
        gs = dot(gps[...], ww[...], NT)
        o = res + dot(acts[...], wn[...]) + prm_ref[7:8, :]
        for w in range(NW):
            out_ref[w] = jnp.where(
                i * NW + w < live, o[w * TP : w * TP + tokens], xs[w * TP : w * TP + tokens]
            ).astype(BF)
        gres = us + norm_back(gs, xhat, inv, prm_ref[5:6, :])
        gr_ref[...] = gres
        ga = gres.astype(BF)
        for c in range(count):
            cols = slice(c * step, (c + 1) * step)
            er[:, cols] += dot(second, gps[:, cols], TN)
            rr[cols, :] += dot(acts[:, cols], up, TN)
        om[...] += dot(ctx, ga, TN)
        sb_ref[0:1, :] += jnp.sum(us, axis=0, keepdims=True)
        sb_ref[1:2, :] += jnp.sum(ga.astype(F32), axis=0, keepdims=True)
        gc = dot(ga, wo[...], NT)
        for w in range(NW):
            gc_ref[w] = gc[w * TP : (w + 1) * TP].astype(BF)

    @pl.when(i == pl.num_programs(0) - 1)
    def _():
        bit = scal[1] & 1
        split_blocks(bit, keep_ref, send_ref, 0, BLK, om)
        split_blocks(bit, keep_ref, send_ref, BLK, 4 * BLK, rr)
        for c in range(4):
            split_blocks(
                bit, keep_ref, send_ref, (5 + c) * BLK, BLK, er, slice(c * width, (c + 1) * width)
            )


def hidden_both(scal, tokens, x, u, ctx, prm, bw, sources):
    windows, _, width = x.shape
    hidden = 4 * width
    rows = NW * TP
    pairs = width // BLK // 2
    share = (pairs, 9 * BLK, width)
    return call(
        functools.partial(hidden_body, tokens), "hidden", (windows // NW,), (scal,),
        [x, u, ctx, prm, bw] + sources,
        [win_spec((TP, width), False), win_spec((TP, width)), rows_spec(width),
         whole(prm.shape), whole(bw.shape)] + [any_spec()] * 8,
        [sds((windows, tokens, width), BF), sds((windows * TP, width), F32), sds((windows, TP, width), BF),
         sds((1, hidden), F32), sds((2, width), F32), sds(share, BF), sds(share, BF)],
        [win_spec((tokens, width), False), rows_spec(width), win_spec((TP, width)),
         whole((1, hidden)), whole((2, width)), whole(share), whole(share)],
        [pltpu.VMEM((rows, hidden), BF), pltpu.VMEM((rows, hidden), BF),
         pltpu.VMEM((width, hidden), F32), pltpu.VMEM((hidden, width), F32), pltpu.VMEM((width, width), F32),
         pltpu.VMEM((width, width), BF), pltpu.VMEM((hidden, width), BF), pltpu.VMEM((width, hidden), BF),
         pltpu.SemaphoreType.DMA((6, 2 * pairs))],
        52,
    )


def three_terms(v):
    hi = v.astype(BF)
    rest = v - hi.astype(F32)
    mid = rest.astype(BF)
    return hi, mid, (rest - mid.astype(F32)).astype(BF)


def table_row(scores):
    side = 2 * WS - 1
    reach = side * (WS - 1) + WS - 1
    j = lax.broadcasted_iota(jnp.int32, (SEG, 256), 0)
    k = lax.broadcasted_iota(jnp.int32, (SEG, 256), 1)
    pick = jnp.where(k == reach - (side * (j // WS) + j % WS), 1.0, 0.0).astype(BF)
    u = sum(dot(t, pick) for t in three_terms(scores))
    u = jnp.concatenate([u, jnp.zeros((TP, 128), F32)], axis=1)
    u = pltpu.roll(u, 0, 1, stride=1, stride_axis=0)
    r = lax.broadcasted_iota(jnp.int32, (16, TP), 0)
    i = lax.broadcasted_iota(jnp.int32, (16, TP), 1)
    group = jnp.where(r == i // WS, 1.0, 0.0).astype(BF)
    v = sum(dot(group, t) for t in three_terms(u))
    skip = side - WS
    low = pltpu.roll(v[0:8], 0, 1, stride=skip, stride_axis=0)
    high = pltpu.roll(v[8:16], 0, 1, stride=skip, stride_axis=0)
    return jnp.sum(low + pltpu.roll(high, 8 * skip, 1), axis=0, keepdims=True)


def attention_back_body(
    scal, qkv_ref, p_ref, gc_ref, first_ref, eb_ref, sb_ref,
    gj_ref, keep_ref, send_ref,
    gjs, pj, gb, ra, small,
):
    i = pl.program_id(0)
    width = gc_ref.shape[2]
    live = scal[0]

    @pl.when(i == 0)
    def _():
        pj[...] = jnp.zeros_like(pj)
        gb[...] = jnp.zeros_like(gb)
        ra[...] = jnp.zeros_like(ra)
        small[...] = jnp.zeros_like(small)

    @pl.when(i * NW < live)
    def _():
        masks = head_masks()
        ones = head_ones()
        scale = 32.0**-0.5

        def lanes_of(g, part=0):
            c = part * width + 128 * g
            return slice(c, c + 128)

        def to_probs(n):
            w, g = n
            stacked = stack_heads(qkv_ref[w, :, lanes_of(g, 2)], ones)
            return dot(gc_ref[w, :, lanes_of(g)], stacked, NT)

        def softmax_back(n, dp):
            w, g = n
            out = []
            for h in range(4):
                lanes = slice(SEG * h, SEG * (h + 1))
                ph = p_ref[w, g, :, lanes].astype(F32)
                t = dp[:, lanes] * ph
                out.append(t - ph * jnp.sum(t, axis=1, keepdims=True))
            return jnp.concatenate(out, axis=1).astype(BF)

        def combine(r):
            o = jnp.where(masks[0], r[0:TP], 0.0)
            for h in range(1, 4):
                o = jnp.where(masks[h], r[SEG * h : SEG * h + TP], o)
            return o

        def to_joint(n, ds):
            w, g = n
            rows = slice(w * TP, (w + 1) * TP)
            keys = stack_heads(qkv_ref[w, :, lanes_of(g, 1)], ones)
            gjs[rows, lanes_of(g)] = dot(ds, keys) * scale
            gjs[rows, lanes_of(g, 1)] = combine(dot(ds, qkv_ref[w, 0:TP, lanes_of(g)], TN))
            gjs[rows, lanes_of(g, 2)] = combine(dot(p_ref[w, g], gc_ref[w, :, lanes_of(g)], TN))

        pairs = [(w, g) for g in range(width // 128) for w in range(NW)]
        size = 2
        parts = [pairs[k : k + size] for k in range(0, len(pairs), size)]
        dps = [to_probs(n) for n in parts[0]]
        before = None
        for k, group in enumerate(parts):
            later = [to_probs(n) for n in parts[k + 1]] if k + 1 < len(parts) else None
            dss = [softmax_back(n, dp) for n, dp in zip(group, dps)]
            if before is not None:
                for n, ds in zip(*before):
                    to_joint(n, ds)
            total = dss[0].astype(F32)
            for ds in dss[1:]:
                total += ds.astype(F32)
            ra[group[0][1]] += total
            before = (group, dss)
            dps = later
        for n, ds in zip(*before):
            to_joint(n, ds)
        gj = gjs[...].astype(BF)
        gj_ref[...] = gj
        gb[...] += jnp.sum(gj.astype(F32), axis=0, keepdims=True)
        pj[...] += dot(first_ref[...], gj, TN)

    @pl.when(i == pl.num_programs(0) - 1)
    def _():
        split_blocks(scal[1] & 1, keep_ref, send_ref, 0, BLK, pj)
        for h in range(width // 32):
            lanes = slice(SEG * (h % 4), SEG * (h % 4 + 1))
            small[h : h + 1, 0:384] = table_row(ra[h // 4, :, lanes])
        small[0:1, 384:1408] = eb_ref[:, 0:1024]
        small[1:2, 384:1408] = eb_ref[:, 1024:2048]
        small[2:3, 384:896] = sb_ref[0:1, :]
        small[2:3, 896:1408] = sb_ref[1:2, :]
        small[3:4, 384:1408] = gb[:, 0:1024]
        small[4:5, 384:896] = gb[:, 1024:1536]
        sums = small[...].astype(BF)
        keep_ref[keep_ref.shape[0] - 1] = sums
        send_ref[send_ref.shape[0] - 1] = sums


def read_small(v):
    table = v[:, 0:384]
    eb = jnp.concatenate([v[0:1, 384:1408], v[1:2, 384:1408]], axis=1)
    gb = jnp.concatenate([v[3:4, 384:1408], v[4:5, 384:896]], axis=1)
    return table, eb, v[2:3, 384:896], v[2:3, 896:1408], gb


def attention_back(scal, qkv, p, gc, first, eb, sb, gate):
    windows = qkv.shape[0]
    width = gc.shape[2]
    rows = NW * TP
    groups = width // 128
    share = (width // BLK // 2 + 1, BLK, 3 * width)
    return call(
        attention_back_body, "attn_back", (windows // NW,), (scal,),
        (qkv, p, gc, first, eb, sb),
        [win_spec((SEG, 3 * width)), win_spec((groups, TP, 512)), win_spec((TP, width)),
         rows_spec(width), whole(eb.shape), whole(sb.shape)],
        [sds((windows * TP, 3 * width), BF), sds(share, BF), sds(share, BF)],
        [rows_spec(3 * width), whole(share), whole(share)],
        [pltpu.VMEM((rows, 3 * width), F32), pltpu.VMEM((width, 3 * width), F32),
         pltpu.VMEM((1, 3 * width), F32), pltpu.VMEM((groups, TP, 512), F32),
         pltpu.VMEM((16, 3 * width), F32)],
        27, gate,
    )


def input_grad_body(tokens, scal, x_ref, u_ref, gj_ref, gr_ref, prm_ref, *refs):
    sources = refs[:8]
    gi_ref, wq, sem = refs[8:]
    i = pl.program_id(0)
    width = x_ref.shape[2]
    live = scal[0]

    @pl.when(i == 0)
    def _():
        fetch_blocks(scal[1], sources, [(0, BLK, wq, slice(None))], sem)

    @pl.when(i * NW >= live)
    def _():
        gi_ref[...] = u_ref[:, 0:tokens, :]

    @pl.when(i * NW < live)
    def _():
        us = load_rows(u_ref)
        xhat, inv = normalize(load_rows(x_ref))
        gf = dot(gj_ref[...], wq[:, 0 : 3 * width], NT)
        o = gr_ref[...] + norm_back(gf, xhat, inv, prm_ref[0:1, :])
        for w in range(NW):
            rows = slice(w * TP, w * TP + tokens)
            gi_ref[w] = jnp.where(i * NW + w < live, o[rows], us[rows]).astype(BF)


def input_grad(scal, tokens, x, u, gj, gr, prm, sources, gate):
    windows, _, width = x.shape
    return call(
        functools.partial(input_grad_body, tokens), "input_grad", (windows // NW,), (scal,),
        [x, u, gj, gr, prm] + sources,
        [win_spec((TP, width)), win_spec((TP, width), False), rows_spec(3 * width),
         rows_spec(width), whole(prm.shape)] + [any_spec()] * 8,
        [sds((windows, tokens, width), BF)],
        [win_spec((tokens, width), False)],
        [pltpu.VMEM((width, sources[0].shape[2]), BF), pltpu.SemaphoreType.DMA((1, width // BLK))],
        12, gate,
    )[0]


AXES = ("wide", "narrow")


def exchange(v, mask, n):
    return lax.ppermute(v, AXES, [(i, i ^ mask) for i in range(n)])


def join_body(scal, *refs):
    out = refs[-1]
    size = refs[0].shape[0]
    for k, r in enumerate(refs[:-1]):
        out[k * size : (k + 1) * size] = r[...]


def join(scal, arrays, gate):
    shape = (arrays[0].shape[0] * len(arrays),) + arrays[0].shape[1:]
    return call(
        join_body, "join", (), (scal,), arrays, [whole(a.shape) for a in arrays],
        [sds(shape, BF)], [whole(shape)], [], 0.01, gate,
    )[0]


def hand_on(scal, arrays, gate):
    count = len(arrays)
    return pl.pallas_call(
        lambda *refs: None,
        grid_spec=pltpu.PrefetchScalarGridSpec(
            num_scalar_prefetch=1,
            grid=(),
            in_specs=[any_spec()] * (count + len(gate)),
            out_specs=[any_spec()] * count,
        ),
        out_shape=[sds(a.shape, a.dtype) for a in arrays],
        input_output_aliases={1 + k: k for k in range(count)},
        name="hand_on",
    )(scal, *arrays, *gate)


def pack_joint_body(scal, wqkv_ref, *refs):
    vectors, out = refs[:-1], refs[-1]
    width = wqkv_ref.shape[1]
    out[0, :, 0:width] = wqkv_ref[...]

    def row(ref, at):
        v = ref[...].astype(F32).reshape(1, ref.shape[0])
        rest = 128 - ref.shape[0] - at
        parts = [jnp.zeros((1, at), F32)] * (at > 0) + [v] + [jnp.zeros((1, rest), F32)] * (rest > 0)
        return jnp.concatenate(parts, axis=1)

    first = sum(row(r, BLK * k) for k, r in enumerate(vectors[:8]))
    small = jnp.concatenate([first, row(vectors[8], 0), jnp.zeros((BLK - 2, 128), F32)], axis=0)
    out[0, :, width:] = small.astype(BF)


def pack_joint(scal, wqkv, vectors):
    rows, width = wqkv.shape
    shape = (1, rows, width + 128)
    args = [wqkv] + vectors
    return call(
        pack_joint_body, "pack_joint", (), (scal,), args, [whole(a.shape) for a in args],
        [sds(shape, BF)], [whole(shape)], [], 0.01,
    )[0]


def pack_hidden_body(scal, wout_ref, narrow_ref, widen_ref, out):
    width = wout_ref.shape[1]
    out[0, 0:BLK] = wout_ref[...]
    out[0, BLK : 5 * BLK] = narrow_ref[...]
    for c in range(4):
        out[0, (5 + c) * BLK : (6 + c) * BLK] = widen_ref[:, c * width : (c + 1) * width]


def pack_hidden(scal, wout, narrow, widen, gate):
    shape = (1, 9 * BLK, wout.shape[1])
    args = [wout, narrow, widen]
    return call(
        pack_hidden_body, "pack_hidden", (), (scal,), args, [whole(a.shape) for a in args],
        [sds(shape, BF)], [whole(shape)], [], 0.01, gate,
    )[0]


def others(v, shift, n):
    return [exchange(v, m << shift, n) for m in (1, 2, 3)]


def total_at(ins, at):
    total = ins[0][at].astype(F32)
    for r in ins[1:]:
        total += r[at].astype(F32)
    return total


def deal_body(count, shift, extra, scal, *refs):
    ins, outs = refs[:count], refs[-4:]
    me = (scal[1] >> shift) & 3
    quads = ins[0].shape[0] // 4
    for q in range(quads):
        for m in range(4):
            outs[m][q] = total_at(ins, 4 * q + (m ^ me)).astype(BF)
    if extra:
        rest = total_at(ins, 4 * quads).astype(BF)
        for m in range(4):
            outs[m][quads] = rest


def deal(scal, arrays, shift, gate):
    blocks, rows, cols = arrays[0].shape
    quads, extra = blocks // 4, blocks % 4
    count = len(arrays)
    if extra or quads == 1:
        grid, spec_in, spec_out = (), whole(arrays[0].shape), whole((quads + extra, rows, cols))
    else:
        grid = (quads,)
        spec_in = pl.BlockSpec((4, rows, cols), lambda i, s: (i, 0, 0))
        spec_out = pl.BlockSpec((1, rows, cols), lambda i, s: (i, 0, 0))
    return call(
        functools.partial(deal_body, count, shift, extra), "deal", grid, (scal,),
        arrays, [spec_in] * count,
        [sds((quads + extra, rows, cols), BF)] * 4, [spec_out] * 4, [], 0.01, gate,
    )


def finish_hidden_body(scal, a, b, c, d, expander_ref, outmatrix_ref, reducer_ref):
    v = total_at([a, b, c, d], 0)
    width = v.shape[1]
    outmatrix_ref[...] = v[0:BLK]
    reducer_ref[...] = v[BLK : 5 * BLK]
    for k in range(4):
        expander_ref[:, k * width : (k + 1) * width] = v[(5 + k) * BLK : (6 + k) * BLK]


def finish_hidden(scal, arrays, gate):
    width = arrays[0].shape[2]
    shapes = [(BLK, 4 * width), (BLK, width), (4 * BLK, width)]
    return call(
        finish_hidden_body, "finish_hidden", (), (scal,), arrays,
        [whole(a.shape) for a in arrays],
        [sds(s, F32) for s in shapes], [whole(s) for s in shapes], [], 0.01, gate,
    )


def finish_joint_body(
    scal, a, b, c, d, wqkv_ref, widen_ref, expander_ref, small_ref,
    projector_ref, table_ref, pregain_ref, shift_ref, qb_ref, vb_ref, ob_ref, midgain_ref,
    midshift_ref, xb_ref, rb_ref,
):
    me = scal[1]
    ins = [a, b, c, d]
    projector = total_at(ins, 0)
    width = projector.shape[1] // 3
    projector_ref[...] = projector
    table, eb, reducebias, outbias, gb = read_small(total_at(ins, 1))
    table_ref[...] = table[:, 0 : table_ref.shape[1]]

    shares = small_ref[0][:, small_ref.shape[2] - 128 :].astype(F32)
    eye = lax.broadcasted_iota(jnp.int32, (BLK, 128), 0)
    lanes = lax.broadcasted_iota(jnp.int32, (BLK, 128), 1)

    def column(k):
        return jnp.sum(jnp.where(lanes == eye + BLK * k, shares[0:1], 0.0), axis=1, keepdims=True)

    def gains(w_ref, grad, bias, shift, gain):
        w = w_ref[...].astype(F32)
        g = jnp.sum(w * (grad - shift * bias), axis=1, keepdims=True) / gain
        return g, jnp.sum(w * bias, axis=1, keepdims=True)

    pregain, offset = gains(wqkv_ref, projector, gb, column(1), column(0))
    midgain, midshift = gains(widen_ref, expander_ref[...], eb, column(6), column(5))
    lane = lax.broadcasted_iota(jnp.int32, (BLK, 128), 1)
    mat = jnp.where(lane == 0, pregain, 0.0)
    for k, v in ((1, offset), (2, midgain), (3, midshift)):
        mat = jnp.where(lane == k, v, mat)
    mat = jnp.transpose(mat)
    for k, r in enumerate((pregain_ref, shift_ref, midgain_ref, midshift_ref)):
        r[...] = mat[k : k + 1, 0:BLK]

    def mine(v, size):
        lanes = v.shape[1]
        v = pltpu.roll(jnp.broadcast_to(v, (8, lanes)), lanes - me * size, 1)
        return v[0:1, 0:size]

    qb_ref[...] = mine(gb[:, 0:width], BLK)
    vb_ref[...] = mine(gb[:, 2 * width : 3 * width], BLK)
    ob_ref[...] = mine(outbias, BLK)
    rb_ref[...] = mine(reducebias, BLK)
    xb_ref[...] = mine(eb, 4 * BLK)


def finish_joint(scal, arrays, wqkv, widen, expander, small, entries):
    args = list(arrays) + [wqkv, widen, expander, small]
    row = (1, BLK)
    shapes = [wqkv.shape, (BLK, entries)] + [row] * 7 + [(1, 4 * BLK), row]
    return call(
        finish_joint_body, "finish_joint", (), (scal,), args, [whole(a.shape) for a in args],
        [sds(s, F32) for s in shapes], [whole(s) for s in shapes], [], 0.01,
    )


def score_bias(table, tokens):
    heads = table.shape[0]
    position = jnp.arange(WS * WS, dtype=jnp.int32)
    r, c = position // WS, position % WS
    offset = (
        (r[:, None] - r[None, :] + WS - 1) * (2 * WS - 1) + c[:, None] - c[None, :] + WS - 1
    )
    entries = jnp.arange((2 * WS - 1) ** 2, dtype=jnp.int32)
    onehot = (offset.reshape(-1, 1) == entries[None, :]).astype(BF)
    bias = lax.dot_general(table, onehot, NT, preferred_element_type=F32)
    bias = bias.reshape(heads // 4, 4, tokens, tokens).transpose(0, 2, 1, 3)
    bias = jnp.pad(bias, ((0, 0), (0, TP - tokens), (0, 0), (0, SEG - tokens)))
    return bias.reshape(heads // 4, TP, 4 * SEG)


def as_sources(v):
    return [v[2 * q + c :: 8] for c in (0, 1) for q in range(4)]


def per_device(
    x, tally, labels, gain1, shift1, wqkv, qbias, vbias, wout, obias,
    gain2, shift2, widen, widen_b, narrow, narrow_b, table, up,
):
    tokens, width = x.shape[1:]
    heads, entries = table.shape
    n = lax.axis_size("wide") * lax.axis_size("narrow")
    me = lax.axis_index("wide") * lax.axis_size("narrow") + lax.axis_index("narrow")
    me = me.astype(jnp.int32)
    own = width // n
    fast = own == BLK and n == 32
    scal = jnp.stack([tally[0], me if fast else jnp.int32(0)])
    blocks = width // BLK

    vectors = [gain1, shift1, qbias, vbias, obias, gain2, shift2, narrow_b]
    bias = score_bias(table, tokens)
    x = jnp.pad(x, ((0, 0), (0, TP - tokens), (0, 0)))
    up = jnp.pad(up, ((0, 0), (0, TP - tokens), (0, 0)))
    regions = jnp.pad(labels.astype(F32), ((0, 0), (0, SEG - tokens)), constant_values=-1.0)
    regions = regions[:, None, :]

    if fast:
        pay_q = pack_joint(scal, wqkv, vectors + [widen_b])
        near_q = join(scal, [pay_q] + others(pay_q, 3, n), [])
        pay_a = pack_hidden(scal, wout, narrow, widen, [pay_q])
        sources_q = [near_q] + others(near_q, 1, n)
        sources_q += [exchange(v, 1, n) for v in sources_q]
        near_a = join(scal, [pay_a] + others(pay_a, 3, n), [x, up, bias, regions] + sources_q[1:4])
        got_a = others(near_a, 1, n)
        start = [near_a]
    else:
        def gather(v):
            return lax.all_gather(v, AXES, axis=0, tiled=True)

        def blocked(v, rows):
            return gather(v).reshape(blocks, rows, -1)

        shares = jnp.stack([gather(v).reshape(blocks, BLK) for v in vectors], axis=1)
        rows = jnp.stack(
            [shares.reshape(blocks, 128), jnp.pad(blocked(widen_b, 64)[:, :, 0], ((0, 0), (0, 64)))], axis=1
        )
        every = jnp.pad(rows, ((0, 0), (0, BLK - 2), (0, 0)))
        sources_q = as_sources(jnp.concatenate([blocked(wqkv, BLK), every], axis=2))
        wide = blocked(widen, BLK).reshape(blocks, BLK, 4, width).transpose(0, 2, 1, 3)
        sources_a = as_sources(
            jnp.concatenate(
                [blocked(wout, BLK), blocked(narrow, 4 * BLK), wide.reshape(blocks, 4 * BLK, width)], axis=1
            )
        )
        start = []

    first, qkv, p, ctx, prm, bw = attention_forward(scal, x, regions, bias, sources_q, start)
    if fast:
        sources_a = list(hand_on(scal, [near_a] + got_a, [ctx]))
        sources_a += [exchange(v, 1, n) for v in sources_a]
    out, gr, gc, eb, sb, keep_h, send_h = hidden_both(scal, tokens, x, up, ctx, prm, bw, sources_a)
    between, last = [], []
    if fast:
        dealt_h = deal(scal, [keep_h, exchange(send_h, 1, n)], 1, [])
        got_h = others_of(dealt_h, 1, n)
        between = [dealt_h[0]]
    gj, keep_j, send_j = attention_back(scal, qkv, p, gc, first, eb, sb, between)
    if fast:
        dealt_h = deal(scal, [dealt_h[0]] + got_h, 3, [keep_j])
        got_h = others_of(dealt_h, 3, n)
        (send_j,) = hand_on(scal, [send_j], [dealt_h[0]])
        dealt_j = deal(scal, [keep_j, exchange(send_j, 1, n)], 1, [])
        got_j = others_of(dealt_j, 1, n)
        last = [dealt_h[0], dealt_j[0]]
    grad_in = input_grad(scal, tokens, x, up, gj, gr, prm, sources_q, last)
    if fast:
        dealt_j = deal(scal, [dealt_j[0]] + got_j, 3, [grad_in] + got_h)
        got_j = others_of(dealt_j, 3, n)
        expander, outmatrix, reducer = finish_hidden(scal, [dealt_h[0]] + got_h, [dealt_j[0]])
        done = finish_joint(scal, [dealt_j[0]] + got_j, wqkv, widen, expander, pay_q, entries)
        projector, grad_table = done[:2]
        pregain, offset, qb, vb, ob, midgain, midshift, xb, rb = [v.reshape(-1) for v in done[2:]]
    else:
        def scatter(v):
            return lax.psum_scatter(v, AXES, scatter_dimension=0, tiled=True).astype(F32)

        def natural(keep, send):
            pairs = blocks // 2
            return jnp.stack([keep[:pairs], send[:pairs]], axis=1).reshape((blocks,) + keep.shape[1:])

        all_h = natural(keep_h, send_h)
        outmatrix = scatter(all_h[:, :BLK].reshape(width, width))
        reducer = scatter(all_h[:, BLK : 5 * BLK].reshape(4 * width, width))
        expander = all_h[:, 5 * BLK :].reshape(blocks, 4, BLK, width).transpose(0, 2, 1, 3)
        expander = scatter(expander.reshape(width, 4 * width))
        projector = scatter(natural(keep_j, send_j).reshape(width, 3 * width))
        sums = lax.psum(keep_j[-1].astype(F32), AXES)
        grad_table, eb, rb, ob, gb = read_small(sums)
        grad_table = grad_table[:, :entries]

        def gains(w, grad, bias, shift, gain):
            w = w.astype(F32)
            g = jnp.sum(w * (grad - shift.astype(F32)[:, None] * bias), axis=1)
            return g / gain.astype(F32), jnp.sum(w * bias, axis=1)

        pregain, offset = gains(wqkv, projector, gb, shift1, gain1)
        midgain, midshift = gains(widen, expander, eb, shift2, gain2)

        def mine(v, size):
            return lax.dynamic_slice_in_dim(v[0], me * size, size, 0)

        qb, vb = mine(gb[:, :width], own), mine(gb[:, 2 * width :], own)
        ob, rb, xb = mine(ob, own), mine(rb, own), mine(eb, 4 * own)
    return (
        out, grad_in, pregain, offset, projector, qb, vb, outmatrix, ob, midgain, midshift,
        expander, xb, reducer, rb, grad_table,
    )


def others_of(dealt, shift, n):
    return [exchange(dealt[m], m << shift, n) for m in (1, 2, 3)]


def solution(mesh):
    both = ("wide", "narrow")
    v1, v2, v3 = P(both), P(both, None), P(both, None, None)
    in_specs = (v3, v1, v2, v1, v1, v2, v1, v1, v2, v1, v1, v1, v2, v1, v2, v1, P(), v3)
    out_specs = (v3, v3, v1, v1, v2, v1, v1, v2, v1, v1, v1, v2, v1, v2, v1, P())
    return jax.shard_map(
        per_device, mesh=mesh, in_specs=in_specs, out_specs=out_specs, check_vma=False
    )
```

```python
import functools

import jax
import jax.numpy as jnp
from jax import lax
from jax.experimental import pallas as pl
from jax.experimental.pallas import tpu as pltpu
from jax.sharding import PartitionSpec as P

F32 = jnp.float32
BF = jnp.bfloat16
WS = 10
TP = 104
SEG = 128
BLK = 16
EPS = 1e-5
NW = 4
VMEM = 60 << 20

NT = (((1,), (1,)), ((), ()))
TN = (((0,), (0,)), ((), ()))
NN = (((1,), (0,)), ((), ()))


def dot(a, b, dims=NN):
    return lax.dot_general(a, b, dims, preferred_element_type=F32)


def normalize(v):
    c = v - jnp.mean(v, axis=-1, keepdims=True)
    inv = lax.rsqrt(jnp.mean(c * c, axis=-1, keepdims=True) + EPS)
    return c * inv, inv


def norm_back(g, xhat, inv, gain):
    s = g * gain
    return inv * (
        s
        - jnp.mean(s, axis=-1, keepdims=True)
        - xhat * jnp.mean(s * xhat, axis=-1, keepdims=True)
    )


def head_masks():
    lane = lax.broadcasted_iota(jnp.int32, (1, 128), 1)
    return [(lane // 32) == h for h in range(4)]


def head_ones():
    return [jnp.where(m, 1.0, 0.0).astype(BF) for m in head_masks()]


def stack_heads(v, ones):
    return jnp.concatenate([v * m for m in ones], axis=0)


def load_rows(src_ref):
    return src_ref[...].astype(F32).reshape(NW * TP, src_ref.shape[2])


def fetch_blocks(me, sources, parts, sem):
    copies = []
    for s, src in enumerate(sources):
        for z in range(src.shape[0]):
            m = 8 * z + 2 * (s % 4) + s // 4
            d = m ^ me
            for k, (row, rows, dst, lanes) in enumerate(parts):
                to = pl.ds(pl.multiple_of(d * rows, rows), rows)
                copies.append(
                    pltpu.make_async_copy(
                        src.at[z, pl.ds(row, rows), :], dst.at[to, lanes], sem.at[k, m]
                    )
                )
    for c in copies:
        c.start()
    for c in copies:
        c.wait()


def split_blocks(bit, keep_ref, send_ref, row, rows, acc, cols=None):
    lanes = slice(None) if cols is None else cols
    for k in range(acc.shape[0] // (2 * rows)):
        mine = pl.multiple_of(k * 2 * rows + bit * rows, rows)
        other = pl.multiple_of(k * 2 * rows + (1 - bit) * rows, rows)
        keep_ref[k, row : row + rows, :] = acc[pl.ds(mine, rows), lanes].astype(BF)
        send_ref[k, row : row + rows, :] = acc[pl.ds(other, rows), lanes].astype(BF)


def block_at(i, scal):
    return jnp.minimum(i, (scal[0] + NW - 1) // NW - 1)


def whole(shape):
    return pl.BlockSpec(shape, lambda *a: (0,) * len(shape))


def rows_spec(cols, col=0):
    return pl.BlockSpec((NW * TP, cols), lambda i, scal, *r: (block_at(i, scal), col))


def win_spec(shape, live_only=True):
    if live_only:
        return pl.BlockSpec(
            (NW,) + shape, lambda i, scal, *r: (block_at(i, scal),) + (0,) * len(shape)
        )
    return pl.BlockSpec((NW,) + shape, lambda i, *r: (i,) + (0,) * len(shape))


def vmem_spec():
    return pl.BlockSpec(memory_space=pltpu.VMEM)


def any_spec():
    return pl.BlockSpec(memory_space=pl.ANY)


def call(
    body, name, grid, prefetch, args, in_specs, out_shape, out_specs, scratch, cost, gate=(), vmem=VMEM
):
    first = len(prefetch) + len(args)

    def without_gate(*refs):
        body(*refs[:first], *refs[first + len(gate) :])

    return pl.pallas_call(
        without_gate,
        grid_spec=pltpu.PrefetchScalarGridSpec(
            num_scalar_prefetch=len(prefetch),
            grid=grid,
            in_specs=list(in_specs) + [any_spec()] * len(gate),
            out_specs=out_specs,
            scratch_shapes=scratch,
        ),
        out_shape=out_shape,
        compiler_params=pltpu.CompilerParams(vmem_limit_bytes=vmem),
        cost_estimate=pl.CostEstimate(
            flops=int(cost * 8e8), bytes_accessed=int(cost * 1e6), transcendentals=0
        ),
        name=name,
    )(*prefetch, *args, *gate)


def small_call(body, name, scal, args, outs, gate=(), far=(), scratch=(), far_out=False):
    first = 1 + len(args) + len(far)

    def without_gate(*refs):
        body(*refs[:first], *refs[first + len(gate) :])

    here = pl.BlockSpec(memory_space=pltpu.VMEM)
    return pl.pallas_call(
        without_gate,
        grid_spec=pltpu.PrefetchScalarGridSpec(
            num_scalar_prefetch=1,
            grid=(),
            in_specs=[here] * len(args) + [whole(a.shape) for a in far] + [any_spec()] * len(gate),
            out_specs=[whole(s) if far_out else here for s, _ in outs],
            scratch_shapes=list(scratch),
        ),
        out_shape=[sds(s, t) if far_out else pltpu.VMEM(s, t) for s, t in outs],
        compiler_params=pltpu.CompilerParams(vmem_limit_bytes=VMEM if far else 12 << 20),
        cost_estimate=pl.CostEstimate(flops=1000, bytes_accessed=1000, transcendentals=0),
        name=name,
    )(scal, *[pltpu.with_memory_space_constraint(a, pltpu.VMEM) for a in args], *far, *gate)


def sds(shape, dtype):
    return jax.ShapeDtypeStruct(shape, dtype)


def attention_body(
    scal, x_ref, reg_ref, bias_ref, *refs
):
    sources, refs = refs[:8], refs[8:]
    first_ref, qkv_ref, p_ref, ctx_ref, prm_ref, bw_ref, js, cs, wq, sem = refs
    i = pl.program_id(0)
    width = x_ref.shape[2]
    rows = NW * TP
    live = scal[0]

    @pl.when(i == 0)
    def _():
        js[rows : rows + SEG - TP, :] = jnp.zeros((SEG - TP, 3 * width), F32)
        fetch_blocks(scal[1], sources, [(0, BLK, wq, slice(None))], sem)
        small = wq[:, 3 * width :].astype(F32)
        shares = jnp.concatenate([small[r : r + 1] for r in range(0, width, BLK)], axis=0)
        count = width // BLK
        place = lax.broadcasted_iota(jnp.int32, (count, width), 1)
        mine = place // BLK == lax.broadcasted_iota(jnp.int32, (count, width), 0)
        source = lax.broadcasted_iota(jnp.int32, (128, width), 0)
        target = lax.broadcasted_iota(jnp.int32, (128, width), 1) % BLK
        for v in range(8):
            pick = jnp.where(source == target + BLK * v, 1.0, 0.0).astype(BF)
            spread = dot(shares.astype(BF), pick)
            prm_ref[v : v + 1, :] = jnp.sum(jnp.where(mine, spread, 0.0), axis=0, keepdims=True)
        left = lax.broadcasted_iota(jnp.int32, (1, 128), 1) < 64
        for k in range(width // (2 * BLK)):
            r = 2 * BLK * k
            right = pltpu.roll(small[r + BLK : r + BLK + 8], 64, 1)[1:2]
            bw_ref[0:1, 128 * k : 128 * k + 128] = jnp.where(left, small[r + 1 : r + 2], right)

    @pl.when(i * NW < live)
    def _():
        xhat, _ = normalize(load_rows(x_ref))
        first = (xhat * prm_ref[0:1, :] + prm_ref[1:2, :]).astype(BF)
        first_ref[...] = first
        scale = 32.0**-0.5
        for part in range(3):
            j = dot(first, wq[:, part * width : (part + 1) * width])
            if part == 0:
                j = (j + prm_ref[2:3, :]) * scale
            if part == 2:
                j = j + prm_ref[3:4, :]
            js[0:rows, part * width : (part + 1) * width] = j
        ones = head_ones()
        eye = lax.broadcasted_iota(jnp.int32, (TP, SEG), 0) == lax.broadcasted_iota(
            jnp.int32, (TP, SEG), 1
        )
        masks = []
        for w in range(NW):
            qkv_ref[w] = js[w * TP : w * TP + SEG, :].astype(BF)
            row = reg_ref[pl.ds(i * NW + w, 1), :].astype(F32)
            row = jnp.concatenate([row, jnp.full((1, SEG - row.shape[1]), -1.0, F32)], axis=1)
            row = jnp.broadcast_to(row, (TP, SEG))
            col = jnp.max(jnp.where(eye, row, -1.0), axis=1, keepdims=True)
            masks.append(jnp.where(row == col, 0.0, -1e30))

        def scores(n):
            w, g = n
            c = 128 * g
            keys = stack_heads(qkv_ref[w, :, width + c : width + c + 128], ones)
            return dot(qkv_ref[w, 0:TP, c : c + 128], keys, NT)

        def softmax(n, s):
            w, g = n
            out = []
            for h in range(4):
                lanes = slice(SEG * h, SEG * (h + 1))
                sh = s[:, lanes] + bias_ref[g, :, lanes] + masks[w]
                e = jnp.exp(sh - jnp.max(sh, axis=1, keepdims=True))
                out.append((e * (1.0 / jnp.sum(e, axis=1, keepdims=True))).astype(BF))
            p_ref[w, g] = jnp.concatenate(out, axis=1)

        def values(n):
            w, g = n
            c = 128 * g
            stacked = stack_heads(qkv_ref[w, :, 2 * width + c : 2 * width + c + 128], ones)
            cs[w * TP : (w + 1) * TP, c : c + 128] = dot(p_ref[w, g], stacked)

        pairs = [(w, g) for w in range(NW) for g in range(width // 128)]
        lag = 3
        ss = {}
        for k in range(len(pairs) + lag + 1):
            if k < len(pairs):
                ss[k] = scores(pairs[k])
            if 0 <= k - 1 - lag < len(pairs):
                values(pairs[k - 1 - lag])
            if 0 <= k - lag < len(pairs):
                softmax(pairs[k - lag], ss.pop(k - lag))
        ctx_ref[...] = cs[...].astype(BF)


def attention_forward(scal, x, regions, bias, sources, gate):
    windows, _, width = x.shape
    rows = NW * TP
    groups = width // 128
    return call(
        attention_body, "attn_fwd", (windows // NW,), (scal,), [x, regions, bias] + sources,
        [win_spec((TP, width)), whole(regions.shape), whole(bias.shape)] + [any_spec()] * 8,
        [sds((windows * TP, width), BF), sds((windows, SEG, 3 * width), BF),
         sds((windows, groups, TP, 512), BF), sds((windows * TP, width), BF),
         sds((8, width), F32), sds((1, 4 * width), F32)],
        [rows_spec(width), win_spec((SEG, 3 * width)), win_spec((groups, TP, 512)), rows_spec(width),
         whole((8, width)), whole((1, 4 * width))],
        [pltpu.VMEM((rows + SEG - TP, 3 * width), F32),
         pltpu.VMEM((rows, width), F32), pltpu.VMEM((width, sources[0].shape[2]), BF),
         pltpu.SemaphoreType.DMA((1, width // BLK))],
        24, gate,
    )


def normal_parts(z):
    return 0.5 + 0.5 * lax.erf(z * 0.7071067811865476), jnp.exp(z * z * -0.5)


def hidden_body(
    tokens, scal, x_ref, u_ref, ctx_ref, prm_ref, bw_ref, *refs
):
    sources, refs = refs[:8], refs[8:]
    out_ref, gr_ref, gc_ref, eb_ref, sb_ref, keep_ref, send_ref = refs[:7]
    acts, gps, er, rr, om, wo, wn, ww, sem = refs[7:]
    i = pl.program_id(0)
    width = x_ref.shape[2]
    hidden = ww.shape[1]
    live = scal[0]
    step = 256

    @pl.when(i == 0)
    def _():
        parts = [(0, BLK, wo, slice(None)), (BLK, 4 * BLK, wn, slice(None))]
        for c in range(4):
            parts.append(((5 + c) * BLK, BLK, ww, slice(c * width, (c + 1) * width)))
        fetch_blocks(scal[1], sources, parts, sem)
        er[...] = jnp.zeros_like(er)
        rr[...] = jnp.zeros_like(rr)
        om[...] = jnp.zeros_like(om)
        eb_ref[...] = jnp.zeros_like(eb_ref)
        sb_ref[...] = jnp.zeros_like(sb_ref)

    @pl.when(i * NW >= live)
    def _():
        out_ref[...] = x_ref[:, 0:tokens, :]

    @pl.when(i * NW < live)
    def _():
        xs = load_rows(x_ref)
        row = lax.broadcasted_iota(jnp.int32, (NW * TP, 1), 0)
        us = jnp.where(row < (live - i * NW) * TP, load_rows(u_ref), 0.0)
        ctx = ctx_ref[...]
        up = us.astype(BF)
        res = xs + dot(ctx, wo[...]) + prm_ref[4:5, :]
        xhat, inv = normalize(res)
        second = (xhat * prm_ref[5:6, :] + prm_ref[6:7, :]).astype(BF)

        def products(c):
            cols = slice(c * step, (c + 1) * step)
            return dot(up, wn[cols, :], NT), dot(second, ww[:, cols])

        def activate(c, ga, z):
            cols = slice(c * step, (c + 1) * step)
            z = z + bw_ref[:, cols]
            phi, bell = normal_parts(z)
            acts[:, cols] = (z * phi).astype(BF)
            gp = (ga * (phi + z * bell * 0.3989422804014327)).astype(BF)
            gps[:, cols] = gp
            eb_ref[:, cols] += jnp.sum(gp.astype(F32), axis=0, keepdims=True)

        count = hidden // step
        t = products(0)
        for c in range(count):
            later = products(c + 1) if c + 1 < count else None
            activate(c, *t)
            t = later
        gs = dot(gps[...], ww[...], NT)
        o = res + dot(acts[...], wn[...]) + prm_ref[7:8, :]
        for w in range(NW):
            out_ref[w] = jnp.where(
                i * NW + w < live, o[w * TP : w * TP + tokens], xs[w * TP : w * TP + tokens]
            ).astype(BF)
        gres = us + norm_back(gs, xhat, inv, prm_ref[5:6, :])
        ga = gres.astype(BF)
        gr_ref[...] = ga
        for c in range(count):
            cols = slice(c * step, (c + 1) * step)
            er[:, cols] += dot(second, gps[:, cols], TN)
            rr[cols, :] += dot(acts[:, cols], up, TN)
        om[...] += dot(ctx, ga, TN)
        sb_ref[0:1, :] += jnp.sum(us, axis=0, keepdims=True)
        sb_ref[1:2, :] += jnp.sum(ga.astype(F32), axis=0, keepdims=True)
        gc = dot(ga, wo[...], NT)
        for w in range(NW):
            gc_ref[w] = gc[w * TP : (w + 1) * TP].astype(BF)

    @pl.when(i == pl.num_programs(0) - 1)
    def _():
        bit = scal[1] & 1
        split_blocks(bit, keep_ref, send_ref, 0, BLK, om)
        split_blocks(bit, keep_ref, send_ref, BLK, 4 * BLK, rr)
        for c in range(4):
            split_blocks(
                bit, keep_ref, send_ref, (5 + c) * BLK, BLK, er, slice(c * width, (c + 1) * width)
            )


def hidden_both(scal, tokens, x, u, ctx, prm, bw, sources):
    windows, _, width = x.shape
    hidden = 4 * width
    rows = NW * TP
    pairs = width // BLK // 2
    share = (pairs, 9 * BLK, width)
    return call(
        functools.partial(hidden_body, tokens), "hidden", (windows // NW,), (scal,),
        [x, u, ctx, prm, bw] + sources,
        [win_spec((TP, width), False), win_spec((TP, width)), rows_spec(width),
         whole(prm.shape), whole(bw.shape)] + [any_spec()] * 8,
        [sds((windows, tokens, width), BF), sds((windows * TP, width), BF), sds((windows, TP, width), BF),
         sds((1, hidden), F32), sds((2, width), F32), pltpu.VMEM(share, BF), pltpu.VMEM(share, BF)],
        [win_spec((tokens, width), False), rows_spec(width), win_spec((TP, width)),
         whole((1, hidden)), whole((2, width)), vmem_spec(), vmem_spec()],
        [pltpu.VMEM((rows, hidden), BF), pltpu.VMEM((rows, hidden), BF),
         pltpu.VMEM((width, hidden), F32), pltpu.VMEM((hidden, width), F32), pltpu.VMEM((width, width), F32),
         pltpu.VMEM((width, width), BF), pltpu.VMEM((hidden, width), BF), pltpu.VMEM((width, hidden), BF),
         pltpu.SemaphoreType.DMA((6, 2 * pairs))],
        52, (), 52 << 20,
    )


def three_terms(v):
    hi = v.astype(BF)
    rest = v - hi.astype(F32)
    mid = rest.astype(BF)
    return hi, mid, (rest - mid.astype(F32)).astype(BF)


def table_row(scores):
    side = 2 * WS - 1
    reach = side * (WS - 1) + WS - 1
    j = lax.broadcasted_iota(jnp.int32, (SEG, 256), 0)
    k = lax.broadcasted_iota(jnp.int32, (SEG, 256), 1)
    pick = jnp.where(k == reach - (side * (j // WS) + j % WS), 1.0, 0.0).astype(BF)
    u = sum(dot(t, pick) for t in three_terms(scores))
    u = jnp.concatenate([u, jnp.zeros((TP, 128), F32)], axis=1)
    u = pltpu.roll(u, 0, 1, stride=1, stride_axis=0)
    r = lax.broadcasted_iota(jnp.int32, (16, TP), 0)
    i = lax.broadcasted_iota(jnp.int32, (16, TP), 1)
    group = jnp.where(r == i // WS, 1.0, 0.0).astype(BF)
    v = sum(dot(group, t) for t in three_terms(u))
    skip = side - WS
    low = pltpu.roll(v[0:8], 0, 1, stride=skip, stride_axis=0)
    high = pltpu.roll(v[8:16], 0, 1, stride=skip, stride_axis=0)
    return jnp.sum(low + pltpu.roll(high, 8 * skip, 1), axis=0, keepdims=True)


def attention_back_body(
    scal, qkv_ref, p_ref, gc_ref, first_ref, eb_ref, sb_ref,
    gj_ref, keep_ref, send_ref,
    gjs, pj, gb, ra, small,
):
    i = pl.program_id(0)
    width = gc_ref.shape[2]
    live = scal[0]

    @pl.when(i == 0)
    def _():
        pj[...] = jnp.zeros_like(pj)
        gb[...] = jnp.zeros_like(gb)
        ra[...] = jnp.zeros_like(ra)
        small[...] = jnp.zeros_like(small)

    @pl.when(i * NW < live)
    def _():
        masks = head_masks()
        ones = head_ones()
        scale = 32.0**-0.5

        def lanes_of(g, part=0):
            c = part * width + 128 * g
            return slice(c, c + 128)

        def to_probs(n):
            w, g = n
            stacked = stack_heads(qkv_ref[w, :, lanes_of(g, 2)], ones)
            return dot(gc_ref[w, :, lanes_of(g)], stacked, NT)

        def softmax_back(n, dp):
            w, g = n
            out = []
            for h in range(4):
                lanes = slice(SEG * h, SEG * (h + 1))
                ph = p_ref[w, g, :, lanes].astype(F32)
                t = dp[:, lanes] * ph
                out.append(t - ph * jnp.sum(t, axis=1, keepdims=True))
            return jnp.concatenate(out, axis=1).astype(BF)

        def combine(r):
            o = jnp.where(masks[0], r[0:TP], 0.0)
            for h in range(1, 4):
                o = jnp.where(masks[h], r[SEG * h : SEG * h + TP], o)
            return o

        def to_joint(n, ds):
            w, g = n
            rows = slice(w * TP, (w + 1) * TP)
            keys = stack_heads(qkv_ref[w, :, lanes_of(g, 1)], ones)
            gjs[rows, lanes_of(g)] = dot(ds, keys) * scale
            gjs[rows, lanes_of(g, 1)] = combine(dot(ds, qkv_ref[w, 0:TP, lanes_of(g)], TN))
            gjs[rows, lanes_of(g, 2)] = combine(dot(p_ref[w, g], gc_ref[w, :, lanes_of(g)], TN))

        pairs = [(w, g) for g in range(width // 128) for w in range(NW)]
        size = 2
        parts = [pairs[k : k + size] for k in range(0, len(pairs), size)]
        dps = [to_probs(n) for n in parts[0]]
        before = None
        for k, group in enumerate(parts):
            later = [to_probs(n) for n in parts[k + 1]] if k + 1 < len(parts) else None
            dss = [softmax_back(n, dp) for n, dp in zip(group, dps)]
            if before is not None:
                for n, ds in zip(*before):
                    to_joint(n, ds)
            total = dss[0].astype(F32)
            for ds in dss[1:]:
                total += ds.astype(F32)
            ra[group[0][1]] += total
            before = (group, dss)
            dps = later
        for n, ds in zip(*before):
            to_joint(n, ds)
        gj = gjs[...].astype(BF)
        gj_ref[...] = gj
        gb[...] += jnp.sum(gj.astype(F32), axis=0, keepdims=True)
        pj[...] += dot(first_ref[...], gj, TN)

    @pl.when(i == pl.num_programs(0) - 1)
    def _():
        split_blocks(scal[1] & 1, keep_ref, send_ref, 0, BLK, pj)
        for h in range(width // 32):
            lanes = slice(SEG * (h % 4), SEG * (h % 4 + 1))
            small[h : h + 1, 0:384] = table_row(ra[h // 4, :, lanes])
        small[0:1, 384:1408] = eb_ref[:, 0:1024]
        small[1:2, 384:1408] = eb_ref[:, 1024:2048]
        small[2:3, 384:896] = sb_ref[0:1, :]
        small[2:3, 896:1408] = sb_ref[1:2, :]
        small[3:4, 384:1408] = gb[:, 0:1024]
        small[4:5, 384:896] = gb[:, 1024:1536]
        sums = small[...].astype(BF)
        keep_ref[keep_ref.shape[0] - 1] = sums
        send_ref[send_ref.shape[0] - 1] = sums


def read_small(v):
    table = v[:, 0:384]
    eb = jnp.concatenate([v[0:1, 384:1408], v[1:2, 384:1408]], axis=1)
    gb = jnp.concatenate([v[3:4, 384:1408], v[4:5, 384:896]], axis=1)
    return table, eb, v[2:3, 384:896], v[2:3, 896:1408], gb


def attention_back(scal, qkv, p, gc, first, eb, sb, gate):
    windows = qkv.shape[0]
    width = gc.shape[2]
    rows = NW * TP
    groups = width // 128
    share = (width // BLK // 2 + 1, BLK, 3 * width)
    return call(
        attention_back_body, "attn_back", (windows // NW,), (scal,),
        (qkv, p, gc, first, eb, sb),
        [win_spec((SEG, 3 * width)), win_spec((groups, TP, 512)), win_spec((TP, width)),
         rows_spec(width), whole(eb.shape), whole(sb.shape)],
        [sds((windows * TP, 3 * width), BF), pltpu.VMEM(share, BF), pltpu.VMEM(share, BF)],
        [rows_spec(3 * width), vmem_spec(), vmem_spec()],
        [pltpu.VMEM((rows, 3 * width), F32), pltpu.VMEM((width, 3 * width), F32),
         pltpu.VMEM((1, 3 * width), F32), pltpu.VMEM((groups, TP, 512), F32),
         pltpu.VMEM((16, 3 * width), F32)],
        27, gate, 56 << 20,
    )


def input_grad_body(tokens, scal, x_ref, u_ref, gj_ref, gr_ref, prm_ref, *refs):
    sources = refs[:8]
    gi_ref, wq, sem = refs[8:]
    i = pl.program_id(0)
    width = x_ref.shape[2]
    live = scal[0]

    @pl.when(i == 0)
    def _():
        fetch_blocks(scal[1], sources, [(0, BLK, wq, slice(None))], sem)

    @pl.when(i * NW >= live)
    def _():
        gi_ref[...] = u_ref[:, 0:tokens, :]

    @pl.when(i * NW < live)
    def _():
        us = load_rows(u_ref)
        xhat, inv = normalize(load_rows(x_ref))
        gf = dot(gj_ref[...], wq[:, 0 : 3 * width], NT)
        o = gr_ref[...].astype(F32) + norm_back(gf, xhat, inv, prm_ref[0:1, :])
        for w in range(NW):
            rows = slice(w * TP, w * TP + tokens)
            gi_ref[w] = jnp.where(i * NW + w < live, o[rows], us[rows]).astype(BF)


def input_grad(scal, tokens, x, u, gj, gr, prm, sources, gate):
    windows, _, width = x.shape
    return call(
        functools.partial(input_grad_body, tokens), "input_grad", (windows // NW,), (scal,),
        [x, u, gj, gr, prm] + sources,
        [win_spec((TP, width)),
         pl.BlockSpec(
             (NW, TP, width),
             lambda i, s: (jnp.maximum(i, jnp.minimum(s[0] // NW, windows // NW - 1)), 0, 0),
         ),
         rows_spec(3 * width), rows_spec(width), whole(prm.shape)] + [any_spec()] * 8,
        [sds((windows, tokens, width), BF)],
        [win_spec((tokens, width), False)],
        [pltpu.VMEM((width, sources[0].shape[2]), BF), pltpu.SemaphoreType.DMA((1, width // BLK))],
        12, gate,
    )[0]


AXES = ("wide", "narrow")


def exchange(v, mask, n):
    return lax.ppermute(v, AXES, [(i, i ^ mask) for i in range(n)])


def join_body(scal, *refs):
    out = refs[-1]
    size = refs[0].shape[0]
    for k, r in enumerate(refs[:-1]):
        out[k * size : (k + 1) * size] = r[...]


def join(scal, arrays, gate):
    shape = (arrays[0].shape[0] * len(arrays),) + arrays[0].shape[1:]
    return small_call(join_body, "join", scal, arrays, [(shape, BF)], gate)[0]


def hand_on(scal, arrays, gate):
    count = len(arrays)
    return pl.pallas_call(
        lambda *refs: None,
        grid_spec=pltpu.PrefetchScalarGridSpec(
            num_scalar_prefetch=1,
            grid=(),
            in_specs=[any_spec()] * (count + len(gate)),
            out_specs=[any_spec()] * count,
        ),
        out_shape=[sds(a.shape, a.dtype) for a in arrays],
        input_output_aliases={1 + k: k for k in range(count)},
        name="hand_on",
    )(scal, *arrays, *gate)


def pack_joint_body(scal, wqkv_ref, *refs):
    vectors, out = refs[:-1], refs[-1]
    width = wqkv_ref.shape[1]
    out[0, :, 0:width] = wqkv_ref[...]

    def row(ref, at):
        v = ref[...].astype(F32).reshape(1, ref.shape[0])
        rest = 128 - ref.shape[0] - at
        parts = [jnp.zeros((1, at), F32)] * (at > 0) + [v] + [jnp.zeros((1, rest), F32)] * (rest > 0)
        return jnp.concatenate(parts, axis=1)

    first = sum(row(r, BLK * k) for k, r in enumerate(vectors[:8]))
    small = jnp.concatenate([first, row(vectors[8], 0), jnp.zeros((BLK - 2, 128), F32)], axis=0)
    out[0, :, width:] = small.astype(BF)


def pack_joint(scal, wqkv, vectors):
    rows, width = wqkv.shape
    outs = [((1, rows, width + 128), BF)]
    return small_call(pack_joint_body, "pack_joint", scal, [], outs, far=[wqkv] + vectors)[0]


def pack_hidden_body(scal, wout_ref, narrow_ref, widen_ref, out):
    width = wout_ref.shape[1]
    out[0, 0:BLK] = wout_ref[...]
    out[0, BLK : 5 * BLK] = narrow_ref[...]
    for c in range(4):
        out[0, (5 + c) * BLK : (6 + c) * BLK] = widen_ref[:, c * width : (c + 1) * width]


def pack_hidden(scal, wout, narrow, widen, gate):
    shape = (1, 9 * BLK, wout.shape[1])
    args = [wout, narrow, widen]
    return small_call(pack_hidden_body, "pack_hidden", scal, [], [(shape, BF)], gate, far=args)[0]


def others(v, shift, n):
    return [exchange(v, m << shift, n) for m in (1, 2, 3)]


def total_at(ins, at):
    total = ins[0][at].astype(F32)
    for r in ins[1:]:
        total += r[at].astype(F32)
    return total


def deal_body(count, shift, extra, scal, *refs):
    ins, outs = refs[:count], refs[-4:]
    me = (scal[1] >> shift) & 3
    quads = ins[0].shape[0] // 4
    for q in range(quads):
        for m in range(4):
            outs[m][q] = total_at(ins, 4 * q + (m ^ me)).astype(BF)
    if extra:
        rest = total_at(ins, 4 * quads).astype(BF)
        for m in range(4):
            outs[m][quads] = rest


def deal(scal, arrays, shift, gate):
    blocks, rows, cols = arrays[0].shape
    quads, extra = blocks // 4, blocks % 4
    body = functools.partial(deal_body, len(arrays), shift, extra)
    return small_call(body, "deal", scal, arrays, [((quads + extra, rows, cols), BF)] * 4, gate)


def finish_hidden_body(scal, a, b, c, d, expander_ref, outmatrix_ref, reducer_ref):
    v = total_at([a, b, c, d], 0)
    width = v.shape[1]
    outmatrix_ref[...] = v[0:BLK]
    reducer_ref[...] = v[BLK : 5 * BLK]
    for k in range(4):
        expander_ref[:, k * width : (k + 1) * width] = v[(5 + k) * BLK : (6 + k) * BLK]


def finish_hidden(scal, arrays, gate):
    width = arrays[0].shape[2]
    shapes = [(BLK, 4 * width), (BLK, width), (4 * BLK, width)]
    return small_call(
        finish_hidden_body, "finish_hidden", scal, arrays, [(s, F32) for s in shapes], gate, far_out=True
    )


def finish_joint_body(
    scal, a, b, c, d, wqkv_ref, widen_ref, expander_ref, small_ref,
    projector_ref, table_ref, pregain_ref, shift_ref, qb_ref, vb_ref, ob_ref, midgain_ref,
    midshift_ref, xb_ref, rb_ref,
):
    me = scal[1]
    ins = [a, b, c, d]
    projector = total_at(ins, 0)
    width = projector.shape[1] // 3
    projector_ref[...] = projector
    table, eb, reducebias, outbias, gb = read_small(total_at(ins, 1))
    table_ref[...] = table[:, 0 : table_ref.shape[1]]

    shares = small_ref[0][:, small_ref.shape[2] - 128 :].astype(F32)
    eye = lax.broadcasted_iota(jnp.int32, (BLK, 128), 0)
    lanes = lax.broadcasted_iota(jnp.int32, (BLK, 128), 1)

    def column(k):
        return jnp.sum(jnp.where(lanes == eye + BLK * k, shares[0:1], 0.0), axis=1, keepdims=True)

    def gains(w_ref, grad, bias, shift, gain):
        w = w_ref[...].astype(F32)
        g = jnp.sum(w * (grad - shift * bias), axis=1, keepdims=True) / gain
        return g, jnp.sum(w * bias, axis=1, keepdims=True)

    pregain, offset = gains(wqkv_ref, projector, gb, column(1), column(0))
    midgain, midshift = gains(widen_ref, expander_ref[...], eb, column(6), column(5))
    lane = lax.broadcasted_iota(jnp.int32, (BLK, 128), 1)
    mat = jnp.where(lane == 0, pregain, 0.0)
    for k, v in ((1, offset), (2, midgain), (3, midshift)):
        mat = jnp.where(lane == k, v, mat)
    mat = jnp.transpose(mat)
    for k, r in enumerate((pregain_ref, shift_ref, midgain_ref, midshift_ref)):
        r[...] = mat[k : k + 1, 0:BLK]

    def mine(v, size):
        lanes = v.shape[1]
        v = pltpu.roll(jnp.broadcast_to(v, (8, lanes)), lanes - me * size, 1)
        return v[0:1, 0:size]

    qb_ref[...] = mine(gb[:, 0:width], BLK)
    vb_ref[...] = mine(gb[:, 2 * width : 3 * width], BLK)
    ob_ref[...] = mine(outbias, BLK)
    rb_ref[...] = mine(reducebias, BLK)
    xb_ref[...] = mine(eb, 4 * BLK)


def finish_joint(scal, arrays, wqkv, widen, expander, small, entries):
    row = (1, BLK)
    shapes = [wqkv.shape, (BLK, entries)] + [row] * 7 + [(1, 4 * BLK), row]
    return small_call(
        finish_joint_body, "finish_joint", scal, arrays, [(s, F32) for s in shapes],
        far=[wqkv, widen, expander, small], far_out=True,
    )


def score_bias_body(scal, table_ref, bias_ref):
    side = 2 * WS - 1
    reach = side * (WS - 1) + WS - 1
    heads, entries = table_ref.shape
    i = lax.broadcasted_iota(jnp.int32, (TP, 384), 0)
    e = lax.broadcasted_iota(jnp.int32, (TP, 384), 1)
    pick = jnp.where(e == reach + side * (i // WS) + i % WS, 1.0, 0.0).astype(BF)
    j = lax.broadcasted_iota(jnp.int32, (SEG, 16), 0)
    r = lax.broadcasted_iota(jnp.int32, (SEG, 16), 1)
    group = jnp.where(r == j // WS, 1.0, 0.0).astype(BF)
    table = jnp.concatenate(
        [table_ref[...].astype(F32), jnp.zeros((heads, 384 - entries), F32)], axis=1
    )
    skip = side - WS
    for h in range(heads):
        t = jnp.broadcast_to(table[h : h + 1], (8, 384))
        low = pltpu.roll(t, 0, 1, stride=skip, stride_axis=0)
        v = jnp.concatenate([low, pltpu.roll(low, 8 * skip, 1)], axis=0).astype(BF)
        u = pltpu.roll(dot(group, v), 0, 1, stride=1, stride_axis=0).astype(BF)
        bias_ref[h // 4, :, SEG * (h % 4) : SEG * (h % 4 + 1)] = dot(pick, u, NT)


def score_bias(scal, table, gate):
    heads = table.shape[0]
    shape = (heads // 4, TP, 4 * SEG)
    return small_call(
        score_bias_body, "score_bias", scal, [], [(shape, F32)], gate, far=[table], far_out=True
    )[0]


def by_window(v):
    return jnp.pad(v, ((0, 0), (0, TP - v.shape[1]), (0, 0)))


def as_sources(v):
    return [v[2 * q + c :: 8] for c in (0, 1) for q in range(4)]


def per_device(
    x, tally, labels, gain1, shift1, wqkv, qbias, vbias, wout, obias,
    gain2, shift2, widen, widen_b, narrow, narrow_b, table, up,
):
    tokens, width = x.shape[1:]
    heads, entries = table.shape
    n = lax.axis_size("wide") * lax.axis_size("narrow")
    me = lax.axis_index("wide") * lax.axis_size("narrow") + lax.axis_index("narrow")
    me = me.astype(jnp.int32)
    own = width // n
    fast = own == BLK and n == 32
    scal = jnp.stack([tally[0], me if fast else jnp.int32(0)])
    blocks = width // BLK

    vectors = [gain1, shift1, qbias, vbias, obias, gain2, shift2, narrow_b]
    if fast:
        pay_q = pack_joint(scal, wqkv, vectors + [widen_b])
        pay_a = pack_hidden(scal, wout, narrow, widen, [pay_q])
        x = by_window(x)
        near_q = join(scal, [pay_q] + others(pay_q, 3, n), [x, pay_a])
        got_a = others(pay_a, 3, n)
        bias = score_bias(scal, table, [near_q])
        sources_q = hand_on(scal, [near_q] + others(near_q, 1, n), [bias] + got_a)
        near_a = join(scal, [pay_a] + got_a, [sources_q[0]])
        sources_q = list(sources_q) + [exchange(v, 1, n) for v in sources_q]
        got_a = others(near_a, 1, n)
        start = [near_a]
    else:
        def gather(v):
            return lax.all_gather(v, AXES, axis=0, tiled=True)

        def blocked(v, rows):
            return gather(v).reshape(blocks, rows, -1)

        shares = jnp.stack([gather(v).reshape(blocks, BLK) for v in vectors], axis=1)
        rows = jnp.stack(
            [shares.reshape(blocks, 128), jnp.pad(blocked(widen_b, 64)[:, :, 0], ((0, 0), (0, 64)))], axis=1
        )
        every = jnp.pad(rows, ((0, 0), (0, BLK - 2), (0, 0)))
        sources_q = as_sources(jnp.concatenate([blocked(wqkv, BLK), every], axis=2))
        wide = blocked(widen, BLK).reshape(blocks, BLK, 4, width).transpose(0, 2, 1, 3)
        sources_a = as_sources(
            jnp.concatenate(
                [blocked(wout, BLK), blocked(narrow, 4 * BLK), wide.reshape(blocks, 4 * BLK, width)], axis=1
            )
        )
        start = []
        x = by_window(x)
        bias = score_bias(scal, table, [])

    first, qkv, p, ctx, prm, bw = attention_forward(scal, x, labels, bias, sources_q, start)
    if fast:
        sources_a = list(hand_on(scal, [near_a] + got_a, [ctx]))
        sources_a += [exchange(v, 1, n) for v in sources_a]
    up = by_window(up)
    out, gr, gc, eb, sb, keep_h, send_h = hidden_both(scal, tokens, x, up, ctx, prm, bw, sources_a)
    between, last = [], []
    if fast:
        dealt_h = deal(scal, [keep_h, exchange(send_h, 1, n)], 1, [])
        got_h = others_of(dealt_h, 1, n)
        between = [dealt_h[0]]
    gj, keep_j, send_j = attention_back(scal, qkv, p, gc, first, eb, sb, between)
    if fast:
        dealt_h = deal(scal, [dealt_h[0]] + got_h, 3, [keep_j])
        got_h = others_of(dealt_h, 3, n)
        (send_j,) = hand_on(scal, [send_j], [dealt_h[0]])
        dealt_j = deal(scal, [keep_j, exchange(send_j, 1, n)], 1, [])
        got_j = others_of(dealt_j, 1, n)
        last = [dealt_h[0], dealt_j[0]]
    grad_in = input_grad(scal, tokens, x, up, gj, gr, prm, sources_q, last)
    if fast:
        dealt_j = deal(scal, [dealt_j[0]] + got_j, 3, [grad_in] + got_h)
        got_j = others_of(dealt_j, 3, n)
        expander, outmatrix, reducer = finish_hidden(scal, [dealt_h[0]] + got_h, [dealt_j[0]])
        done = finish_joint(scal, [dealt_j[0]] + got_j, wqkv, widen, expander, pay_q, entries)
        projector, grad_table = done[:2]
        pregain, offset, qb, vb, ob, midgain, midshift, xb, rb = [v.reshape(-1) for v in done[2:]]
    else:
        def scatter(v):
            return lax.psum_scatter(v, AXES, scatter_dimension=0, tiled=True).astype(F32)

        def natural(keep, send):
            pairs = blocks // 2
            return jnp.stack([keep[:pairs], send[:pairs]], axis=1).reshape((blocks,) + keep.shape[1:])

        all_h = natural(keep_h, send_h)
        outmatrix = scatter(all_h[:, :BLK].reshape(width, width))
        reducer = scatter(all_h[:, BLK : 5 * BLK].reshape(4 * width, width))
        expander = all_h[:, 5 * BLK :].reshape(blocks, 4, BLK, width).transpose(0, 2, 1, 3)
        expander = scatter(expander.reshape(width, 4 * width))
        projector = scatter(natural(keep_j, send_j).reshape(width, 3 * width))
        sums = lax.psum(keep_j[-1].astype(F32), AXES)
        grad_table, eb, rb, ob, gb = read_small(sums)
        grad_table = grad_table[:, :entries]

        def gains(w, grad, bias, shift, gain):
            w = w.astype(F32)
            g = jnp.sum(w * (grad - shift.astype(F32)[:, None] * bias), axis=1)
            return g / gain.astype(F32), jnp.sum(w * bias, axis=1)

        pregain, offset = gains(wqkv, projector, gb, shift1, gain1)
        midgain, midshift = gains(widen, expander, eb, shift2, gain2)

        def mine(v, size):
            return lax.dynamic_slice_in_dim(v[0], me * size, size, 0)

        qb, vb = mine(gb[:, :width], own), mine(gb[:, 2 * width :], own)
        ob, rb, xb = mine(ob, own), mine(rb, own), mine(eb, 4 * own)
    return (
        out, grad_in, pregain, offset, projector, qb, vb, outmatrix, ob, midgain, midshift,
        expander, xb, reducer, rb, grad_table,
    )


def others_of(dealt, shift, n):
    return [exchange(dealt[m], m << shift, n) for m in (1, 2, 3)]


def solution(mesh):
    both = ("wide", "narrow")
    v1, v2, v3 = P(both), P(both, None), P(both, None, None)
    in_specs = (v3, v1, v2, v1, v1, v2, v1, v1, v2, v1, v1, v1, v2, v1, v2, v1, P(), v3)
    out_specs = (v3, v3, v1, v1, v2, v1, v1, v2, v1, v1, v1, v2, v1, v2, v1, P())
    return jax.shard_map(
        per_device, mesh=mesh, in_specs=in_specs, out_specs=out_specs, check_vma=False
    )
```

```python
import functools

import jax
import jax.numpy as jnp
from jax import lax
from jax.experimental import pallas as pl
from jax.experimental.pallas import tpu as pltpu
from jax.sharding import PartitionSpec as P

F32 = jnp.float32
BF = jnp.bfloat16
WS = 10
TP = 104
SEG = 128
BLK = 16
EPS = 1e-5
NW = 4
VMEM = 60 << 20

NT = (((1,), (1,)), ((), ()))
TN = (((0,), (0,)), ((), ()))
NN = (((1,), (0,)), ((), ()))


def dot(a, b, dims=NN):
    return lax.dot_general(a, b, dims, preferred_element_type=F32)


def normalize(v):
    c = v - jnp.mean(v, axis=-1, keepdims=True)
    inv = lax.rsqrt(jnp.mean(c * c, axis=-1, keepdims=True) + EPS)
    return c * inv, inv


def norm_back(g, xhat, inv, gain):
    s = g * gain
    return inv * (
        s
        - jnp.mean(s, axis=-1, keepdims=True)
        - xhat * jnp.mean(s * xhat, axis=-1, keepdims=True)
    )


def head_masks():
    lane = lax.broadcasted_iota(jnp.int32, (1, 128), 1)
    return [(lane // 32) == h for h in range(4)]


def head_ones():
    return [jnp.where(m, 1.0, 0.0).astype(BF) for m in head_masks()]


def stack_heads(v, ones):
    return jnp.concatenate([v * m for m in ones], axis=0)


def load_rows(src_ref):
    return src_ref[...].astype(F32).reshape(NW * TP, src_ref.shape[2])


def fetch_blocks(me, sources, parts, sem):
    copies = []
    for s, src in enumerate(sources):
        for z in range(src.shape[0]):
            m = 8 * z + 2 * (s % 4) + s // 4
            d = m ^ me
            for k, (row, rows, dst, lanes) in enumerate(parts):
                to = pl.ds(pl.multiple_of(d * rows, rows), rows)
                copies.append(
                    pltpu.make_async_copy(
                        src.at[z, pl.ds(row, rows), :], dst.at[to, lanes], sem.at[k, m]
                    )
                )
    for c in copies:
        c.start()
    for c in copies:
        c.wait()


def split_blocks(bit, keep_ref, send_ref, row, rows, acc, cols=None):
    lanes = slice(None) if cols is None else cols
    for k in range(acc.shape[0] // (2 * rows)):
        mine = pl.multiple_of(k * 2 * rows + bit * rows, rows)
        other = pl.multiple_of(k * 2 * rows + (1 - bit) * rows, rows)
        keep_ref[k, row : row + rows, :] = acc[pl.ds(mine, rows), lanes].astype(BF)
        send_ref[k, row : row + rows, :] = acc[pl.ds(other, rows), lanes].astype(BF)


def block_at(i, scal):
    return jnp.minimum(i, (scal[0] + NW - 1) // NW - 1)


def whole(shape):
    return pl.BlockSpec(shape, lambda *a: (0,) * len(shape))


def rows_spec(cols, col=0):
    return pl.BlockSpec((NW * TP, cols), lambda i, scal, *r: (block_at(i, scal), col))


def win_spec(shape, live_only=True):
    if live_only:
        return pl.BlockSpec(
            (NW,) + shape, lambda i, scal, *r: (block_at(i, scal),) + (0,) * len(shape)
        )
    return pl.BlockSpec((NW,) + shape, lambda i, *r: (i,) + (0,) * len(shape))


def vmem_spec():
    return pl.BlockSpec(memory_space=pltpu.VMEM)


def any_spec():
    return pl.BlockSpec(memory_space=pl.ANY)


def call(
    body, name, grid, prefetch, args, in_specs, out_shape, out_specs, scratch, cost, gate=(), vmem=VMEM
):
    first = len(prefetch) + len(args)

    def without_gate(*refs):
        body(*refs[:first], *refs[first + len(gate) :])

    return pl.pallas_call(
        without_gate,
        grid_spec=pltpu.PrefetchScalarGridSpec(
            num_scalar_prefetch=len(prefetch),
            grid=grid,
            in_specs=list(in_specs) + [any_spec()] * len(gate),
            out_specs=out_specs,
            scratch_shapes=scratch,
        ),
        out_shape=out_shape,
        compiler_params=pltpu.CompilerParams(vmem_limit_bytes=vmem),
        cost_estimate=pl.CostEstimate(
            flops=int(cost * 8e8), bytes_accessed=int(cost * 1e6), transcendentals=0
        ),
        name=name,
    )(*prefetch, *args, *gate)


def small_call(body, name, scal, args, outs, gate=(), far=(), scratch=(), far_out=False):
    first = 1 + len(args) + len(far)

    def without_gate(*refs):
        body(*refs[:first], *refs[first + len(gate) :])

    here = pl.BlockSpec(memory_space=pltpu.VMEM)
    return pl.pallas_call(
        without_gate,
        grid_spec=pltpu.PrefetchScalarGridSpec(
            num_scalar_prefetch=1,
            grid=(),
            in_specs=[here] * len(args) + [whole(a.shape) for a in far] + [any_spec()] * len(gate),
            out_specs=[whole(s) if far_out else here for s, _ in outs],
            scratch_shapes=list(scratch),
        ),
        out_shape=[sds(s, t) if far_out else pltpu.VMEM(s, t) for s, t in outs],
        compiler_params=pltpu.CompilerParams(vmem_limit_bytes=VMEM if far else 12 << 20),
        cost_estimate=pl.CostEstimate(flops=1000, bytes_accessed=1000, transcendentals=0),
        name=name,
    )(scal, *[pltpu.with_memory_space_constraint(a, pltpu.VMEM) for a in args], *far, *gate)


def sds(shape, dtype):
    return jax.ShapeDtypeStruct(shape, dtype)


def attention_body(
    scal, x_ref, reg_ref, bias_ref, *refs
):
    sources, refs = refs[:8], refs[8:]
    first_ref, qkv_ref, p_ref, ctx_ref, prm_ref, bw_ref, js, cs, wq, sem = refs
    i = pl.program_id(0)
    width = x_ref.shape[2]
    rows = NW * TP
    live = scal[0]

    @pl.when(i == 0)
    def _():
        js[rows : rows + SEG - TP, :] = jnp.zeros((SEG - TP, 3 * width), F32)
        fetch_blocks(scal[1], sources, [(0, BLK, wq, slice(None))], sem)
        small = wq[:, 3 * width :].astype(F32)
        shares = jnp.concatenate([small[r : r + 1] for r in range(0, width, BLK)], axis=0)
        count = width // BLK
        place = lax.broadcasted_iota(jnp.int32, (count, width), 1)
        mine = place // BLK == lax.broadcasted_iota(jnp.int32, (count, width), 0)
        source = lax.broadcasted_iota(jnp.int32, (128, width), 0)
        target = lax.broadcasted_iota(jnp.int32, (128, width), 1) % BLK
        for v in range(8):
            pick = jnp.where(source == target + BLK * v, 1.0, 0.0).astype(BF)
            spread = dot(shares.astype(BF), pick)
            prm_ref[v : v + 1, :] = jnp.sum(jnp.where(mine, spread, 0.0), axis=0, keepdims=True)
        left = lax.broadcasted_iota(jnp.int32, (1, 128), 1) < 64
        for k in range(width // (2 * BLK)):
            r = 2 * BLK * k
            right = pltpu.roll(small[r + BLK : r + BLK + 8], 64, 1)[1:2]
            bw_ref[0:1, 128 * k : 128 * k + 128] = jnp.where(left, small[r + 1 : r + 2], right)

    @pl.when(i * NW < live)
    def _():
        xhat, _ = normalize(load_rows(x_ref))
        first = (xhat * prm_ref[0:1, :] + prm_ref[1:2, :]).astype(BF)
        first_ref[...] = first
        scale = 32.0**-0.5
        for part in range(3):
            j = dot(first, wq[:, part * width : (part + 1) * width])
            if part == 0:
                j = (j + prm_ref[2:3, :]) * scale
            if part == 2:
                j = j + prm_ref[3:4, :]
            js[0:rows, part * width : (part + 1) * width] = j
        ones = head_ones()
        eye = lax.broadcasted_iota(jnp.int32, (TP, SEG), 0) == lax.broadcasted_iota(
            jnp.int32, (TP, SEG), 1
        )
        masks = []
        for w in range(NW):
            qkv_ref[w] = js[w * TP : w * TP + SEG, :].astype(BF)
            row = reg_ref[pl.ds(i * NW + w, 1), :].astype(F32)
            row = jnp.concatenate([row, jnp.full((1, SEG - row.shape[1]), -1.0, F32)], axis=1)
            row = jnp.broadcast_to(row, (TP, SEG))
            col = jnp.max(jnp.where(eye, row, -1.0), axis=1, keepdims=True)
            masks.append(jnp.where(row == col, 0.0, -1e30))

        def scores(n):
            w, g = n
            c = 128 * g
            keys = stack_heads(qkv_ref[w, :, width + c : width + c + 128], ones)
            return dot(qkv_ref[w, 0:TP, c : c + 128], keys, NT)

        def softmax(n, s):
            w, g = n
            out = []
            for h in range(4):
                lanes = slice(SEG * h, SEG * (h + 1))
                sh = s[:, lanes] + bias_ref[g, :, lanes] + masks[w]
                e = jnp.exp(sh - jnp.max(sh, axis=1, keepdims=True))
                out.append((e * (1.0 / jnp.sum(e, axis=1, keepdims=True))).astype(BF))
            p_ref[w, g] = jnp.concatenate(out, axis=1)

        def values(n):
            w, g = n
            c = 128 * g
            stacked = stack_heads(qkv_ref[w, :, 2 * width + c : 2 * width + c + 128], ones)
            cs[w * TP : (w + 1) * TP, c : c + 128] = dot(p_ref[w, g], stacked)

        pairs = [(w, g) for w in range(NW) for g in range(width // 128)]
        lag = 3
        ss = {}
        for k in range(len(pairs) + lag + 1):
            if k < len(pairs):
                ss[k] = scores(pairs[k])
            if 0 <= k - 1 - lag < len(pairs):
                values(pairs[k - 1 - lag])
            if 0 <= k - lag < len(pairs):
                softmax(pairs[k - lag], ss.pop(k - lag))
        ctx_ref[...] = cs[...].astype(BF)


def attention_forward(scal, x, regions, bias, sources, gate):
    windows, _, width = x.shape
    rows = NW * TP
    groups = width // 128
    return call(
        attention_body, "attn_fwd", (windows // NW,), (scal,), [x, regions, bias] + sources,
        [win_spec((TP, width)), whole(regions.shape), whole(bias.shape)] + [any_spec()] * 8,
        [sds((windows * TP, width), BF), sds((windows, SEG, 3 * width), BF),
         sds((windows, groups, TP, 512), BF), sds((windows * TP, width), BF),
         sds((8, width), F32), sds((1, 4 * width), F32)],
        [rows_spec(width), win_spec((SEG, 3 * width)), win_spec((groups, TP, 512)), rows_spec(width),
         whole((8, width)), whole((1, 4 * width))],
        [pltpu.VMEM((rows + SEG - TP, 3 * width), F32),
         pltpu.VMEM((rows, width), F32), pltpu.VMEM((width, sources[0].shape[2]), BF),
         pltpu.SemaphoreType.DMA((1, width // BLK))],
        24, gate,
    )


def normal_parts(z):
    return 0.5 + 0.5 * lax.erf(z * 0.7071067811865476), jnp.exp(z * z * -0.5)


def hidden_body(
    tokens, scal, x_ref, u_ref, ctx_ref, prm_ref, bw_ref, *refs
):
    sources, refs = refs[:8], refs[8:]
    out_ref, gr_ref, gc_ref, eb_ref, sb_ref, keep_ref, send_ref = refs[:7]
    acts, gps, er, rr, om, wo, wn, ww, sem = refs[7:]
    i = pl.program_id(0)
    width = x_ref.shape[2]
    hidden = ww.shape[1]
    live = scal[0]
    step = 256

    @pl.when(i == 0)
    def _():
        parts = [(0, BLK, wo, slice(None)), (BLK, 4 * BLK, wn, slice(None))]
        for c in range(4):
            parts.append(((5 + c) * BLK, BLK, ww, slice(c * width, (c + 1) * width)))
        fetch_blocks(scal[1], sources, parts, sem)
        er[...] = jnp.zeros_like(er)
        rr[...] = jnp.zeros_like(rr)
        om[...] = jnp.zeros_like(om)
        eb_ref[...] = jnp.zeros_like(eb_ref)
        sb_ref[...] = jnp.zeros_like(sb_ref)

    @pl.when(i * NW >= live)
    def _():
        out_ref[...] = x_ref[:, 0:tokens, :]

    @pl.when(i * NW < live)
    def _():
        xs = load_rows(x_ref)
        row = lax.broadcasted_iota(jnp.int32, (NW * TP, 1), 0)
        us = jnp.where(row < (live - i * NW) * TP, load_rows(u_ref), 0.0)
        ctx = ctx_ref[...]
        up = us.astype(BF)
        res = xs + dot(ctx, wo[...]) + prm_ref[4:5, :]
        xhat, inv = normalize(res)
        second = (xhat * prm_ref[5:6, :] + prm_ref[6:7, :]).astype(BF)

        def products(c):
            cols = slice(c * step, (c + 1) * step)
            return dot(up, wn[cols, :], NT), dot(second, ww[:, cols])

        def activate(c, ga, z):
            cols = slice(c * step, (c + 1) * step)
            z = z + bw_ref[:, cols]
            phi, bell = normal_parts(z)
            acts[:, cols] = (z * phi).astype(BF)
            gp = (ga * (phi + z * bell * 0.3989422804014327)).astype(BF)
            gps[:, cols] = gp
            eb_ref[:, cols] += jnp.sum(gp.astype(F32), axis=0, keepdims=True)

        count = hidden // step
        t = products(0)
        for c in range(count):
            later = products(c + 1) if c + 1 < count else None
            activate(c, *t)
            t = later
        for c in range(count):
            cols = slice(c * step, (c + 1) * step)
            er[:, cols] += dot(second, gps[:, cols], TN)
            rr[cols, :] += dot(acts[:, cols], up, TN)
        gs = dot(gps[...], ww[...], NT)
        o = res + dot(acts[...], wn[...]) + prm_ref[7:8, :]
        for w in range(NW):
            out_ref[w] = jnp.where(
                i * NW + w < live, o[w * TP : w * TP + tokens], xs[w * TP : w * TP + tokens]
            ).astype(BF)
        gres = us + norm_back(gs, xhat, inv, prm_ref[5:6, :])
        ga = gres.astype(BF)
        gr_ref[...] = ga
        om[...] += dot(ctx, ga, TN)
        sb_ref[0:1, :] += jnp.sum(us, axis=0, keepdims=True)
        sb_ref[1:2, :] += jnp.sum(ga.astype(F32), axis=0, keepdims=True)
        gc = dot(ga, wo[...], NT)
        for w in range(NW):
            gc_ref[w] = gc[w * TP : (w + 1) * TP].astype(BF)

    @pl.when(i == pl.num_programs(0) - 1)
    def _():
        bit = scal[1] & 1
        split_blocks(bit, keep_ref, send_ref, 0, BLK, om)
        split_blocks(bit, keep_ref, send_ref, BLK, 4 * BLK, rr)
        for c in range(4):
            split_blocks(
                bit, keep_ref, send_ref, (5 + c) * BLK, BLK, er, slice(c * width, (c + 1) * width)
            )


def hidden_both(scal, tokens, x, u, ctx, prm, bw, sources):
    windows, _, width = x.shape
    hidden = 4 * width
    rows = NW * TP
    pairs = width // BLK // 2
    share = (pairs, 9 * BLK, width)
    return call(
        functools.partial(hidden_body, tokens), "hidden", (windows // NW,), (scal,),
        [x, u, ctx, prm, bw] + sources,
        [win_spec((TP, width), False), win_spec((TP, width)), rows_spec(width),
         whole(prm.shape), whole(bw.shape)] + [any_spec()] * 8,
        [sds((windows, tokens, width), BF), sds((windows * TP, width), BF), sds((windows, TP, width), BF),
         sds((1, hidden), F32), sds((2, width), F32), pltpu.VMEM(share, BF), pltpu.VMEM(share, BF)],
        [win_spec((tokens, width), False), rows_spec(width), win_spec((TP, width)),
         whole((1, hidden)), whole((2, width)), vmem_spec(), vmem_spec()],
        [pltpu.VMEM((rows, hidden), BF), pltpu.VMEM((rows, hidden), BF),
         pltpu.VMEM((width, hidden), F32), pltpu.VMEM((hidden, width), F32), pltpu.VMEM((width, width), F32),
         pltpu.VMEM((width, width), BF), pltpu.VMEM((hidden, width), BF), pltpu.VMEM((width, hidden), BF),
         pltpu.SemaphoreType.DMA((6, 2 * pairs))],
        52, (), 52 << 20,
    )


def three_terms(v):
    hi = v.astype(BF)
    rest = v - hi.astype(F32)
    mid = rest.astype(BF)
    return hi, mid, (rest - mid.astype(F32)).astype(BF)


def table_row(scores):
    side = 2 * WS - 1
    reach = side * (WS - 1) + WS - 1
    j = lax.broadcasted_iota(jnp.int32, (SEG, 256), 0)
    k = lax.broadcasted_iota(jnp.int32, (SEG, 256), 1)
    pick = jnp.where(k == reach - (side * (j // WS) + j % WS), 1.0, 0.0).astype(BF)
    u = sum(dot(t, pick) for t in three_terms(scores))
    u = jnp.concatenate([u, jnp.zeros((TP, 128), F32)], axis=1)
    u = pltpu.roll(u, 0, 1, stride=1, stride_axis=0)
    r = lax.broadcasted_iota(jnp.int32, (16, TP), 0)
    i = lax.broadcasted_iota(jnp.int32, (16, TP), 1)
    group = jnp.where(r == i // WS, 1.0, 0.0).astype(BF)
    v = sum(dot(group, t) for t in three_terms(u))
    skip = side - WS
    low = pltpu.roll(v[0:8], 0, 1, stride=skip, stride_axis=0)
    high = pltpu.roll(v[8:16], 0, 1, stride=skip, stride_axis=0)
    return jnp.sum(low + pltpu.roll(high, 8 * skip, 1), axis=0, keepdims=True)


def attention_back_body(
    scal, qkv_ref, p_ref, gc_ref, first_ref, eb_ref, sb_ref,
    gj_ref, keep_ref, send_ref,
    gjs, pj, gb, ra, small,
):
    i = pl.program_id(0)
    width = gc_ref.shape[2]
    live = scal[0]

    @pl.when(i == 0)
    def _():
        pj[...] = jnp.zeros_like(pj)
        gb[...] = jnp.zeros_like(gb)
        ra[...] = jnp.zeros_like(ra)
        small[...] = jnp.zeros_like(small)

    @pl.when(i * NW < live)
    def _():
        masks = head_masks()
        ones = head_ones()
        scale = 32.0**-0.5

        def lanes_of(g, part=0):
            c = part * width + 128 * g
            return slice(c, c + 128)

        def to_probs(n):
            w, g = n
            stacked = stack_heads(qkv_ref[w, :, lanes_of(g, 2)], ones)
            return dot(gc_ref[w, :, lanes_of(g)], stacked, NT)

        def softmax_back(n, dp):
            w, g = n
            out = []
            for h in range(4):
                lanes = slice(SEG * h, SEG * (h + 1))
                ph = p_ref[w, g, :, lanes].astype(F32)
                t = dp[:, lanes] * ph
                out.append(t - ph * jnp.sum(t, axis=1, keepdims=True))
            return jnp.concatenate(out, axis=1).astype(BF)

        def combine(r):
            o = jnp.where(masks[0], r[0:TP], 0.0)
            for h in range(1, 4):
                o = jnp.where(masks[h], r[SEG * h : SEG * h + TP], o)
            return o

        def to_joint(n, ds):
            w, g = n
            rows = slice(w * TP, (w + 1) * TP)
            keys = stack_heads(qkv_ref[w, :, lanes_of(g, 1)], ones)
            gjs[rows, lanes_of(g)] = dot(ds, keys) * scale
            gjs[rows, lanes_of(g, 1)] = combine(dot(ds, qkv_ref[w, 0:TP, lanes_of(g)], TN))
            gjs[rows, lanes_of(g, 2)] = combine(dot(p_ref[w, g], gc_ref[w, :, lanes_of(g)], TN))

        pairs = [(w, g) for g in range(width // 128) for w in range(NW)]
        size = 2
        parts = [pairs[k : k + size] for k in range(0, len(pairs), size)]
        dps = [to_probs(n) for n in parts[0]]
        before = None
        for k, group in enumerate(parts):
            later = [to_probs(n) for n in parts[k + 1]] if k + 1 < len(parts) else None
            dss = [softmax_back(n, dp) for n, dp in zip(group, dps)]
            if before is not None:
                for n, ds in zip(*before):
                    to_joint(n, ds)
            total = dss[0].astype(F32)
            for ds in dss[1:]:
                total += ds.astype(F32)
            ra[group[0][1]] += total
            before = (group, dss)
            dps = later
        for n, ds in zip(*before):
            to_joint(n, ds)
        gj = gjs[...].astype(BF)
        gj_ref[...] = gj
        gb[...] += jnp.sum(gj.astype(F32), axis=0, keepdims=True)
        pj[...] += dot(first_ref[...], gj, TN)

    @pl.when(i == pl.num_programs(0) - 1)
    def _():
        split_blocks(scal[1] & 1, keep_ref, send_ref, 0, BLK, pj)
        for h in range(width // 32):
            lanes = slice(SEG * (h % 4), SEG * (h % 4 + 1))
            small[h : h + 1, 0:384] = table_row(ra[h // 4, :, lanes])
        small[0:1, 384:1408] = eb_ref[:, 0:1024]
        small[1:2, 384:1408] = eb_ref[:, 1024:2048]
        small[2:3, 384:896] = sb_ref[0:1, :]
        small[2:3, 896:1408] = sb_ref[1:2, :]
        small[3:4, 384:1408] = gb[:, 0:1024]
        small[4:5, 384:896] = gb[:, 1024:1536]
        sums = small[...].astype(BF)
        keep_ref[keep_ref.shape[0] - 1] = sums
        send_ref[send_ref.shape[0] - 1] = sums


def read_small(v):
    table = v[:, 0:384]
    eb = jnp.concatenate([v[0:1, 384:1408], v[1:2, 384:1408]], axis=1)
    gb = jnp.concatenate([v[3:4, 384:1408], v[4:5, 384:896]], axis=1)
    return table, eb, v[2:3, 384:896], v[2:3, 896:1408], gb


def attention_back(scal, qkv, p, gc, first, eb, sb, gate):
    windows = qkv.shape[0]
    width = gc.shape[2]
    rows = NW * TP
    groups = width // 128
    share = (width // BLK // 2 + 1, BLK, 3 * width)
    return call(
        attention_back_body, "attn_back", (windows // NW,), (scal,),
        (qkv, p, gc, first, eb, sb),
        [win_spec((SEG, 3 * width)), win_spec((groups, TP, 512)), win_spec((TP, width)),
         rows_spec(width), whole(eb.shape), whole(sb.shape)],
        [sds((windows * TP, 3 * width), BF), pltpu.VMEM(share, BF), pltpu.VMEM(share, BF)],
        [rows_spec(3 * width), vmem_spec(), vmem_spec()],
        [pltpu.VMEM((rows, 3 * width), F32), pltpu.VMEM((width, 3 * width), F32),
         pltpu.VMEM((1, 3 * width), F32), pltpu.VMEM((groups, TP, 512), F32),
         pltpu.VMEM((16, 3 * width), F32)],
        27, gate, 56 << 20,
    )


def input_grad_body(tokens, scal, x_ref, u_ref, gj_ref, gr_ref, prm_ref, *refs):
    sources = refs[:8]
    gi_ref, wq, sem = refs[8:]
    i = pl.program_id(0)
    width = x_ref.shape[2]
    live = scal[0]

    @pl.when(i == 0)
    def _():
        fetch_blocks(scal[1], sources, [(0, BLK, wq, slice(None))], sem)

    @pl.when(i * NW >= live)
    def _():
        gi_ref[...] = u_ref[:, 0:tokens, :]

    @pl.when(i * NW < live)
    def _():
        us = load_rows(u_ref)
        xhat, inv = normalize(load_rows(x_ref))
        gf = dot(gj_ref[...], wq[:, 0 : 3 * width], NT)
        o = gr_ref[...].astype(F32) + norm_back(gf, xhat, inv, prm_ref[0:1, :])
        for w in range(NW):
            rows = slice(w * TP, w * TP + tokens)
            gi_ref[w] = jnp.where(i * NW + w < live, o[rows], us[rows]).astype(BF)


def input_grad(scal, tokens, x, u, gj, gr, prm, sources, gate):
    windows, _, width = x.shape
    return call(
        functools.partial(input_grad_body, tokens), "input_grad", (windows // NW,), (scal,),
        [x, u, gj, gr, prm] + sources,
        [win_spec((TP, width)),
         pl.BlockSpec(
             (NW, TP, width),
             lambda i, s: (jnp.maximum(i, jnp.minimum(s[0] // NW, windows // NW - 1)), 0, 0),
         ),
         rows_spec(3 * width), rows_spec(width), whole(prm.shape)] + [any_spec()] * 8,
        [sds((windows, tokens, width), BF)],
        [win_spec((tokens, width), False)],
        [pltpu.VMEM((width, sources[0].shape[2]), BF), pltpu.SemaphoreType.DMA((1, width // BLK))],
        12, gate,
    )[0]


AXES = ("wide", "narrow")


def exchange(v, mask, n):
    return lax.ppermute(v, AXES, [(i, i ^ mask) for i in range(n)])


def join_body(scal, *refs):
    out = refs[-1]
    size = refs[0].shape[0]
    for k, r in enumerate(refs[:-1]):
        out[k * size : (k + 1) * size] = r[...]


def join(scal, arrays, gate):
    shape = (arrays[0].shape[0] * len(arrays),) + arrays[0].shape[1:]
    return small_call(join_body, "join", scal, arrays, [(shape, BF)], gate)[0]


def hand_on(scal, arrays, gate):
    count = len(arrays)
    return pl.pallas_call(
        lambda *refs: None,
        grid_spec=pltpu.PrefetchScalarGridSpec(
            num_scalar_prefetch=1,
            grid=(),
            in_specs=[any_spec()] * (count + len(gate)),
            out_specs=[any_spec()] * count,
        ),
        out_shape=[sds(a.shape, a.dtype) for a in arrays],
        input_output_aliases={1 + k: k for k in range(count)},
        name="hand_on",
    )(scal, *arrays, *gate)


def pack_joint_body(scal, wqkv_ref, *refs):
    vectors, out = refs[:-1], refs[-1]
    width = wqkv_ref.shape[1]
    out[0, :, 0:width] = wqkv_ref[...]

    def row(ref, at):
        v = ref[...].astype(F32).reshape(1, ref.shape[0])
        rest = 128 - ref.shape[0] - at
        parts = [jnp.zeros((1, at), F32)] * (at > 0) + [v] + [jnp.zeros((1, rest), F32)] * (rest > 0)
        return jnp.concatenate(parts, axis=1)

    first = sum(row(r, BLK * k) for k, r in enumerate(vectors[:8]))
    small = jnp.concatenate([first, row(vectors[8], 0), jnp.zeros((BLK - 2, 128), F32)], axis=0)
    out[0, :, width:] = small.astype(BF)


def pack_joint(scal, wqkv, vectors):
    rows, width = wqkv.shape
    outs = [((1, rows, width + 128), BF)]
    return small_call(pack_joint_body, "pack_joint", scal, [], outs, far=[wqkv] + vectors)[0]


def pack_hidden_body(scal, wout_ref, narrow_ref, widen_ref, out):
    width = wout_ref.shape[1]
    out[0, 0:BLK] = wout_ref[...]
    out[0, BLK : 5 * BLK] = narrow_ref[...]
    for c in range(4):
        out[0, (5 + c) * BLK : (6 + c) * BLK] = widen_ref[:, c * width : (c + 1) * width]


def pack_hidden(scal, wout, narrow, widen, gate):
    shape = (1, 9 * BLK, wout.shape[1])
    args = [wout, narrow, widen]
    return small_call(pack_hidden_body, "pack_hidden", scal, [], [(shape, BF)], gate, far=args)[0]


def others(v, shift, n):
    return [exchange(v, m << shift, n) for m in (1, 2, 3)]


def total_at(ins, at):
    total = ins[0][at].astype(F32)
    for r in ins[1:]:
        total += r[at].astype(F32)
    return total


def deal_body(count, shift, extra, scal, *refs):
    ins, outs = refs[:count], refs[-4:]
    me = (scal[1] >> shift) & 3
    quads = ins[0].shape[0] // 4
    for q in range(quads):
        for m in range(4):
            outs[m][q] = total_at(ins, 4 * q + (m ^ me)).astype(BF)
    if extra:
        rest = total_at(ins, 4 * quads).astype(BF)
        for m in range(4):
            outs[m][quads] = rest


def deal(scal, arrays, shift, gate):
    blocks, rows, cols = arrays[0].shape
    quads, extra = blocks // 4, blocks % 4
    body = functools.partial(deal_body, len(arrays), shift, extra)
    return small_call(body, "deal", scal, arrays, [((quads + extra, rows, cols), BF)] * 4, gate)


def finish_hidden_body(scal, a, b, c, d, expander_ref, outmatrix_ref, reducer_ref):
    v = total_at([a, b, c, d], 0)
    width = v.shape[1]
    outmatrix_ref[...] = v[0:BLK]
    reducer_ref[...] = v[BLK : 5 * BLK]
    for k in range(4):
        expander_ref[:, k * width : (k + 1) * width] = v[(5 + k) * BLK : (6 + k) * BLK]


def finish_hidden(scal, arrays, gate):
    width = arrays[0].shape[2]
    shapes = [(BLK, 4 * width), (BLK, width), (4 * BLK, width)]
    return small_call(
        finish_hidden_body, "finish_hidden", scal, arrays, [(s, F32) for s in shapes], gate, far_out=True
    )


def finish_joint_body(
    scal, a, b, c, d, wqkv_ref, widen_ref, expander_ref, small_ref,
    projector_ref, table_ref, pregain_ref, shift_ref, qb_ref, vb_ref, ob_ref, midgain_ref,
    midshift_ref, xb_ref, rb_ref,
):
    me = scal[1]
    ins = [a, b, c, d]
    projector = total_at(ins, 0)
    width = projector.shape[1] // 3
    projector_ref[...] = projector
    table, eb, reducebias, outbias, gb = read_small(total_at(ins, 1))
    table_ref[...] = table[:, 0 : table_ref.shape[1]]

    shares = small_ref[0][:, small_ref.shape[2] - 128 :].astype(F32)
    eye = lax.broadcasted_iota(jnp.int32, (BLK, 128), 0)
    lanes = lax.broadcasted_iota(jnp.int32, (BLK, 128), 1)

    def column(k):
        return jnp.sum(jnp.where(lanes == eye + BLK * k, shares[0:1], 0.0), axis=1, keepdims=True)

    def gains(w_ref, grad, bias, shift, gain):
        w = w_ref[...].astype(F32)
        g = jnp.sum(w * (grad - shift * bias), axis=1, keepdims=True) / gain
        return g, jnp.sum(w * bias, axis=1, keepdims=True)

    pregain, offset = gains(wqkv_ref, projector, gb, column(1), column(0))
    midgain, midshift = gains(widen_ref, expander_ref[...], eb, column(6), column(5))
    lane = lax.broadcasted_iota(jnp.int32, (BLK, 128), 1)
    mat = jnp.where(lane == 0, pregain, 0.0)
    for k, v in ((1, offset), (2, midgain), (3, midshift)):
        mat = jnp.where(lane == k, v, mat)
    mat = jnp.transpose(mat)
    for k, r in enumerate((pregain_ref, shift_ref, midgain_ref, midshift_ref)):
        r[...] = mat[k : k + 1, 0:BLK]

    def mine(v, size):
        lanes = v.shape[1]
        v = pltpu.roll(jnp.broadcast_to(v, (8, lanes)), lanes - me * size, 1)
        return v[0:1, 0:size]

    qb_ref[...] = mine(gb[:, 0:width], BLK)
    vb_ref[...] = mine(gb[:, 2 * width : 3 * width], BLK)
    ob_ref[...] = mine(outbias, BLK)
    rb_ref[...] = mine(reducebias, BLK)
    xb_ref[...] = mine(eb, 4 * BLK)


def finish_joint(scal, arrays, wqkv, widen, expander, small, entries):
    row = (1, BLK)
    shapes = [wqkv.shape, (BLK, entries)] + [row] * 7 + [(1, 4 * BLK), row]
    return small_call(
        finish_joint_body, "finish_joint", scal, arrays, [(s, F32) for s in shapes],
        far=[wqkv, widen, expander, small], far_out=True,
    )


def score_bias_body(scal, table_ref, bias_ref):
    side = 2 * WS - 1
    reach = side * (WS - 1) + WS - 1
    heads, entries = table_ref.shape
    i = lax.broadcasted_iota(jnp.int32, (TP, 384), 0)
    e = lax.broadcasted_iota(jnp.int32, (TP, 384), 1)
    pick = jnp.where(e == reach + side * (i // WS) + i % WS, 1.0, 0.0).astype(BF)
    j = lax.broadcasted_iota(jnp.int32, (SEG, 16), 0)
    r = lax.broadcasted_iota(jnp.int32, (SEG, 16), 1)
    group = jnp.where(r == j // WS, 1.0, 0.0).astype(BF)
    table = jnp.concatenate(
        [table_ref[...].astype(F32), jnp.zeros((heads, 384 - entries), F32)], axis=1
    )
    skip = side - WS
    vs, us = [], []
    for h in range(heads):
        t = jnp.broadcast_to(table[h : h + 1], (8, 384))
        low = pltpu.roll(t, 0, 1, stride=skip, stride_axis=0)
        vs.append(jnp.concatenate([low, pltpu.roll(low, 8 * skip, 1)], axis=0).astype(BF))
    for h in range(heads):
        us.append(pltpu.roll(dot(group, vs[h]), 0, 1, stride=1, stride_axis=0).astype(BF))
    for h in range(heads):
        bias_ref[h // 4, :, SEG * (h % 4) : SEG * (h % 4 + 1)] = dot(pick, us[h], NT)


def score_bias(scal, table, gate):
    heads = table.shape[0]
    shape = (heads // 4, TP, 4 * SEG)
    return small_call(
        score_bias_body, "score_bias", scal, [], [(shape, F32)], gate, far=[table], far_out=True
    )[0]


def by_window(v):
    return jnp.pad(v, ((0, 0), (0, TP - v.shape[1]), (0, 0)))


def as_sources(v):
    return [v[2 * q + c :: 8] for c in (0, 1) for q in range(4)]


def per_device(
    x, tally, labels, gain1, shift1, wqkv, qbias, vbias, wout, obias,
    gain2, shift2, widen, widen_b, narrow, narrow_b, table, up,
):
    tokens, width = x.shape[1:]
    heads, entries = table.shape
    n = lax.axis_size("wide") * lax.axis_size("narrow")
    me = lax.axis_index("wide") * lax.axis_size("narrow") + lax.axis_index("narrow")
    me = me.astype(jnp.int32)
    own = width // n
    fast = own == BLK and n == 32
    scal = jnp.stack([tally[0], me if fast else jnp.int32(0)])
    blocks = width // BLK

    vectors = [gain1, shift1, qbias, vbias, obias, gain2, shift2, narrow_b]
    if fast:
        pay_q = pack_joint(scal, wqkv, vectors + [widen_b])
        pay_a = pack_hidden(scal, wout, narrow, widen, [pay_q])
        x = by_window(x)
        near_q = join(scal, [pay_q] + others(pay_q, 3, n), [x])
        got_a = others(pay_a, 3, n)
        bias = score_bias(scal, table, [near_q])
        sources_q = hand_on(scal, [near_q] + others(near_q, 1, n), [bias])
        near_a = join(scal, [pay_a] + got_a, [sources_q[0]])
        sources_q = list(sources_q) + [exchange(v, 1, n) for v in sources_q]
        got_a = others(near_a, 1, n)
        start = [near_a]
    else:
        def gather(v):
            return lax.all_gather(v, AXES, axis=0, tiled=True)

        def blocked(v, rows):
            return gather(v).reshape(blocks, rows, -1)

        shares = jnp.stack([gather(v).reshape(blocks, BLK) for v in vectors], axis=1)
        rows = jnp.stack(
            [shares.reshape(blocks, 128), jnp.pad(blocked(widen_b, 64)[:, :, 0], ((0, 0), (0, 64)))], axis=1
        )
        every = jnp.pad(rows, ((0, 0), (0, BLK - 2), (0, 0)))
        sources_q = as_sources(jnp.concatenate([blocked(wqkv, BLK), every], axis=2))
        wide = blocked(widen, BLK).reshape(blocks, BLK, 4, width).transpose(0, 2, 1, 3)
        sources_a = as_sources(
            jnp.concatenate(
                [blocked(wout, BLK), blocked(narrow, 4 * BLK), wide.reshape(blocks, 4 * BLK, width)], axis=1
            )
        )
        start = []
        x = by_window(x)
        bias = score_bias(scal, table, [])

    first, qkv, p, ctx, prm, bw = attention_forward(scal, x, labels, bias, sources_q, start)
    if fast:
        sources_a = list(hand_on(scal, [near_a] + got_a, [ctx]))
        sources_a += [exchange(v, 1, n) for v in sources_a]
    up = by_window(up)
    out, gr, gc, eb, sb, keep_h, send_h = hidden_both(scal, tokens, x, up, ctx, prm, bw, sources_a)
    between, last = [], []
    if fast:
        dealt_h = deal(scal, [keep_h, exchange(send_h, 1, n)], 1, [])
        got_h = others_of(dealt_h, 1, n)
        between = [dealt_h[0]]
    gj, keep_j, send_j = attention_back(scal, qkv, p, gc, first, eb, sb, between)
    if fast:
        dealt_h = deal(scal, [dealt_h[0]] + got_h, 3, [keep_j])
        got_h = others_of(dealt_h, 3, n)
        (send_j,) = hand_on(scal, [send_j], [dealt_h[0]])
        dealt_j = deal(scal, [keep_j, exchange(send_j, 1, n)], 1, [])
        got_j = others_of(dealt_j, 1, n)
        last = [dealt_h[0], dealt_j[0]]
    grad_in = input_grad(scal, tokens, x, up, gj, gr, prm, sources_q, last)
    if fast:
        dealt_j = deal(scal, [dealt_j[0]] + got_j, 3, [grad_in] + got_h)
        got_j = others_of(dealt_j, 3, n)
        expander, outmatrix, reducer = finish_hidden(scal, [dealt_h[0]] + got_h, [dealt_j[0]])
        done = finish_joint(scal, [dealt_j[0]] + got_j, wqkv, widen, expander, pay_q, entries)
        projector, grad_table = done[:2]
        pregain, offset, qb, vb, ob, midgain, midshift, xb, rb = [v.reshape(-1) for v in done[2:]]
    else:
        def scatter(v):
            return lax.psum_scatter(v, AXES, scatter_dimension=0, tiled=True).astype(F32)

        def natural(keep, send):
            pairs = blocks // 2
            return jnp.stack([keep[:pairs], send[:pairs]], axis=1).reshape((blocks,) + keep.shape[1:])

        all_h = natural(keep_h, send_h)
        outmatrix = scatter(all_h[:, :BLK].reshape(width, width))
        reducer = scatter(all_h[:, BLK : 5 * BLK].reshape(4 * width, width))
        expander = all_h[:, 5 * BLK :].reshape(blocks, 4, BLK, width).transpose(0, 2, 1, 3)
        expander = scatter(expander.reshape(width, 4 * width))
        projector = scatter(natural(keep_j, send_j).reshape(width, 3 * width))
        sums = lax.psum(keep_j[-1].astype(F32), AXES)
        grad_table, eb, rb, ob, gb = read_small(sums)
        grad_table = grad_table[:, :entries]

        def gains(w, grad, bias, shift, gain):
            w = w.astype(F32)
            g = jnp.sum(w * (grad - shift.astype(F32)[:, None] * bias), axis=1)
            return g / gain.astype(F32), jnp.sum(w * bias, axis=1)

        pregain, offset = gains(wqkv, projector, gb, shift1, gain1)
        midgain, midshift = gains(widen, expander, eb, shift2, gain2)

        def mine(v, size):
            return lax.dynamic_slice_in_dim(v[0], me * size, size, 0)

        qb, vb = mine(gb[:, :width], own), mine(gb[:, 2 * width :], own)
        ob, rb, xb = mine(ob, own), mine(rb, own), mine(eb, 4 * own)
    return (
        out, grad_in, pregain, offset, projector, qb, vb, outmatrix, ob, midgain, midshift,
        expander, xb, reducer, rb, grad_table,
    )


def others_of(dealt, shift, n):
    return [exchange(dealt[m], m << shift, n) for m in (1, 2, 3)]


def solution(mesh):
    both = ("wide", "narrow")
    v1, v2, v3 = P(both), P(both, None), P(both, None, None)
    in_specs = (v3, v1, v2, v1, v1, v2, v1, v1, v2, v1, v1, v1, v2, v1, v2, v1, P(), v3)
    out_specs = (v3, v3, v1, v1, v2, v1, v1, v2, v1, v1, v1, v2, v1, v2, v1, P())
    return jax.shard_map(
        per_device, mesh=mesh, in_specs=in_specs, out_specs=out_specs, check_vma=False
    )
```

```python
import functools

import jax
import jax.numpy as jnp
from jax import lax
from jax.experimental import pallas as pl
from jax.experimental.pallas import tpu as pltpu
from jax.sharding import PartitionSpec as P

F32 = jnp.float32
BF = jnp.bfloat16
WS = 10
TP = 104
SEG = 128
BLK = 16
EPS = 1e-5
NW = 4
VMEM = 60 << 20

NT = (((1,), (1,)), ((), ()))
TN = (((0,), (0,)), ((), ()))
NN = (((1,), (0,)), ((), ()))


def dot(a, b, dims=NN):
    return lax.dot_general(a, b, dims, preferred_element_type=F32)


def normalize(v):
    c = v - jnp.mean(v, axis=-1, keepdims=True)
    inv = lax.rsqrt(jnp.mean(c * c, axis=-1, keepdims=True) + EPS)
    return c * inv, inv


def norm_back(g, xhat, inv, gain):
    s = g * gain
    return inv * (
        s
        - jnp.mean(s, axis=-1, keepdims=True)
        - xhat * jnp.mean(s * xhat, axis=-1, keepdims=True)
    )


def head_masks():
    lane = lax.broadcasted_iota(jnp.int32, (1, 128), 1)
    return [(lane // 32) == h for h in range(4)]


def head_ones():
    return [jnp.where(m, 1.0, 0.0).astype(BF) for m in head_masks()]


def stack_heads(v, ones):
    return jnp.concatenate([v * m for m in ones], axis=0)


def load_rows(src_ref):
    return src_ref[...].astype(F32).reshape(NW * TP, src_ref.shape[2])


def fetch_blocks(me, sources, parts, sem):
    copies = []
    for s, src in enumerate(sources):
        for z in range(src.shape[0]):
            m = 8 * z + 2 * (s % 4) + s // 4
            d = m ^ me
            for k, (row, rows, dst, lanes) in enumerate(parts):
                to = pl.ds(pl.multiple_of(d * rows, rows), rows)
                copies.append(
                    pltpu.make_async_copy(
                        src.at[z, pl.ds(row, rows), :], dst.at[to, lanes], sem.at[k, m]
                    )
                )
    for c in copies:
        c.start()
    for c in copies:
        c.wait()


def split_blocks(bit, keep_ref, send_ref, row, rows, acc, cols=None):
    lanes = slice(None) if cols is None else cols
    for k in range(acc.shape[0] // (2 * rows)):
        mine = pl.multiple_of(k * 2 * rows + bit * rows, rows)
        other = pl.multiple_of(k * 2 * rows + (1 - bit) * rows, rows)
        keep_ref[k, row : row + rows, :] = acc[pl.ds(mine, rows), lanes].astype(BF)
        send_ref[k, row : row + rows, :] = acc[pl.ds(other, rows), lanes].astype(BF)


def block_at(i, scal):
    return jnp.minimum(i, (scal[0] + NW - 1) // NW - 1)


def whole(shape):
    return pl.BlockSpec(shape, lambda *a: (0,) * len(shape))


def rows_spec(cols, col=0):
    return pl.BlockSpec((NW * TP, cols), lambda i, scal, *r: (block_at(i, scal), col))


def win_spec(shape, live_only=True):
    if live_only:
        return pl.BlockSpec(
            (NW,) + shape, lambda i, scal, *r: (block_at(i, scal),) + (0,) * len(shape)
        )
    return pl.BlockSpec((NW,) + shape, lambda i, *r: (i,) + (0,) * len(shape))


def vmem_spec():
    return pl.BlockSpec(memory_space=pltpu.VMEM)


def any_spec():
    return pl.BlockSpec(memory_space=pl.ANY)


def call(
    body, name, grid, prefetch, args, in_specs, out_shape, out_specs, scratch, cost, gate=(), vmem=VMEM
):
    first = len(prefetch) + len(args)

    def without_gate(*refs):
        body(*refs[:first], *refs[first + len(gate) :])

    return pl.pallas_call(
        without_gate,
        grid_spec=pltpu.PrefetchScalarGridSpec(
            num_scalar_prefetch=len(prefetch),
            grid=grid,
            in_specs=list(in_specs) + [any_spec()] * len(gate),
            out_specs=out_specs,
            scratch_shapes=scratch,
        ),
        out_shape=out_shape,
        compiler_params=pltpu.CompilerParams(vmem_limit_bytes=vmem),
        cost_estimate=pl.CostEstimate(
            flops=int(cost * 8e8), bytes_accessed=int(cost * 1e6), transcendentals=0
        ),
        name=name,
    )(*prefetch, *args, *gate)


def small_call(body, name, scal, args, outs, gate=(), far=(), scratch=(), far_out=False):
    first = 1 + len(args) + len(far)

    def without_gate(*refs):
        body(*refs[:first], *refs[first + len(gate) :])

    here = pl.BlockSpec(memory_space=pltpu.VMEM)
    return pl.pallas_call(
        without_gate,
        grid_spec=pltpu.PrefetchScalarGridSpec(
            num_scalar_prefetch=1,
            grid=(),
            in_specs=[here] * len(args) + [whole(a.shape) for a in far] + [any_spec()] * len(gate),
            out_specs=[whole(s) if far_out else here for s, _ in outs],
            scratch_shapes=list(scratch),
        ),
        out_shape=[sds(s, t) if far_out else pltpu.VMEM(s, t) for s, t in outs],
        compiler_params=pltpu.CompilerParams(vmem_limit_bytes=VMEM if far else 12 << 20),
        cost_estimate=pl.CostEstimate(flops=1000, bytes_accessed=1000, transcendentals=0),
        name=name,
    )(scal, *[pltpu.with_memory_space_constraint(a, pltpu.VMEM) for a in args], *far, *gate)


def sds(shape, dtype):
    return jax.ShapeDtypeStruct(shape, dtype)


def attention_body(
    scal, x_ref, reg_ref, bias_ref, *refs
):
    sources, refs = refs[:8], refs[8:]
    first_ref, qkv_ref, p_ref, ctx_ref, prm_ref, bw_ref, js, cs, wq, sem = refs
    i = pl.program_id(0)
    width = x_ref.shape[2]
    rows = NW * TP
    live = scal[0]

    @pl.when(i == 0)
    def _():
        js[rows : rows + SEG - TP, :] = jnp.zeros((SEG - TP, 3 * width), F32)
        fetch_blocks(scal[1], sources, [(0, BLK, wq, slice(None))], sem)
        small = wq[:, 3 * width :].astype(F32)
        shares = jnp.concatenate([small[r : r + 1] for r in range(0, width, BLK)], axis=0)
        count = width // BLK
        place = lax.broadcasted_iota(jnp.int32, (count, width), 1)
        mine = place // BLK == lax.broadcasted_iota(jnp.int32, (count, width), 0)
        source = lax.broadcasted_iota(jnp.int32, (128, width), 0)
        target = lax.broadcasted_iota(jnp.int32, (128, width), 1) % BLK
        for v in range(8):
            pick = jnp.where(source == target + BLK * v, 1.0, 0.0).astype(BF)
            spread = dot(shares.astype(BF), pick)
            prm_ref[v : v + 1, :] = jnp.sum(jnp.where(mine, spread, 0.0), axis=0, keepdims=True)
        left = lax.broadcasted_iota(jnp.int32, (1, 128), 1) < 64
        for k in range(width // (2 * BLK)):
            r = 2 * BLK * k
            right = pltpu.roll(small[r + BLK : r + BLK + 8], 64, 1)[1:2]
            bw_ref[0:1, 128 * k : 128 * k + 128] = jnp.where(left, small[r + 1 : r + 2], right)

    @pl.when(i * NW < live)
    def _():
        xhat, _ = normalize(load_rows(x_ref))
        first = (xhat * prm_ref[0:1, :] + prm_ref[1:2, :]).astype(BF)
        first_ref[...] = first
        scale = 32.0**-0.5
        for part in range(3):
            j = dot(first, wq[:, part * width : (part + 1) * width])
            if part == 0:
                j = (j + prm_ref[2:3, :]) * scale
            if part == 2:
                j = j + prm_ref[3:4, :]
            js[0:rows, part * width : (part + 1) * width] = j
        ones = head_ones()
        eye = lax.broadcasted_iota(jnp.int32, (TP, SEG), 0) == lax.broadcasted_iota(
            jnp.int32, (TP, SEG), 1
        )
        masks = []
        for w in range(NW):
            qkv_ref[w] = js[w * TP : w * TP + SEG, :].astype(BF)
            row = reg_ref[pl.ds(i * NW + w, 1), :].astype(F32)
            row = jnp.concatenate([row, jnp.full((1, SEG - row.shape[1]), -1.0, F32)], axis=1)
            row = jnp.broadcast_to(row, (TP, SEG))
            col = jnp.max(jnp.where(eye, row, -1.0), axis=1, keepdims=True)
            masks.append(jnp.where(row == col, 0.0, -1e30))

        def scores(n):
            w, g = n
            c = 128 * g
            keys = stack_heads(qkv_ref[w, :, width + c : width + c + 128], ones)
            return dot(qkv_ref[w, 0:TP, c : c + 128], keys, NT)

        def softmax(n, s):
            w, g = n
            out = []
            for h in range(4):
                lanes = slice(SEG * h, SEG * (h + 1))
                sh = s[:, lanes] + bias_ref[g, :, lanes] + masks[w]
                e = jnp.exp(sh - jnp.max(sh, axis=1, keepdims=True))
                out.append((e * (1.0 / jnp.sum(e, axis=1, keepdims=True))).astype(BF))
            p_ref[w, g] = jnp.concatenate(out, axis=1)

        def values(n):
            w, g = n
            c = 128 * g
            stacked = stack_heads(qkv_ref[w, :, 2 * width + c : 2 * width + c + 128], ones)
            cs[w * TP : (w + 1) * TP, c : c + 128] = dot(p_ref[w, g], stacked)

        pairs = [(w, g) for w in range(NW) for g in range(width // 128)]
        lag = 3
        ss = {}
        for k in range(len(pairs) + lag + 1):
            if k < len(pairs):
                ss[k] = scores(pairs[k])
            if 0 <= k - 1 - lag < len(pairs):
                values(pairs[k - 1 - lag])
            if 0 <= k - lag < len(pairs):
                softmax(pairs[k - lag], ss.pop(k - lag))
        ctx_ref[...] = cs[...].astype(BF)


def attention_forward(scal, x, regions, bias, sources, gate):
    windows, _, width = x.shape
    rows = NW * TP
    groups = width // 128
    return call(
        attention_body, "attn_fwd", (windows // NW,), (scal,), [x, regions, bias] + sources,
        [win_spec((TP, width)), whole(regions.shape), whole(bias.shape)] + [any_spec()] * 8,
        [sds((windows * TP, width), BF), sds((windows, SEG, 3 * width), BF),
         sds((windows, groups, TP, 512), BF), sds((windows * TP, width), BF),
         sds((8, width), F32), sds((1, 4 * width), F32)],
        [rows_spec(width), win_spec((SEG, 3 * width)), win_spec((groups, TP, 512)), rows_spec(width),
         whole((8, width)), whole((1, 4 * width))],
        [pltpu.VMEM((rows + SEG - TP, 3 * width), F32),
         pltpu.VMEM((rows, width), F32), pltpu.VMEM((width, sources[0].shape[2]), BF),
         pltpu.SemaphoreType.DMA((1, width // BLK))],
        24, gate,
    )


def normal_parts(z):
    return 0.5 + 0.5 * lax.erf(z * 0.7071067811865476), jnp.exp(z * z * -0.5)


def hidden_body(
    tokens, scal, x_ref, u_ref, ctx_ref, prm_ref, bw_ref, *refs
):
    sources, refs = refs[:8], refs[8:]
    out_ref, gr_ref, gc_ref, eb_ref, sb_ref, keep_ref, send_ref = refs[:7]
    acts, gps, er, rr, om, wo, wn, ww, sem = refs[7:]
    i = pl.program_id(0)
    width = x_ref.shape[2]
    hidden = ww.shape[1]
    live = scal[0]
    step = 256

    @pl.when(i == 0)
    def _():
        parts = [(0, BLK, wo, slice(None)), (BLK, 4 * BLK, wn, slice(None))]
        for c in range(4):
            parts.append(((5 + c) * BLK, BLK, ww, slice(c * width, (c + 1) * width)))
        fetch_blocks(scal[1], sources, parts, sem)
        er[...] = jnp.zeros_like(er)
        rr[...] = jnp.zeros_like(rr)
        om[...] = jnp.zeros_like(om)
        eb_ref[...] = jnp.zeros_like(eb_ref)
        sb_ref[...] = jnp.zeros_like(sb_ref)

    @pl.when(i * NW >= live)
    def _():
        out_ref[...] = x_ref[:, 0:tokens, :]

    @pl.when(i * NW < live)
    def _():
        xs = load_rows(x_ref)
        row = lax.broadcasted_iota(jnp.int32, (NW * TP, 1), 0)
        us = jnp.where(row < (live - i * NW) * TP, load_rows(u_ref), 0.0)
        ctx = ctx_ref[...]
        up = us.astype(BF)
        res = xs + dot(ctx, wo[...]) + prm_ref[4:5, :]
        xhat, inv = normalize(res)
        second = (xhat * prm_ref[5:6, :] + prm_ref[6:7, :]).astype(BF)

        def products(c):
            cols = slice(c * step, (c + 1) * step)
            return dot(up, wn[cols, :], NT), dot(second, ww[:, cols])

        def activate(c, ga, z):
            cols = slice(c * step, (c + 1) * step)
            z = z + bw_ref[:, cols]
            phi, bell = normal_parts(z)
            acts[:, cols] = (z * phi).astype(BF)
            gp = (ga * (phi + z * bell * 0.3989422804014327)).astype(BF)
            gps[:, cols] = gp
            eb_ref[:, cols] += jnp.sum(gp.astype(F32), axis=0, keepdims=True)

        count = hidden // step
        t = products(0)
        for c in range(count):
            later = products(c + 1) if c + 1 < count else None
            activate(c, *t)
            t = later
        for c in range(count):
            cols = slice(c * step, (c + 1) * step)
            er[:, cols] += dot(second, gps[:, cols], TN)
            rr[cols, :] += dot(acts[:, cols], up, TN)
        gs = dot(gps[...], ww[...], NT)
        o = res + dot(acts[...], wn[...]) + prm_ref[7:8, :]
        for w in range(NW):
            out_ref[w] = jnp.where(
                i * NW + w < live, o[w * TP : w * TP + tokens], xs[w * TP : w * TP + tokens]
            ).astype(BF)
        gres = us + norm_back(gs, xhat, inv, prm_ref[5:6, :])
        ga = gres.astype(BF)
        gr_ref[...] = ga
        om[...] += dot(ctx, ga, TN)
        sb_ref[0:1, :] += jnp.sum(us, axis=0, keepdims=True)
        sb_ref[1:2, :] += jnp.sum(ga.astype(F32), axis=0, keepdims=True)
        gc = dot(ga, wo[...], NT)
        for w in range(NW):
            gc_ref[w] = gc[w * TP : (w + 1) * TP].astype(BF)

    @pl.when(i == pl.num_programs(0) - 1)
    def _():
        bit = scal[1] & 1
        split_blocks(bit, keep_ref, send_ref, 0, BLK, om)
        split_blocks(bit, keep_ref, send_ref, BLK, 4 * BLK, rr)
        for c in range(4):
            split_blocks(
                bit, keep_ref, send_ref, (5 + c) * BLK, BLK, er, slice(c * width, (c + 1) * width)
            )


def hidden_both(scal, tokens, x, u, ctx, prm, bw, sources):
    windows, _, width = x.shape
    hidden = 4 * width
    rows = NW * TP
    pairs = width // BLK // 2
    share = (pairs, 9 * BLK, width)
    return call(
        functools.partial(hidden_body, tokens), "hidden", (windows // NW,), (scal,),
        [x, u, ctx, prm, bw] + sources,
        [win_spec((TP, width), False), win_spec((TP, width)), rows_spec(width),
         whole(prm.shape), whole(bw.shape)] + [any_spec()] * 8,
        [sds((windows, tokens, width), BF), sds((windows * TP, width), BF), sds((windows, TP, width), BF),
         sds((1, hidden), F32), sds((2, width), F32), pltpu.VMEM(share, BF), pltpu.VMEM(share, BF)],
        [win_spec((tokens, width), False), rows_spec(width), win_spec((TP, width)),
         whole((1, hidden)), whole((2, width)), vmem_spec(), vmem_spec()],
        [pltpu.VMEM((rows, hidden), BF), pltpu.VMEM((rows, hidden), BF),
         pltpu.VMEM((width, hidden), F32), pltpu.VMEM((hidden, width), F32), pltpu.VMEM((width, width), F32),
         pltpu.VMEM((width, width), BF), pltpu.VMEM((hidden, width), BF), pltpu.VMEM((width, hidden), BF),
         pltpu.SemaphoreType.DMA((6, 2 * pairs))],
        52, (), 52 << 20,
    )


def three_terms(v):
    hi = v.astype(BF)
    rest = v - hi.astype(F32)
    mid = rest.astype(BF)
    return hi, mid, (rest - mid.astype(F32)).astype(BF)


def table_rows(scores):
    side = 2 * WS - 1
    reach = side * (WS - 1) + WS - 1
    j = lax.broadcasted_iota(jnp.int32, (SEG, 256), 0)
    k = lax.broadcasted_iota(jnp.int32, (SEG, 256), 1)
    pick = jnp.where(k == reach - (side * (j // WS) + j % WS), 1.0, 0.0).astype(BF)
    r = lax.broadcasted_iota(jnp.int32, (16, TP), 0)
    i = lax.broadcasted_iota(jnp.int32, (16, TP), 1)
    group = jnp.where(r == i // WS, 1.0, 0.0).astype(BF)
    rest = jnp.zeros((TP, 128), F32)
    skip = side - WS
    us = [sum(dot(t, pick) for t in three_terms(v)) for v in scores]
    us = [jnp.concatenate([u, rest], axis=1) for u in us]
    us = [pltpu.roll(u, 0, 1, stride=1, stride_axis=0) for u in us]
    vs = [sum(dot(group, t) for t in three_terms(u)) for u in us]
    low = [pltpu.roll(v[0:8], 0, 1, stride=skip, stride_axis=0) for v in vs]
    high = [pltpu.roll(v[8:16], 0, 1, stride=skip, stride_axis=0) for v in vs]
    high = [pltpu.roll(h, 8 * skip, 1) for h in high]
    return [jnp.sum(p + q, axis=0, keepdims=True) for p, q in zip(low, high)]


def attention_back_body(
    scal, qkv_ref, p_ref, gc_ref, first_ref, eb_ref, sb_ref,
    gj_ref, keep_ref, send_ref,
    gjs, pj, gb, ra, small,
):
    i = pl.program_id(0)
    width = gc_ref.shape[2]
    live = scal[0]

    @pl.when(i == 0)
    def _():
        pj[...] = jnp.zeros_like(pj)
        gb[...] = jnp.zeros_like(gb)
        ra[...] = jnp.zeros_like(ra)
        small[...] = jnp.zeros_like(small)

    @pl.when(i * NW < live)
    def _():
        masks = head_masks()
        ones = head_ones()
        scale = 32.0**-0.5

        def lanes_of(g, part=0):
            c = part * width + 128 * g
            return slice(c, c + 128)

        def to_probs(n):
            w, g = n
            stacked = stack_heads(qkv_ref[w, :, lanes_of(g, 2)], ones)
            return dot(gc_ref[w, :, lanes_of(g)], stacked, NT)

        def softmax_back(n, dp):
            w, g = n
            out = []
            for h in range(4):
                lanes = slice(SEG * h, SEG * (h + 1))
                ph = p_ref[w, g, :, lanes].astype(F32)
                t = dp[:, lanes] * ph
                out.append(t - ph * jnp.sum(t, axis=1, keepdims=True))
            return jnp.concatenate(out, axis=1).astype(BF)

        def combine(r):
            o = jnp.where(masks[0], r[0:TP], 0.0)
            for h in range(1, 4):
                o = jnp.where(masks[h], r[SEG * h : SEG * h + TP], o)
            return o

        def to_joint(n, ds):
            w, g = n
            rows = slice(w * TP, (w + 1) * TP)
            keys = stack_heads(qkv_ref[w, :, lanes_of(g, 1)], ones)
            gjs[rows, lanes_of(g)] = dot(ds, keys) * scale
            gjs[rows, lanes_of(g, 1)] = combine(dot(ds, qkv_ref[w, 0:TP, lanes_of(g)], TN))
            gjs[rows, lanes_of(g, 2)] = combine(dot(p_ref[w, g], gc_ref[w, :, lanes_of(g)], TN))

        pairs = [(w, g) for g in range(width // 128) for w in range(NW)]
        size = 2
        parts = [pairs[k : k + size] for k in range(0, len(pairs), size)]
        dps = [to_probs(n) for n in parts[0]]
        before = None
        for k, group in enumerate(parts):
            later = [to_probs(n) for n in parts[k + 1]] if k + 1 < len(parts) else None
            dss = [softmax_back(n, dp) for n, dp in zip(group, dps)]
            if before is not None:
                for n, ds in zip(*before):
                    to_joint(n, ds)
            total = dss[0].astype(F32)
            for ds in dss[1:]:
                total += ds.astype(F32)
            ra[group[0][1]] += total
            before = (group, dss)
            dps = later
        for n, ds in zip(*before):
            to_joint(n, ds)
        gj = gjs[...].astype(BF)
        gj_ref[...] = gj
        gb[...] += jnp.sum(gj.astype(F32), axis=0, keepdims=True)
        pj[...] += dot(first_ref[...], gj, TN)

    @pl.when(i == pl.num_programs(0) - 1)
    def _():
        split_blocks(scal[1] & 1, keep_ref, send_ref, 0, BLK, pj)
        for h in range(0, width // 32, 8):
            heads = range(h, h + 8)
            lanes = [slice(SEG * (k % 4), SEG * (k % 4 + 1)) for k in heads]
            rows = table_rows([ra[k // 4, :, c] for k, c in zip(heads, lanes)])
            small[h : h + 8, 0:384] = jnp.concatenate(rows, axis=0)
        small[0:1, 384:1408] = eb_ref[:, 0:1024]
        small[1:2, 384:1408] = eb_ref[:, 1024:2048]
        small[2:3, 384:896] = sb_ref[0:1, :]
        small[2:3, 896:1408] = sb_ref[1:2, :]
        small[3:4, 384:1408] = gb[:, 0:1024]
        small[4:5, 384:896] = gb[:, 1024:1536]
        sums = small[...].astype(BF)
        keep_ref[keep_ref.shape[0] - 1] = sums
        send_ref[send_ref.shape[0] - 1] = sums


def read_small(v):
    table = v[:, 0:384]
    eb = jnp.concatenate([v[0:1, 384:1408], v[1:2, 384:1408]], axis=1)
    gb = jnp.concatenate([v[3:4, 384:1408], v[4:5, 384:896]], axis=1)
    return table, eb, v[2:3, 384:896], v[2:3, 896:1408], gb


def attention_back(scal, qkv, p, gc, first, eb, sb, gate):
    windows = qkv.shape[0]
    width = gc.shape[2]
    rows = NW * TP
    groups = width // 128
    share = (width // BLK // 2 + 1, BLK, 3 * width)
    return call(
        attention_back_body, "attn_back", (windows // NW,), (scal,),
        (qkv, p, gc, first, eb, sb),
        [win_spec((SEG, 3 * width)), win_spec((groups, TP, 512)), win_spec((TP, width)),
         rows_spec(width), whole(eb.shape), whole(sb.shape)],
        [sds((windows * TP, 3 * width), BF), pltpu.VMEM(share, BF), pltpu.VMEM(share, BF)],
        [rows_spec(3 * width), vmem_spec(), vmem_spec()],
        [pltpu.VMEM((rows, 3 * width), F32), pltpu.VMEM((width, 3 * width), F32),
         pltpu.VMEM((1, 3 * width), F32), pltpu.VMEM((groups, TP, 512), F32),
         pltpu.VMEM((16, 3 * width), F32)],
        27, gate, 56 << 20,
    )


def input_grad_body(tokens, scal, x_ref, u_ref, gj_ref, gr_ref, prm_ref, *refs):
    sources = refs[:8]
    gi_ref, wq, sem = refs[8:]
    i = pl.program_id(0)
    width = x_ref.shape[2]
    live = scal[0]

    @pl.when(i == 0)
    def _():
        fetch_blocks(scal[1], sources, [(0, BLK, wq, slice(None))], sem)

    @pl.when(i * NW >= live)
    def _():
        gi_ref[...] = u_ref[:, 0:tokens, :]

    @pl.when(i * NW < live)
    def _():
        us = load_rows(u_ref)
        xhat, inv = normalize(load_rows(x_ref))
        gf = dot(gj_ref[...], wq[:, 0 : 3 * width], NT)
        o = gr_ref[...].astype(F32) + norm_back(gf, xhat, inv, prm_ref[0:1, :])
        for w in range(NW):
            rows = slice(w * TP, w * TP + tokens)
            gi_ref[w] = jnp.where(i * NW + w < live, o[rows], us[rows]).astype(BF)


def input_grad(scal, tokens, x, u, gj, gr, prm, sources, gate):
    windows, _, width = x.shape
    return call(
        functools.partial(input_grad_body, tokens), "input_grad", (windows // NW,), (scal,),
        [x, u, gj, gr, prm] + sources,
        [win_spec((TP, width)),
         pl.BlockSpec(
             (NW, TP, width),
             lambda i, s: (jnp.maximum(i, jnp.minimum(s[0] // NW, windows // NW - 1)), 0, 0),
         ),
         rows_spec(3 * width), rows_spec(width), whole(prm.shape)] + [any_spec()] * 8,
        [sds((windows, tokens, width), BF)],
        [win_spec((tokens, width), False)],
        [pltpu.VMEM((width, sources[0].shape[2]), BF), pltpu.SemaphoreType.DMA((1, width // BLK))],
        12, gate,
    )[0]


AXES = ("wide", "narrow")


def exchange(v, mask, n):
    return lax.ppermute(v, AXES, [(i, i ^ mask) for i in range(n)])


def join_body(scal, *refs):
    out = refs[-1]
    size = refs[0].shape[0]
    for k, r in enumerate(refs[:-1]):
        out[k * size : (k + 1) * size] = r[...]


def join(scal, arrays, gate):
    shape = (arrays[0].shape[0] * len(arrays),) + arrays[0].shape[1:]
    return small_call(join_body, "join", scal, arrays, [(shape, BF)], gate)[0]


def hand_on(scal, arrays, gate):
    count = len(arrays)
    return pl.pallas_call(
        lambda *refs: None,
        grid_spec=pltpu.PrefetchScalarGridSpec(
            num_scalar_prefetch=1,
            grid=(),
            in_specs=[any_spec()] * (count + len(gate)),
            out_specs=[any_spec()] * count,
        ),
        out_shape=[sds(a.shape, a.dtype) for a in arrays],
        input_output_aliases={1 + k: k for k in range(count)},
        name="hand_on",
    )(scal, *arrays, *gate)


def pack_joint_body(scal, wqkv_ref, *refs):
    vectors, out = refs[:-1], refs[-1]
    width = wqkv_ref.shape[1]
    out[0, :, 0:width] = wqkv_ref[...]

    def row(ref, at):
        v = ref[...].astype(F32).reshape(1, ref.shape[0])
        rest = 128 - ref.shape[0] - at
        parts = [jnp.zeros((1, at), F32)] * (at > 0) + [v] + [jnp.zeros((1, rest), F32)] * (rest > 0)
        return jnp.concatenate(parts, axis=1)

    first = sum(row(r, BLK * k) for k, r in enumerate(vectors[:8]))
    small = jnp.concatenate([first, row(vectors[8], 0), jnp.zeros((BLK - 2, 128), F32)], axis=0)
    out[0, :, width:] = small.astype(BF)


def pack_joint(scal, wqkv, vectors):
    rows, width = wqkv.shape
    outs = [((1, rows, width + 128), BF)]
    return small_call(pack_joint_body, "pack_joint", scal, [], outs, far=[wqkv] + vectors)[0]


def pack_hidden_body(scal, wout_ref, narrow_ref, widen_ref, out):
    width = wout_ref.shape[1]
    out[0, 0:BLK] = wout_ref[...]
    out[0, BLK : 5 * BLK] = narrow_ref[...]
    for c in range(4):
        out[0, (5 + c) * BLK : (6 + c) * BLK] = widen_ref[:, c * width : (c + 1) * width]


def pack_hidden(scal, wout, narrow, widen, gate):
    shape = (1, 9 * BLK, wout.shape[1])
    args = [wout, narrow, widen]
    return small_call(pack_hidden_body, "pack_hidden", scal, [], [(shape, BF)], gate, far=args)[0]


def others(v, shift, n):
    return [exchange(v, m << shift, n) for m in (1, 2, 3)]


def total_at(ins, at):
    total = ins[0][at].astype(F32)
    for r in ins[1:]:
        total += r[at].astype(F32)
    return total


def deal_body(count, shift, extra, scal, *refs):
    ins, outs = refs[:count], refs[-4:]
    me = (scal[1] >> shift) & 3
    quads = ins[0].shape[0] // 4
    for q in range(quads):
        for m in range(4):
            outs[m][q] = total_at(ins, 4 * q + (m ^ me)).astype(BF)
    if extra:
        rest = total_at(ins, 4 * quads).astype(BF)
        for m in range(4):
            outs[m][quads] = rest


def deal(scal, arrays, shift, gate):
    blocks, rows, cols = arrays[0].shape
    quads, extra = blocks // 4, blocks % 4
    body = functools.partial(deal_body, len(arrays), shift, extra)
    return small_call(body, "deal", scal, arrays, [((quads + extra, rows, cols), BF)] * 4, gate)


def finish_hidden_body(scal, a, b, c, d, expander_ref, outmatrix_ref, reducer_ref):
    v = total_at([a, b, c, d], 0)
    width = v.shape[1]
    outmatrix_ref[...] = v[0:BLK]
    reducer_ref[...] = v[BLK : 5 * BLK]
    for k in range(4):
        expander_ref[:, k * width : (k + 1) * width] = v[(5 + k) * BLK : (6 + k) * BLK]


def finish_hidden(scal, arrays, gate):
    width = arrays[0].shape[2]
    shapes = [(BLK, 4 * width), (BLK, width), (4 * BLK, width)]
    return small_call(
        finish_hidden_body, "finish_hidden", scal, arrays, [(s, F32) for s in shapes], gate, far_out=True
    )


def finish_joint_body(
    scal, a, b, c, d, wqkv_ref, widen_ref, expander_ref, small_ref,
    projector_ref, table_ref, pregain_ref, shift_ref, qb_ref, vb_ref, ob_ref, midgain_ref,
    midshift_ref, xb_ref, rb_ref,
):
    me = scal[1]
    ins = [a, b, c, d]
    projector = total_at(ins, 0)
    width = projector.shape[1] // 3
    projector_ref[...] = projector
    table, eb, reducebias, outbias, gb = read_small(total_at(ins, 1))
    table_ref[...] = table[:, 0 : table_ref.shape[1]]

    shares = small_ref[0][:, small_ref.shape[2] - 128 :].astype(F32)
    eye = lax.broadcasted_iota(jnp.int32, (BLK, 128), 0)
    lanes = lax.broadcasted_iota(jnp.int32, (BLK, 128), 1)

    def column(k):
        return jnp.sum(jnp.where(lanes == eye + BLK * k, shares[0:1], 0.0), axis=1, keepdims=True)

    def gains(w_ref, grad, bias, shift, gain):
        w = w_ref[...].astype(F32)
        g = jnp.sum(w * (grad - shift * bias), axis=1, keepdims=True) / gain
        return g, jnp.sum(w * bias, axis=1, keepdims=True)

    pregain, offset = gains(wqkv_ref, projector, gb, column(1), column(0))
    midgain, midshift = gains(widen_ref, expander_ref[...], eb, column(6), column(5))
    lane = lax.broadcasted_iota(jnp.int32, (BLK, 128), 1)
    mat = jnp.where(lane == 0, pregain, 0.0)
    for k, v in ((1, offset), (2, midgain), (3, midshift)):
        mat = jnp.where(lane == k, v, mat)
    mat = jnp.transpose(mat)
    for k, r in enumerate((pregain_ref, shift_ref, midgain_ref, midshift_ref)):
        r[...] = mat[k : k + 1, 0:BLK]

    def mine(v, size):
        lanes = v.shape[1]
        v = pltpu.roll(jnp.broadcast_to(v, (8, lanes)), lanes - me * size, 1)
        return v[0:1, 0:size]

    qb_ref[...] = mine(gb[:, 0:width], BLK)
    vb_ref[...] = mine(gb[:, 2 * width : 3 * width], BLK)
    ob_ref[...] = mine(outbias, BLK)
    rb_ref[...] = mine(reducebias, BLK)
    xb_ref[...] = mine(eb, 4 * BLK)


def finish_joint(scal, arrays, wqkv, widen, expander, small, entries):
    row = (1, BLK)
    shapes = [wqkv.shape, (BLK, entries)] + [row] * 7 + [(1, 4 * BLK), row]
    return small_call(
        finish_joint_body, "finish_joint", scal, arrays, [(s, F32) for s in shapes],
        far=[wqkv, widen, expander, small], far_out=True,
    )


def score_bias_body(scal, table_ref, bias_ref):
    side = 2 * WS - 1
    reach = side * (WS - 1) + WS - 1
    heads, entries = table_ref.shape
    i = lax.broadcasted_iota(jnp.int32, (TP, 384), 0)
    e = lax.broadcasted_iota(jnp.int32, (TP, 384), 1)
    pick = jnp.where(e == reach + side * (i // WS) + i % WS, 1.0, 0.0).astype(BF)
    j = lax.broadcasted_iota(jnp.int32, (SEG, 16), 0)
    r = lax.broadcasted_iota(jnp.int32, (SEG, 16), 1)
    group = jnp.where(r == j // WS, 1.0, 0.0).astype(BF)
    table = jnp.concatenate(
        [table_ref[...].astype(F32), jnp.zeros((heads, 384 - entries), F32)], axis=1
    )
    skip = side - WS
    vs, us = [], []
    for h in range(heads):
        t = jnp.broadcast_to(table[h : h + 1], (8, 384))
        low = pltpu.roll(t, 0, 1, stride=skip, stride_axis=0)
        vs.append(jnp.concatenate([low, pltpu.roll(low, 8 * skip, 1)], axis=0).astype(BF))
    for h in range(heads):
        us.append(pltpu.roll(dot(group, vs[h]), 0, 1, stride=1, stride_axis=0).astype(BF))
    for h in range(heads):
        bias_ref[h // 4, :, SEG * (h % 4) : SEG * (h % 4 + 1)] = dot(pick, us[h], NT)


def score_bias(scal, table, gate):
    heads = table.shape[0]
    shape = (heads // 4, TP, 4 * SEG)
    return small_call(
        score_bias_body, "score_bias", scal, [], [(shape, F32)], gate, far=[table], far_out=True
    )[0]


def by_window(v):
    return jnp.pad(v, ((0, 0), (0, TP - v.shape[1]), (0, 0)))


def as_sources(v):
    return [v[2 * q + c :: 8] for c in (0, 1) for q in range(4)]


def per_device(
    x, tally, labels, gain1, shift1, wqkv, qbias, vbias, wout, obias,
    gain2, shift2, widen, widen_b, narrow, narrow_b, table, up,
):
    tokens, width = x.shape[1:]
    heads, entries = table.shape
    n = lax.axis_size("wide") * lax.axis_size("narrow")
    me = lax.axis_index("wide") * lax.axis_size("narrow") + lax.axis_index("narrow")
    me = me.astype(jnp.int32)
    own = width // n
    fast = own == BLK and n == 32
    scal = jnp.stack([tally[0], me if fast else jnp.int32(0)])
    blocks = width // BLK

    vectors = [gain1, shift1, qbias, vbias, obias, gain2, shift2, narrow_b]
    if fast:
        pay_q = pack_joint(scal, wqkv, vectors + [widen_b])
        pay_a = pack_hidden(scal, wout, narrow, widen, [pay_q])
        x = by_window(x)
        near_q = join(scal, [pay_q] + others(pay_q, 3, n), [x])
        got_a = others(pay_a, 3, n)
        bias = score_bias(scal, table, [near_q])
        sources_q = hand_on(scal, [near_q] + others(near_q, 1, n), [bias])
        near_a = join(scal, [pay_a] + got_a, [sources_q[0]])
        sources_q = list(sources_q) + [exchange(v, 1, n) for v in sources_q]
        got_a = others(near_a, 1, n)
        start = [near_a]
    else:
        def gather(v):
            return lax.all_gather(v, AXES, axis=0, tiled=True)

        def blocked(v, rows):
            return gather(v).reshape(blocks, rows, -1)

        shares = jnp.stack([gather(v).reshape(blocks, BLK) for v in vectors], axis=1)
        rows = jnp.stack(
            [shares.reshape(blocks, 128), jnp.pad(blocked(widen_b, 64)[:, :, 0], ((0, 0), (0, 64)))], axis=1
        )
        every = jnp.pad(rows, ((0, 0), (0, BLK - 2), (0, 0)))
        sources_q = as_sources(jnp.concatenate([blocked(wqkv, BLK), every], axis=2))
        wide = blocked(widen, BLK).reshape(blocks, BLK, 4, width).transpose(0, 2, 1, 3)
        sources_a = as_sources(
            jnp.concatenate(
                [blocked(wout, BLK), blocked(narrow, 4 * BLK), wide.reshape(blocks, 4 * BLK, width)], axis=1
            )
        )
        start = []
        x = by_window(x)
        bias = score_bias(scal, table, [])

    first, qkv, p, ctx, prm, bw = attention_forward(scal, x, labels, bias, sources_q, start)
    if fast:
        sources_a = list(hand_on(scal, [near_a] + got_a, [ctx]))
        sources_a += [exchange(v, 1, n) for v in sources_a]
    up = by_window(up)
    out, gr, gc, eb, sb, keep_h, send_h = hidden_both(scal, tokens, x, up, ctx, prm, bw, sources_a)
    between, last = [], []
    if fast:
        dealt_h = deal(scal, [keep_h, exchange(send_h, 1, n)], 1, [])
        got_h = others_of(dealt_h, 1, n)
        between = [dealt_h[0]]
    gj, keep_j, send_j = attention_back(scal, qkv, p, gc, first, eb, sb, between)
    if fast:
        dealt_h = deal(scal, [dealt_h[0]] + got_h, 3, [keep_j])
        got_h = others_of(dealt_h, 3, n)
        (send_j,) = hand_on(scal, [send_j], [dealt_h[0]])
        dealt_j = deal(scal, [keep_j, exchange(send_j, 1, n)], 1, [])
        got_j = others_of(dealt_j, 1, n)
        last = [dealt_h[0], dealt_j[0]]
    grad_in = input_grad(scal, tokens, x, up, gj, gr, prm, sources_q, last)
    if fast:
        dealt_j = deal(scal, [dealt_j[0]] + got_j, 3, [grad_in] + got_h)
        got_j = others_of(dealt_j, 3, n)
        expander, outmatrix, reducer = finish_hidden(scal, [dealt_h[0]] + got_h, [dealt_j[0]])
        done = finish_joint(scal, [dealt_j[0]] + got_j, wqkv, widen, expander, pay_q, entries)
        projector, grad_table = done[:2]
        pregain, offset, qb, vb, ob, midgain, midshift, xb, rb = [v.reshape(-1) for v in done[2:]]
    else:
        def scatter(v):
            return lax.psum_scatter(v, AXES, scatter_dimension=0, tiled=True).astype(F32)

        def natural(keep, send):
            pairs = blocks // 2
            return jnp.stack([keep[:pairs], send[:pairs]], axis=1).reshape((blocks,) + keep.shape[1:])

        all_h = natural(keep_h, send_h)
        outmatrix = scatter(all_h[:, :BLK].reshape(width, width))
        reducer = scatter(all_h[:, BLK : 5 * BLK].reshape(4 * width, width))
        expander = all_h[:, 5 * BLK :].reshape(blocks, 4, BLK, width).transpose(0, 2, 1, 3)
        expander = scatter(expander.reshape(width, 4 * width))
        projector = scatter(natural(keep_j, send_j).reshape(width, 3 * width))
        sums = lax.psum(keep_j[-1].astype(F32), AXES)
        grad_table, eb, rb, ob, gb = read_small(sums)
        grad_table = grad_table[:, :entries]

        def gains(w, grad, bias, shift, gain):
            w = w.astype(F32)
            g = jnp.sum(w * (grad - shift.astype(F32)[:, None] * bias), axis=1)
            return g / gain.astype(F32), jnp.sum(w * bias, axis=1)

        pregain, offset = gains(wqkv, projector, gb, shift1, gain1)
        midgain, midshift = gains(widen, expander, eb, shift2, gain2)

        def mine(v, size):
            return lax.dynamic_slice_in_dim(v[0], me * size, size, 0)

        qb, vb = mine(gb[:, :width], own), mine(gb[:, 2 * width :], own)
        ob, rb, xb = mine(ob, own), mine(rb, own), mine(eb, 4 * own)
    return (
        out, grad_in, pregain, offset, projector, qb, vb, outmatrix, ob, midgain, midshift,
        expander, xb, reducer, rb, grad_table,
    )


def others_of(dealt, shift, n):
    return [exchange(dealt[m], m << shift, n) for m in (1, 2, 3)]


def solution(mesh):
    both = ("wide", "narrow")
    v1, v2, v3 = P(both), P(both, None), P(both, None, None)
    in_specs = (v3, v1, v2, v1, v1, v2, v1, v1, v2, v1, v1, v1, v2, v1, v2, v1, P(), v3)
    out_specs = (v3, v3, v1, v1, v2, v1, v1, v2, v1, v1, v1, v2, v1, v2, v1, P())
    return jax.shard_map(
        per_device, mesh=mesh, in_specs=in_specs, out_specs=out_specs, check_vma=False
    )
```
